32 devices in a mesh: dp: 16 (over z, x, core), head: 2 (over y).
Axes of the slice: x: 2, y: 2, z: 4, core: 2. Of those that a mesh axis runs over, the one named last changes fastest.
Arguments:
- inputs: float32 [1024, 16, 512], P('head', 'dp'), may hold values from -6 to 6
- doc_starts: int32 [16, 4], P('dp'), may hold values from 0 to 1023, as said below
- query_weight: float32 [512, 512], P(None, 'head'), may hold values from -1 to 1
- key_weight: float32 [512, 512], P(None, 'head'), may hold values from -0.25 to 0.25
- value_weight: float32 [512, 512], P(None, 'head'), may hold values from -0.25 to 0.25
- control_weight: float32 [512, 512], P(None, 'head'), may hold values from -0.5 to 0.5
- output_weight: float32 [512, 512], P('head'), may hold values from -2 to 2
- up_weight: float32 [512, 2048], P(None, 'head'), may hold values from -0.25 to 0.25
- down_weight: float32 [2048, 512], P('head'), may hold values from -0.125 to 0.125
- first_gain: float32 [512], replicated, may hold values from 0.5 to 1.5
- first_shift: float32 [512], replicated, may hold values from -2 to 2
- second_gain: float32 [512], replicated, may hold values from 0.5 to 1.5
- second_shift: float32 [512], replicated, may hold values from -2 to 2
- cotangent: float32 [1024, 16, 512], P('head', 'dp'), may hold values from -6 to 6
Outputs:
- outputs: float32 [1024, 16, 512], P('head', 'dp')
- grad_inputs: float32 [1024, 16, 512], P('head', 'dp')
- grad_query: float32 [512, 512], P(None, 'head')
- grad_key: float32 [512, 512], P(None, 'head')
- grad_value: float32 [512, 512], P(None, 'head')
- grad_control: float32 [512, 512], P(None, 'head')
- grad_output: float32 [512, 512], P('head')
- grad_up: float32 [512, 2048], P(None, 'head')
- grad_down: float32 [2048, 512], P('head')
- grad_first_gain: float32 [512], replicated
- grad_first_shift: float32 [512], replicated
- grad_second_gain: float32 [512], replicated
- grad_second_shift: float32 [512], replicated
The draws below stay inside these ranges and needn't reach their ends.
Inputs may be any that keep to these rules, and one draw needn't show every extreme that they name: `doc_starts`: each row holds 4 strictly rising document starts, the first 0; one document of each row begins before position 512 and ends after it.
All inputs are finite; a program needn't handle non-finite values.
Results may differ from the reference program's by a relative error of at most 0.0003.
Values sent between devices are 32-bit elements; how exact they have to be, the bound alone decides.
No kernel may reach another device: no remote copies, remote signals or barrier semaphores. Data moves between devices by JAX's collectives and lax.ppermute only.
A program may use at most 128 MiB of HBM per device.

```python
import jax
import jax.numpy as jnp
from jax import lax

D = 512
HEADS = 8
HD = 64
SLOTS = 64
FF = 2048
SEQ = 1024
SEQS = 16


def draw_doc_starts(key, part):
    key = jax.random.fold_in(key, 11)
    first_key, second_key, third_key = jax.random.split(key, 3)
    early = jax.random.randint(first_key, (SEQS, 1), 1, SEQ // 2, dtype=jnp.int32)
    middle = jax.random.randint(second_key, (SEQS, 1), SEQ // 2 + 1, SEQ * 3 // 4 + 1, dtype=jnp.int32)
    late = jax.random.randint(third_key, (SEQS, 1), SEQ * 3 // 4 + 1, SEQ, dtype=jnp.int32)
    return jnp.concatenate([jnp.zeros((SEQS, 1), jnp.int32), early, middle, late], axis=1)


def shard_levels(rng, dims, cuts, smallest, top_value):
    def one(dim, parts):
        draws = jax.random.uniform(jax.random.fold_in(jax.random.fold_in(rng, 6), dim), (parts,), jnp.float32, smallest / len(cuts), top_value / len(cuts))
        return jnp.repeat(jnp.exp(draws), dims[dim] // parts).reshape((-1,) + (1,) * (len(dims) - dim - 1))

    level = one(*cuts[0])
    for cut in cuts[1:]:
        level = level * one(*cut)
    return level


def scatter_about(key, shape, width, reach, cuts=(), kind=jnp.bfloat16):
    values = jax.random.normal(key, shape, jnp.float32) * width
    if len(cuts) > 0:
        values = shard_levels(key, shape, cuts, -0.22, 0.18) * values
    return jnp.clip(values, min=-reach, max=reach).astype(kind)


def setup_inputs(seed: int = 0) -> dict:
    key_list = jax.random.split(jax.random.key(seed), 15)
    return {
        "inputs": scatter_about(key_list[0], (SEQ, SEQS, D), 1.0, 6.0, ((0, 2), (1, 16)), jnp.float32),
        "doc_starts": draw_doc_starts(jax.random.fold_in(key_list[14], 71), 0),
        "query_weight": scatter_about(key_list[2], (D, HEADS * HD), (D // 16) ** -0.5, 1.0, ((1, 2),), jnp.float32),
        "key_weight": scatter_about(key_list[3], (D, HEADS * HD), D ** -0.5, 0.25, ((1, 2),), jnp.float32),
        "value_weight": scatter_about(key_list[4], (D, HEADS * HD), D ** -0.5, 0.25, ((1, 2),), jnp.float32),
        "control_weight": scatter_about(key_list[5], (D, HEADS * SLOTS), (D // 4) ** -0.5, 0.5, ((1, 2),), jnp.float32),
        "output_weight": scatter_about(key_list[6], (HEADS * HD, D), (max(D // 64, 1)) ** -0.5, 2.0, ((0, 2),), jnp.float32),
        "up_weight": scatter_about(key_list[7], (D, FF), D ** -0.5, 0.25, ((1, 2),), jnp.float32),
        "down_weight": scatter_about(key_list[8], (FF, D), FF ** -0.5, 0.125, ((0, 2),), jnp.float32),
        "first_gain": jnp.clip(1.0 + 0.1 * jax.random.normal(key_list[9], (D,), jnp.float32), 0.5, 1.5),
        "first_shift": scatter_about(key_list[10], (D,), 0.3, 2.0, (), jnp.float32),
        "second_gain": jnp.clip(1.0 + 0.1 * jax.random.normal(key_list[11], (D,), jnp.float32), 0.5, 1.5),
        "second_shift": scatter_about(key_list[12], (D,), 0.3, 2.0, (), jnp.float32),
        "cotangent": scatter_about(key_list[13], (SEQ, SEQS, D), 1.0, 6.0, ((0, 2), (1, 16)), jnp.float32),
    }


@jax.custom_vjp
def low(v):
    return lax.optimization_barrier(v.astype(jnp.bfloat16)).astype(jnp.float32)

@jax.custom_vjp
def low_back(v):
    return v

def low_keep(v):
    return (low(v), None)

def low_pass(kept, grad):
    return (grad,)

def back_keep(v):
    return (v, None)

def back_low(kept, grad):
    return (low(grad),)
low.defvjp(low_keep, low_pass)
low_back.defvjp(back_keep, back_low)

def product(left, right):
    return jnp.dot(left, right, precision=lax.Precision.HIGHEST, preferred_element_type=jnp.float32)

def layer_norm(values, gain, shift):
    centre = values - lax.optimization_barrier(jnp.mean(values, axis=-1, keepdims=True))
    spread = lax.optimization_barrier(jnp.mean(centre * centre, axis=-1, keepdims=True))
    return centre * lax.rsqrt(spread + 1e-05) * gain + shift

def slot_attention(query_rows, key_rows, value_rows, control_rows, doc_ids):
    length = query_rows.shape[0]
    position = jnp.arange(length, dtype=jnp.int32)
    allowed = ((position[:, None] >= position[None, :]) & (doc_ids[:, None] == doc_ids[None, :])).astype(query_rows.dtype)
    control_exp = jnp.exp(control_rows)
    totals = product(allowed, control_exp)
    affinity = allowed * product(query_rows, key_rows.T)
    scores = product(affinity, control_exp) / totals * query_rows.shape[-1] ** (-0.5)
    probs = jax.nn.softmax(scores, axis=-1)
    mixing = allowed * product(probs / totals, control_exp.T)
    return product(mixing, value_rows)

def layer_row(row, starts, params):
    query_weight, key_weight, value_weight, control_weight, output_weight, up_weight, down_weight, first_gain, first_shift, second_gain, second_shift = params
    position = jnp.arange(SEQ, dtype=jnp.int32)
    doc_ids = lax.optimization_barrier(jnp.sum((starts[None, :] <= position[:, None]).astype(jnp.int32), axis=1))
    normed = layer_norm(row, first_gain, first_shift)

    def split_heads(tensor, per_head):
        return tensor.reshape(SEQ, HEADS, per_head).transpose(1, 0, 2)
    attended = jax.vmap(slot_attention, in_axes=(0, 0, 0, 0, None))(split_heads(product(normed, query_weight), HD), split_heads(product(normed, key_weight), HD), split_heads(product(normed, value_weight), HD), split_heads(product(normed, control_weight), SLOTS), doc_ids)
    attended = attended.transpose(1, 0, 2).reshape(SEQ, HEADS * HD)
    hidden_state = row + product(attended, output_weight)
    second = layer_norm(hidden_state, second_gain, second_shift)
    activated = jax.nn.gelu(product(second, up_weight), approximate=True)
    return hidden_state + product(activated, down_weight)

def whole_layer(tokens, doc_starts, params):
    rows = jnp.moveaxis(tokens, 1, 0)

    def row_step(paired):
        return layer_row(paired[0], paired[1], params)
    results = lax.map(jax.checkpoint(row_step), (rows, doc_starts))
    return jnp.moveaxis(results, 0, 1)

def reference(inputs, doc_starts, query_weight, key_weight, value_weight, control_weight, output_weight, up_weight, down_weight, first_gain, first_shift, second_gain, second_shift, cotangent):

    def forward(tokens, *params):
        return whole_layer(tokens, doc_starts, params)
    outputs, pullback = jax.vjp(forward, inputs, query_weight, key_weight, value_weight, control_weight, output_weight, up_weight, down_weight, first_gain, first_shift, second_gain, second_shift)
    grad_inputs, grad_query, grad_key, grad_value, grad_control, grad_output, grad_up, grad_down, grad_first_gain, grad_first_shift, grad_second_gain, grad_second_shift = pullback(cotangent)
    return (outputs, grad_inputs, grad_query, grad_key, grad_value, grad_control, grad_output, grad_up, grad_down, grad_first_gain, grad_first_shift, grad_second_gain, grad_second_shift)
```

```python
import jax
import jax.numpy as jnp
from jax import lax
from jax.experimental import pallas as pl
from jax.experimental.pallas import tpu as pltpu
from jax.sharding import PartitionSpec as P

F32 = jnp.float32
HIGH = lax.Precision.HIGH
CHUNK = 256
EPS = 1e-05
GELU_C = 0.7978845608028654
GELU_K = 0.044715
VMEM_LIMIT = 40 * 2**20


def dot(left, right, dims):
    return lax.dot_general(
        left, right, (dims, ((), ())), precision=HIGH, preferred_element_type=F32
    )


def nn(left, right):
    return dot(left, right, ((1,), (0,)))


def nt(left, right):
    return dot(left, right, ((1,), (1,)))


def tn(left, right):
    return dot(left, right, ((0,), (0,)))


def whole():
    return pl.BlockSpec(memory_space=pltpu.VMEM)


def scalars():
    return pl.BlockSpec(memory_space=pltpu.SMEM)


def cost(flops, arrays_in, arrays_out):
    size = sum(a.size * 4 for a in arrays_in) + sum(a.size * 4 for a in arrays_out)
    return pl.CostEstimate(flops=int(flops), bytes_accessed=int(size), transcendentals=0)


def run(kernel, outs, scal, arrays, flops, scratch=()):
    out_shape = [jax.ShapeDtypeStruct(shape, F32) for shape in outs]
    return pl.pallas_call(
        kernel,
        out_shape=out_shape,
        in_specs=[scalars()] * len(scal) + [whole()] * len(arrays),
        out_specs=[whole()] * len(outs),
        scratch_shapes=list(scratch),
        compiler_params=pltpu.CompilerParams(vmem_limit_bytes=VMEM_LIMIT),
        cost_estimate=cost(3 * flops, arrays, out_shape),
    )(*scal, *arrays)


def lane_slice(ref, index, width):
    return ref[:, pl.ds(pl.multiple_of(index * width, width), width)]


def normalize(x):
    centre = x - jnp.mean(x, axis=-1, keepdims=True)
    spread = jnp.mean(centre * centre, axis=-1, keepdims=True)
    r = lax.rsqrt(spread + EPS)
    return centre * r, r


def norm_back(dy, nhat, r, gain):
    dyg = dy * gain
    first = jnp.mean(dyg, axis=-1, keepdims=True)
    second = jnp.mean(dyg * nhat, axis=-1, keepdims=True)
    return r * (dyg - first - nhat * second)


def doc_of(starts, position):
    total = jnp.zeros(jnp.shape(position), jnp.int32)
    for k in range(starts.shape[1]):
        total = total + (position >= starts[0, k]).astype(jnp.int32)
    return total


def column(first, count):
    return first + lax.broadcasted_iota(jnp.int32, (count, 1), 0)


def left_lanes():
    return lax.broadcasted_iota(jnp.int32, (1, 128), 1) < 64


def pack_state(mk, mv, z):
    left = left_lanes()
    return jnp.concatenate(
        [
            jnp.where(left, mk[0:64], mk[64:128]),
            jnp.where(left, mv[0:64], mv[64:128]),
            jnp.broadcast_to(z, (8, 128)),
        ],
        axis=0,
    )


def blocks_only(m):
    diagonal = (lax.broadcasted_iota(jnp.int32, (128, 128), 0) < 64) == (
        lax.broadcasted_iota(jnp.int32, (128, 128), 1) < 64
    )
    return jnp.where(diagonal, m, 0.0)


def unpack_state(state):
    mk = state[0:64]
    mv = state[64:128]
    return (
        blocks_only(jnp.concatenate([mk, mk], axis=0)),
        blocks_only(jnp.concatenate([mv, mv], axis=0)),
        state[128:129],
    )


def end_state(k2, v2, e2, starts, first):
    count = k2.shape[0]
    kept = (doc_of(starts, column(first, count)) == doc_of(starts, first + count - 1)).astype(F32)
    em = e2 * kept
    return pack_state(tn(k2, em), tn(em, v2), jnp.sum(em, axis=0, keepdims=True))


def own_kernel(scal, starts, x, gain, shift, wq, wk, wv, wc, normed, proj, states):
    nhat, _ = normalize(x[...])
    n = nhat * gain[...] + shift[...]
    normed[...] = n
    for w, ref in enumerate((wq, wk, wv, wc)):
        full = nn(n, ref[...])
        if w == 3:
            full = jnp.exp(full)
        for p in range(2):
            proj[p, :, w * 128 : (w + 1) * 128] = full[:, p * 128 : (p + 1) * 128]
    for p in range(2):
        states[p] = end_state(
            proj[p, :, 128:256], proj[p, :, 256:384], proj[p, :, 384:512], starts, scal[0]
        )


def other_kernel(scal, starts, normed, wa, wb, proj, state):
    core = scal[1]
    full = nn(lane_slice(normed, core, 256), wa[...]) + nn(
        lane_slice(normed, 1 - core, 256), wb[...]
    )
    proj[:, 0:384] = full[:, 0:384]
    proj[:, 384:512] = jnp.exp(full[:, 384:512])
    state[...] = end_state(
        proj[:, 128:256], proj[:, 256:384], proj[:, 384:512], starts, scal[0]
    )


def chunk_masks(starts, first, c):
    begin = first + c * CHUNK
    position = column(begin, CHUNK)
    docs = doc_of(starts, position)
    row = begin + lax.broadcasted_iota(jnp.int32, (1, CHUNK), 1)
    mask = (position >= row) & (docs == doc_of(starts, row))
    before = doc_of(starts, begin - 1)
    last = doc_of(starts, begin + CHUNK - 1)
    entering = (docs == before).astype(F32)
    leaving = (docs == last).astype(F32)
    passing = (before == last).astype(F32)
    return mask, entering, leaving, passing


def halves(x):
    left = left_lanes()
    return jnp.where(left, x, 0.0), jnp.where(left, 0.0, x)


def per_head(x):
    left = left_lanes()
    return left, x


def attention_kernel(index, starts, proj, carry, o, saved):
    left = left_lanes()
    mk, mv, z_in = unpack_state(carry[0])
    for c in range(proj.shape[1] // CHUNK):
        rows = slice(c * CHUNK, (c + 1) * CHUNK)
        q2, k2 = proj[0, rows, 0:128], proj[0, rows, 128:256]
        v2, e2 = proj[0, rows, 256:384], proj[0, rows, 384:512]
        mask, entering, leaving, passing = chunk_masks(starts, index[2], c)
        z = nn(mask.astype(F32), e2) + entering * z_in
        total = entering * nn(q2, mk)
        parts = [nn(jnp.where(mask, nt(qh, k2), 0.0), e2) for qh in halves(q2)]
        total = total + jnp.where(left, parts[0], parts[1])
        s = total / z * 0.125
        top = jnp.where(
            left,
            jnp.max(jnp.where(left, s, -jnp.inf), axis=1, keepdims=True),
            jnp.max(jnp.where(left, -jnp.inf, s), axis=1, keepdims=True),
        )
        p = jnp.exp(s - top)
        pa, pb = halves(p)
        p = p / jnp.where(
            left, jnp.sum(pa, axis=1, keepdims=True), jnp.sum(pb, axis=1, keepdims=True)
        )
        r = p / z
        parts = [nn(jnp.where(mask, nt(rh, e2), 0.0), v2) for rh in halves(r)]
        o[rows, :] = jnp.where(left, parts[0], parts[1]) + entering * nn(r, mv)
        saved[rows, 0:128] = z
        saved[rows, 128:256] = s
        saved[rows, 256:384] = p
        if (c + 1) * CHUNK < proj.shape[1]:
            em = e2 * leaving
            mk = blocks_only(tn(k2, em)) + passing * mk
            mv = blocks_only(tn(em, v2)) + passing * mv
            z_in = jnp.sum(em, axis=0, keepdims=True) + passing * z_in


def attention_back_kernel(index, starts, proj, carry, saved, d_o, dproj, dstate):
    left = left_lanes()
    chunks = proj.shape[1] // CHUNK
    states = [unpack_state(carry[0])]
    for c in range(chunks - 1):
        rows = slice(c * CHUNK, (c + 1) * CHUNK)
        k2, v2, e2 = proj[0, rows, 128:256], proj[0, rows, 256:384], proj[0, rows, 384:512]
        _, _, leaving, passing = chunk_masks(starts, index[2], c)
        mk, mv, z_in = states[c]
        em = e2 * leaving
        states.append(
            (
                blocks_only(tn(k2, em)) + passing * mk,
                blocks_only(tn(em, v2)) + passing * mv,
                jnp.sum(em, axis=0, keepdims=True) + passing * z_in,
            )
        )
    ahead = None
    for c in reversed(range(chunks)):
        rows = slice(c * CHUNK, (c + 1) * CHUNK)
        q2, k2 = proj[0, rows, 0:128], proj[0, rows, 128:256]
        v2, e2 = proj[0, rows, 256:384], proj[0, rows, 384:512]
        z, s, p = saved[rows, 0:128], saved[rows, 128:256], saved[rows, 256:384]
        do2 = d_o[rows, :]
        mask, entering, leaving, passing = chunk_masks(starts, index[2], c)
        mk, mv, _ = states[c]
        r = p / z
        do_in = entering * do2
        parts_v, parts_r, parts_e = [], [], []
        for rh, doh in zip(halves(r), halves(do2)):
            mixing = jnp.where(mask, nt(rh, e2), 0.0)
            d_mixing = jnp.where(mask, nt(doh, v2), 0.0)
            parts_v.append(tn(mixing, do2))
            parts_r.append(nn(d_mixing, e2))
            parts_e.append(tn(d_mixing, r))
        dv = jnp.where(left, parts_v[0], parts_v[1])
        dr = jnp.where(left, parts_r[0], parts_r[1]) + nt(do_in, mv)
        de = jnp.where(left, parts_e[0], parts_e[1])
        dp = dr / z
        dz = -dp * r
        pdp = p * dp
        pa, pb = halves(pdp)
        inner = jnp.where(
            left, jnp.sum(pa, axis=1, keepdims=True), jnp.sum(pb, axis=1, keepdims=True)
        )
        ds = p * (dp - inner) / z
        w = ds * 0.125
        dz = dz - ds * s
        w_in = entering * w
        parts_q, parts_k, parts_e = [], [], []
        for qh, wh in zip(halves(q2), halves(w)):
            affinity = jnp.where(mask, nt(qh, k2), 0.0)
            d_affinity = jnp.where(mask, nt(wh, e2), 0.0)
            parts_q.append(nn(d_affinity, k2))
            parts_k.append(tn(d_affinity, q2))
            parts_e.append(tn(affinity, w))
        dq = jnp.where(left, parts_q[0], parts_q[1]) + nt(w_in, mk)
        dk = jnp.where(left, parts_k[0], parts_k[1])
        de = de + jnp.where(left, parts_e[0], parts_e[1]) + tn(mask.astype(F32), dz)
        if ahead is not None:
            dmk, dmv, dz_out = ahead
            em = e2 * leaving
            dv = dv + nn(em, dmv)
            dk = dk + nt(em, dmk)
            de = de + leaving * (nn(k2, dmk) + nt(v2, dmv) + dz_out)
        dproj[rows, 0:128] = dq
        dproj[rows, 128:256] = dk
        dproj[rows, 256:384] = dv
        dproj[rows, 384:512] = de
        now = (
            blocks_only(tn(q2, w_in)),
            blocks_only(tn(r, do_in)),
            jnp.sum(entering * dz, axis=0, keepdims=True),
        )
        if ahead is not None:
            now = tuple(a + passing * b for a, b in zip(now, ahead))
        ahead = now
    dstate[...] = pack_state(*ahead)


def qkvc_kernel(index, starts, proj, dstate, normed, dproj, send, keep, final):
    k2, v2, e2 = proj[0, :, 128:256], proj[0, :, 256:384], proj[0, :, 384:512]
    count = k2.shape[0]
    first = index[2]
    core = index[3]
    dmk, dmv, dz_out = unpack_state(dstate[...])
    leaving = (
        doc_of(starts, column(first, count)) == doc_of(starts, first + count - 1)
    ).astype(F32)
    em = e2 * leaving
    final[:, 0:128] = dproj[:, 0:128]
    final[:, 128:256] = dproj[:, 128:256] + nt(em, dmk)
    final[:, 256:384] = dproj[:, 256:384] + nn(em, dmv)
    de = dproj[:, 384:512] + leaving * (nn(k2, dmk) + nt(v2, dmv) + dz_out)
    final[:, 384:512] = e2 * de
    send[...] = tn(lane_slice(normed, 1 - core, 256), final[...])
    keep[...] = tn(lane_slice(normed, core, 256), final[...])


def pair_call(kernel, outs, index, starts, proj, carry, arrays, flops):
    out_shape = [jax.ShapeDtypeStruct(shape, F32) for shape in outs]

    def pick(which):
        return lambda i, index, starts: (index[which], 0, 0)

    def all_of(a):
        zeros = (0,) * len(a.shape)
        return pl.BlockSpec(a.shape, lambda i, index, starts: zeros)

    return pl.pallas_call(
        kernel,
        out_shape=out_shape,
        grid_spec=pltpu.PrefetchScalarGridSpec(
            num_scalar_prefetch=2,
            grid=(1,),
            in_specs=[
                pl.BlockSpec((1,) + proj.shape[1:], pick(0)),
                pl.BlockSpec((1,) + carry.shape[1:], pick(1)),
            ]
            + [all_of(a) for a in arrays],
            out_specs=[all_of(a) for a in out_shape],
        ),
        compiler_params=pltpu.CompilerParams(vmem_limit_bytes=VMEM_LIMIT),
        cost_estimate=cost(3 * flops, (proj,) + tuple(arrays), out_shape),
    )(index, starts, proj, carry, *arrays)


def middle_kernel(scal, x, o0, o1, o2, o3, wo, wo2, wo3, gain, shift, hidden, second, o_all, w_all):
    pair = scal[2]
    for j, ref in enumerate((o0, o1, o2, o3)):
        o_all[:, j * 128 : (j + 1) * 128] = ref[...]
    for j in range(2):
        which = pair * (1 - 2 * j) + j
        w_all[j * 128 : (j + 1) * 128, :] = wo[pl.ds(pl.multiple_of(which * 128, 128), 128), :]
    w_all[256:384, :] = wo2[...]
    w_all[384:512, :] = wo3[...]
    h = x[...] + nn(o_all[...], w_all[...])
    hidden[...] = h
    nhat, _ = normalize(h)
    second[...] = nhat * gain[...] + shift[...]


def middle_back_kernel(
    scal, hidden, cot, ds0, ds1, ds2, ds3, u0, u1, u2, u3, gain, o_all, w_all,
    outputs, d_hidden, grads, d_o, send, keep, work,
):
    core = scal[1]
    outputs[...] = hidden[...] + ((u0[...] + u1[...]) + (u2[...] + u3[...]))
    d_second = (ds0[...] + ds1[...]) + (ds2[...] + ds3[...])
    nhat, r = normalize(hidden[...])
    grads[0:1, :] = jnp.sum(d_second * nhat, axis=0, keepdims=True)
    grads[1:2, :] = jnp.sum(d_second, axis=0, keepdims=True)
    grads[2:8, :] = jnp.zeros((6, grads.shape[1]), F32)
    d = cot[...] + norm_back(d_second, nhat, r, gain[...])
    d_hidden[...] = d
    d_o[...] = nt(d, w_all[...])
    work[...] = tn(o_all[...], d)
    for ref, which in ((send, 1 - core), (keep, core)):
        for j in range(4):
            rows = pl.ds(pl.multiple_of(j * 128 + which * 64, 64), 64)
            for b in range(4):
                ref[j, b * 64 : (b + 1) * 64, :] = work[rows, b * 128 : (b + 1) * 128]


def ff_kernel(refs_in, second, cot, blocks, received, outs):
    d_second = None
    for half, (up, down) in enumerate(blocks):
        u = nn(second[...], up[...])
        inner = GELU_C * (u + GELU_K * u * u * u)
        t = jnp.tanh(inner)
        act = 0.5 * u * (1.0 + t)
        slope = 0.5 * (1.0 + t) + 0.5 * u * (1.0 - t * t) * (
            GELU_C * (1.0 + 3.0 * GELU_K * u * u)
        )
        du = nt(cot[...], down[...]) * slope
        g_up = tn(second[...], du)
        g_down = tn(act, cot[...])
        if received is not None:
            g_up = g_up + received[half][...]
            g_down = g_down + received[2 + half][...]
        outs[half][...] = g_up
        outs[2 + half][...] = g_down
        if half == 0:
            outs[4][...] = nn(act, down[...])
            outs[5][...] = nt(du, up[...])
        else:
            outs[4][...] = outs[4][...] + nn(act, down[...])
            outs[5][...] = outs[5][...] + nt(du, up[...])


def ff_call(which, second, cot, up_own, down_own, up_oth, down_oth, received):
    rows, width = second.shape
    block = up_oth.shape[1]
    shapes = [(width, block)] * 2 + [(block, width)] * 2 + [(rows, width)] * 2
    out_shape = [jax.ShapeDtypeStruct(shape, F32) for shape in shapes]

    def kernel(index, second, cot, u_own, d_own, u_oth, d_oth, *rest):
        count = 0 if received is None else 4
        ff_kernel(
            None, second, cot, ((u_own, d_own), (u_oth, d_oth)),
            rest[:4] if count else None, rest[count:],
        )

    def all_of(a):
        zeros = (0,) * len(a.shape)
        return pl.BlockSpec(a.shape, lambda i, index: zeros)

    extra = () if received is None else tuple(received)
    arrays = (second, cot, up_own, down_own, up_oth, down_oth) + extra
    return pl.pallas_call(
        kernel,
        out_shape=out_shape,
        grid_spec=pltpu.PrefetchScalarGridSpec(
            num_scalar_prefetch=1,
            grid=(1,),
            in_specs=[
                all_of(second),
                all_of(cot),
                pl.BlockSpec((width, block), lambda i, index: (0, index[0])),
                pl.BlockSpec((block, width), lambda i, index: (index[0], 0)),
                all_of(up_oth),
                all_of(down_oth),
            ]
            + [all_of(a) for a in extra],
            out_specs=[all_of(a) for a in out_shape],
        ),
        compiler_params=pltpu.CompilerParams(vmem_limit_bytes=VMEM_LIMIT),
        cost_estimate=cost(3 * 2 * 6 * rows * width * 2 * block, (second, cot) + extra, out_shape),
    )(which, *arrays)


def first_back_kernel(
    scal, x, gain, d_hidden, f0, f1, f2, f3, wq, wk, wv, wc, a0, b0, a1, b1,
    grad_x, grads, cat, acc,
):
    core, pair = scal[1], scal[2]
    for j, ref in enumerate((f0, f1)):
        which = pair * (1 - 2 * j) + j
        for w in range(4):
            start = pl.multiple_of(w * 256 + which * 128, 128)
            cat[:, pl.ds(start, 128)] = ref[:, w * 128 : (w + 1) * 128]
    total = nt(cat[:, 0:256], wq[...])
    for w, ref in ((1, wk), (2, wv), (3, wc)):
        total = total + nt(cat[:, w * 256 : (w + 1) * 256], ref[...])
    acc[...] = total
    for which, refs in ((core, (a0, a1)), (1 - core, (b0, b1))):
        part = nt(f2[...], refs[0][...]) + nt(f3[...], refs[1][...])
        lanes = pl.ds(pl.multiple_of(which * 256, 256), 256)
        acc[:, lanes] = acc[:, lanes] + part
    d_normed = acc[...]
    nhat, r = normalize(x[...])
    grads[0:1, :] = jnp.sum(d_normed * nhat, axis=0, keepdims=True)
    grads[1:2, :] = jnp.sum(d_normed, axis=0, keepdims=True)
    grads[2:8, :] = jnp.zeros((6, grads.shape[1]), F32)
    grad_x[...] = d_hidden[...] + norm_back(d_normed, nhat, r, gain[...])


def combine(groups, radix, index):
    flat = [a for group in groups for a in group]
    counts = [len(group) for group in groups]
    shapes = []
    for group in groups:
        rows, cols = group[0].shape
        shapes += [(rows // radix, cols)] * radix

    def kernel(idx, *refs):
        ins, outs = refs[: len(flat)], refs[len(flat) :]
        at = 0
        for g, count in enumerate(counts):
            terms = ins[at : at + count]
            at += count
            rows = terms[0].shape[0] // radix
            for k in range(radix):
                if radix == 1:
                    value = terms[0][...]
                    for term in terms[1:]:
                        value = value + term[...]
                else:
                    where = jnp.bitwise_xor(idx[0], k)
                    block = pl.ds(pl.multiple_of(where * rows, rows), rows)
                    value = terms[0][block, :]
                    for term in terms[1:]:
                        value = value + term[block, :]
                outs[g * radix + k][...] = value

    outs = run(kernel, shapes, (index,), flat, 0)
    return [outs[g * radix : (g + 1) * radix] for g in range(len(groups))]


def assemble(groups, index):
    flat = [a for group in groups for a in group]
    radix = len(groups[0])
    shapes = [(group[0].shape[0] * radix, group[0].shape[1]) for group in groups]

    def kernel(idx, *refs):
        ins, outs = refs[: len(flat)], refs[len(flat) :]
        for g in range(len(groups)):
            for k in range(radix):
                piece = ins[g * radix + k]
                rows = piece.shape[0]
                where = jnp.bitwise_xor(idx[0], k)
                outs[g][pl.ds(pl.multiple_of(where * rows, rows), rows), :] = piece[...]

    return run(kernel, shapes, (index,), flat, 0)


def up_assemble_kernel(idx, u0, u1, u2, u3, d0, d1, d2, d3, up, down):
    width = u0.shape[1]
    for k, (u, d) in enumerate(((u0, d0), (u1, d1), (u2, d2), (u3, d3))):
        where = pl.ds(pl.multiple_of(jnp.bitwise_xor(idx[3], k) * width, width), width)
        up[:, where] = u[...]
        down[where, :] = d[...]


def qkvc_assemble_kernel(idx, g0, g1, g2, g3, o0, o1, o2, o3, wq, wk, wv, wc, wo):
    core, pair = idx[1], idx[2]
    for j in range(4):
        g = (g0, g1, g2, g3)[j]
        o = (o0, o1, o2, o3)[j]
        half = core if j % 2 == 0 else 1 - core
        which = pair if j < 2 else 1 - pair
        rows = pl.ds(pl.multiple_of(half * 256, 256), 256)
        lanes = pl.ds(pl.multiple_of(which * 128, 128), 128)
        for w, ref in enumerate((wq, wk, wv, wc)):
            ref[rows, lanes] = g[:, w * 128 : (w + 1) * 128]
        out_rows = pl.ds(pl.multiple_of(which * 128 + half * 64, 64), 64)
        for b in range(4):
            wo[out_rows, b * 128 : (b + 1) * 128] = o[b * 64 : (b + 1) * 64, :]


def per_device(
    inputs, doc_starts, query_weight, key_weight, value_weight, control_weight, output_weight,
    up_weight, down_weight, first_gain, first_shift, second_gain, second_shift, cotangent,
):
    rows, _, width = inputs.shape
    x = inputs.reshape(rows, width)
    cot = cotangent.reshape(rows, width)
    devices = lax.axis_size("dp")
    place = lax.axis_index("dp").astype(jnp.int32)
    y = lax.axis_index("head").astype(jnp.int32)
    core = place & 1
    pair = (place >> 1) & 1
    rank = place & 3
    first = y * rows
    one = lambda *v: jnp.stack([jnp.asarray(a, jnp.int32) for a in v])
    scal = one(first, core, pair, rank)
    gain1, shift1 = first_gain.reshape(1, width), first_shift.reshape(1, width)
    gain2, shift2 = second_gain.reshape(1, width), second_shift.reshape(1, width)

    def swap_y(a):
        return lax.ppermute(a, "head", [(0, 1), (1, 0)])

    def swap(a, bits):
        return lax.ppermute(a, "dp", [(i, i ^ bits) for i in range(devices)])

    weights = (query_weight, key_weight, value_weight, control_weight)
    piece = jnp.concatenate(
        [lax.dynamic_slice(w, (core * 256, pair * 128), (256, 128)) for w in weights], axis=1
    )
    wo_piece = lax.dynamic_slice(output_weight, (pair * 128 + core * 64, 0), (64, width))
    block = up_weight.shape[1] // 4
    up_piece = lax.dynamic_slice(up_weight, (0, rank * block), (width, block))
    down_piece = lax.dynamic_slice(down_weight, (rank * block, 0), (block, width))
    qa0 = swap_y(piece)
    wo0 = swap_y(wo_piece)
    up0 = swap_y(up_piece)
    down0 = swap_y(down_piece)
    qb0 = swap(qa0, 1)
    qa1 = swap(qa0, 2)
    qb1 = swap(qa1, 1)
    wo1 = swap(wo0, 2)
    wo0b, wo1b = swap(wo0, 1), swap(wo1, 1)
    up2, down2 = swap(up0, 2), swap(down0, 2)
    up1, down1 = swap(up0, 1), swap(down0, 1)
    up3, down3 = swap(up2, 1), swap(down2, 1)
    even = core == 0
    wo_pair0 = jnp.where(even, jnp.concatenate([wo0, wo0b]), jnp.concatenate([wo0b, wo0]))
    wo_pair1 = jnp.where(even, jnp.concatenate([wo1, wo1b]), jnp.concatenate([wo1b, wo1]))

    normed, proj_own, states_own = run(
        own_kernel,
        [(rows, width), (2, rows, 512), (2, 136, 128)],
        (scal, doc_starts),
        (x, gain1, shift1) + weights,
        2 * rows * width * 1024,
    )
    proj_oth, states_oth = [], []
    for wa, wb in ((qa0, qb0), (qa1, qb1)):
        got = run(
            other_kernel,
            [(rows, 512), (136, 128)],
            (scal, doc_starts),
            (normed, wa, wb),
            2 * rows * width * 512,
        )
        proj_oth.append(got[0][None])
        states_oth.append(got[1])
    to_second = lambda a: lax.ppermute(a, "head", [(0, 1)])
    to_first = lambda a: lax.ppermute(a, "head", [(1, 0)])
    carry_oth = to_second(states_own)
    carry_own = [to_second(s)[None] for s in states_oth]

    zero = jnp.int32(0)
    setups = []
    for j in range(2):
        setups.append((one(pair ^ j, zero, first, core), proj_own, carry_own[j]))
    for j in range(2):
        setups.append((one(zero, pair ^ j, first, core), proj_oth[j], carry_oth))
    attn_flops = 2 * rows * CHUNK * 128
    fwd = {}
    for j in (2, 0, 3, 1):
        index, proj, carry = setups[j]
        fwd[j] = pair_call(
            attention_kernel, [(rows, 128), (rows, 384)], index, doc_starts, proj, carry, (),
            13 * attn_flops,
        )
    hidden, second, o_all, w_all = run(
        middle_kernel,
        [(rows, width)] * 2 + [(rows, 512), (512, width)],
        (scal,),
        (x,) + tuple(fwd[j][0] for j in range(4))
        + (output_weight, wo_pair0, wo_pair1, gain2, shift2),
        2 * rows * width * 512,
    )

    ups, downs = (up0, up1, up2, up3), (down0, down1, down2, down3)

    def ff(j, received):
        return ff_call(
            one(rank ^ j), second, cot, up_weight, down_weight, ups[j], downs[j], received
        )

    ff3 = ff(3, None)
    sent3 = [swap(a, 1) for a in ff3[:4]]
    ff1 = ff(1, None)
    sent1 = [swap(a, 1) for a in ff1[:4]]
    ff2 = ff(2, sent3)
    ff0 = ff(0, sent1)

    rest = devices // 4
    stages = []
    shift = 2
    while rest > 1:
        radix = 4 if rest % 4 == 0 and rest != 8 else rest
        stages.append((shift, radix))
        shift += radix.bit_length() - 1
        rest //= radix

    def reduce_chunk(own0, oth0, own1, oth1):
        got1 = [swap_y(a) for a in oth1]
        sum1 = [g[0] for g in combine([[a, b] for a, b in zip(own1, got1)], 1, one(zero))]
        got_x = [swap(a, 2) for a in sum1]
        got0 = [swap_y(a) for a in oth0]
        groups = [[a, b, c] for a, b, c in zip(own0, got0, got_x)]
        for at, radix in stages:
            where = (place >> at) & (radix - 1)
            pieces = combine(groups, radix, one(where))
            groups = [
                [group[0]] + [swap(group[m], m << at) for m in range(1, radix)]
                for group in pieces
            ]
        shards = [g[0] for g in combine(groups, 1, one(zero))]
        for at, radix in reversed(stages):
            where = (place >> at) & (radix - 1)
            shards = assemble(
                [[a] + [swap(a, m << at) for m in range(1, radix)] for a in shards], one(where)
            )
        far = [swap(a, 2) for a in shards]
        near_all = [swap(a, 1) for a in shards]
        far_all = [swap(a, 1) for a in far]
        return [list(v) for v in zip(shards, near_all, far, far_all)]

    ff_sums = reduce_chunk(
        [ff0[0], ff0[2]], [ff0[1], ff0[3]], [ff2[0], ff2[2]], [ff2[1], ff2[3]]
    )
    grad_up, grad_down = run(
        up_assemble_kernel,
        [up_weight.shape, down_weight.shape],
        (scal,),
        tuple(ff_sums[0]) + tuple(ff_sums[1]),
        0,
    )

    outputs, d_hidden, grads2, d_o, o_send, o_keep = run(
        middle_back_kernel,
        [(rows, width)] * 2 + [(8, width), (rows, 512), (4, 256, 128), (4, 256, 128)],
        (scal,),
        (hidden, cot, ff0[5], ff1[5], ff2[5], ff3[5], ff0[4], ff1[4], ff2[4], ff3[4], gain2, o_all, w_all),
        4 * rows * width * 512,
        (pltpu.VMEM((512, width), F32),),
    )
    o_got = swap(o_send, 1)

    back = {}
    for j in (1, 3, 0, 2):
        index, proj, carry = setups[j]
        back[j] = pair_call(
            attention_back_kernel, [(rows, 512), (136, 128)], index, doc_starts, proj, carry,
            (fwd[j][1], d_o[:, j * 128 : (j + 1) * 128]), 28 * attn_flops,
        )
    grads = {}
    for j in (1, 3, 0, 2):
        index, proj, _ = setups[j]
        dstate = to_first(back[(j + 2) % 4][1])

        def kernel(idx, starts, proj, dst, normed, dproj, send, keep, final):
            qkvc_kernel(idx, starts, proj, dst.at[0], normed, dproj, send, keep, final)

        index = index.at[1].set(0)
        grads[j] = pair_call(
            kernel, [(256, 512), (256, 512), (rows, 512)], index, doc_starts, proj, dstate[None],
            (normed, back[j][0]), 2 * rows * width * 512,
        )
    summed = {}
    for j in (1, 3, 0, 2):
        got = swap(grads[j][0], 1)
        parts = combine([[grads[j][1], got], [o_keep[j], o_got[j]]], 1, one(zero))
        summed[j] = [p[0] for p in parts]
    sums = reduce_chunk(summed[0], summed[2], summed[1], summed[3])
    grad_query, grad_key, grad_value, grad_control, grad_output = run(
        qkvc_assemble_kernel,
        [w.shape for w in weights] + [output_weight.shape],
        (scal,),
        tuple(sums[0]) + tuple(sums[1]),
        0,
    )

    grad_inputs, grads1 = run(
        first_back_kernel,
        [(rows, width), (8, width)],
        (scal,),
        (x, gain1, d_hidden, grads[0][2], grads[1][2], grads[2][2], grads[3][2]) + weights
        + (qa0, qb0, qa1, qb1),
        2 * rows * width * 2048,
        (pltpu.VMEM((rows, 1024), F32), pltpu.VMEM((rows, width), F32)),
    )
    gains = jnp.concatenate([grads1[0:2], grads2[0:2]], axis=0)
    gains = gains + swap_y(gains)
    gains = gains + swap(gains, 1)
    gains = gains + swap(gains, 2)
    for at, radix in stages:
        gains = gains + sum(swap(gains, m << at) for m in range(1, radix))
    return (
        outputs.reshape(rows, 1, width), grad_inputs.reshape(rows, 1, width),
        grad_query, grad_key, grad_value, grad_control, grad_output, grad_up, grad_down,
        gains[0], gains[1], gains[2], gains[3],
    )


def solution(mesh):
    rows = P("head", "dp", None)
    cols = P(None, "head")
    tall = P("head", None)
    flat = P()
    return jax.shard_map(
        per_device,
        mesh=mesh,
        in_specs=(
            rows, P("dp", None), cols, cols, cols, cols, tall, cols, tall,
            flat, flat, flat, flat, rows,
        ),
        out_specs=(
            rows, rows, cols, cols, cols, cols, tall, cols, tall, flat, flat, flat, flat,
        ),
        check_vma=False,
    )
```

```python
import jax
import jax.numpy as jnp
from jax import lax
from jax.experimental import pallas as pl
from jax.experimental.pallas import tpu as pltpu
from jax.sharding import PartitionSpec as P

F32 = jnp.float32
HIGH = lax.Precision.HIGH
CHUNK = 256
EPS = 1e-05
GELU_C = 0.7978845608028654
GELU_K = 0.044715
VMEM_LIMIT = 16 * 2**20


def dot(left, right, dims):
    return lax.dot_general(
        left, right, (dims, ((), ())), precision=HIGH, preferred_element_type=F32
    )


def nn(left, right):
    return dot(left, right, ((1,), (0,)))


def nt(left, right):
    return dot(left, right, ((1,), (1,)))


def tn(left, right):
    return dot(left, right, ((0,), (0,)))


def whole():
    return pl.BlockSpec(memory_space=pltpu.VMEM)


def anywhere():
    return pl.BlockSpec(memory_space=pl.ANY)


def distant():
    return pl.BlockSpec(memory_space=pltpu.HBM)


def scalars():
    return pl.BlockSpec(memory_space=pltpu.SMEM)


def cost(light=False):
    return pl.CostEstimate(
        flops=(4 if light else 50) * 1153 * 10**6, bytes_accessed=0, transcendentals=0
    )


def run(kernel, outs, scal, arrays, scratch=(), after=(), far=0, light=False):
    out_shape = [jax.ShapeDtypeStruct(shape, F32) for shape in outs]
    first, last = len(scal) + len(arrays), len(scal) + len(arrays) + len(after)
    return pl.pallas_call(
        lambda *refs: kernel(*refs[:first], *refs[last:]),
        out_shape=out_shape,
        in_specs=[scalars()] * len(scal)
        + [whole()] * (len(arrays) - far)
        + [distant()] * far
        + [anywhere()] * len(after),
        out_specs=[whole()] * len(outs),
        scratch_shapes=list(scratch),
        compiler_params=pltpu.CompilerParams(vmem_limit_bytes=VMEM_LIMIT),
        cost_estimate=cost(light),
    )(*scal, *arrays, *after)


def tie(array, after):
    count = 1 + len(after)
    return pl.pallas_call(
        lambda *refs: None,
        out_shape=jax.ShapeDtypeStruct(array.shape, F32),
        in_specs=[anywhere()] * count,
        out_specs=anywhere(),
        input_output_aliases={0: 0},
        compiler_params=pltpu.CompilerParams(vmem_limit_bytes=2**20),
        cost_estimate=pl.CostEstimate(flops=0, bytes_accessed=0, transcendentals=0),
    )(array, *after)


def lane_slice(ref, index, width):
    return ref[:, pl.ds(pl.multiple_of(index * width, width), width)]


def normalize(x):
    centre = x - jnp.mean(x, axis=-1, keepdims=True)
    spread = jnp.mean(centre * centre, axis=-1, keepdims=True)
    r = lax.rsqrt(spread + EPS)
    return centre * r, r


def norm_back(dy, nhat, r, gain):
    dyg = dy * gain
    first = jnp.mean(dyg, axis=-1, keepdims=True)
    second = jnp.mean(dyg * nhat, axis=-1, keepdims=True)
    return r * (dyg - first - nhat * second)


def doc_of(starts, position):
    total = jnp.zeros(jnp.shape(position), jnp.int32)
    for k in range(starts.shape[1]):
        total = total + (position >= starts[0, k]).astype(jnp.int32)
    return total


def column(first, count):
    return first + lax.broadcasted_iota(jnp.int32, (count, 1), 0)


def left_lanes():
    return lax.broadcasted_iota(jnp.int32, (1, 128), 1) < 64


def pack_state(mk, mv, z):
    left = left_lanes()
    return jnp.concatenate(
        [
            jnp.where(left, mk[0:64], mk[64:128]),
            jnp.where(left, mv[0:64], mv[64:128]),
            jnp.broadcast_to(z, (8, 128)),
        ],
        axis=0,
    )


def blocks_only(m):
    diagonal = (lax.broadcasted_iota(jnp.int32, (128, 128), 0) < 64) == (
        lax.broadcasted_iota(jnp.int32, (128, 128), 1) < 64
    )
    return jnp.where(diagonal, m, 0.0)


def unpack_state(state):
    mk = state[0:64]
    mv = state[64:128]
    return (
        blocks_only(jnp.concatenate([mk, mk], axis=0)),
        blocks_only(jnp.concatenate([mv, mv], axis=0)),
        state[128:129],
    )


def end_state(k2, v2, e2, starts, first):
    count = k2.shape[0]
    kept = (doc_of(starts, column(first, count)) == doc_of(starts, first + count - 1)).astype(F32)
    em = e2 * kept
    return pack_state(tn(k2, em), tn(em, v2), jnp.sum(em, axis=0, keepdims=True))


def cut_first_kernel(scal, wq, wk, wv, wc, piece, sems):
    rows = pl.ds(pl.multiple_of(scal[1] * 256, 256), 256)
    lanes = pl.ds(pl.multiple_of(scal[2] * 128, 128), 128)
    copies = [
        pltpu.make_async_copy(
            ref.at[rows, lanes], piece.at[:, w * 128 : (w + 1) * 128], sems.at[w]
        )
        for w, ref in enumerate((wq, wk, wv, wc))
    ]
    for copy in copies:
        copy.start()
    for copy in copies:
        copy.wait()


def cut_second_kernel(scal, wo, up, down, piece, sems):
    unit = pl.ds(pl.multiple_of(scal[3] * 256 + scal[2] * 128, 128), 128)
    thin = pl.ds(pl.multiple_of((scal[2] * 2 + scal[1]) * 64, 64), 64)
    copies = [
        pltpu.make_async_copy(
            up.at[b * 128 : (b + 1) * 128, unit], piece.at[0:128, b * 128 : (b + 1) * 128],
            sems.at[b],
        )
        for b in range(4)
    ]
    copies.append(pltpu.make_async_copy(down.at[unit, :], piece.at[128:256, :], sems.at[4]))
    copies.append(pltpu.make_async_copy(wo.at[thin, :], piece.at[256:320, :], sems.at[5]))
    for copy in copies:
        copy.start()
    for copy in copies:
        copy.wait()


def cut(kernel, shapes, scal, arrays, after=(), limit=2**20, near=False):
    first, last = 1 + len(arrays), 1 + len(arrays) + len(after)
    out_shape = [jax.ShapeDtypeStruct(shape, F32) for shape in shapes]
    return pl.pallas_call(
        lambda *refs: kernel(*refs[:first], *refs[last:]),
        out_shape=out_shape,
        in_specs=[scalars()] + [distant()] * len(arrays) + [anywhere()] * len(after),
        out_specs=[whole() if near else anywhere()] * len(shapes),
        scratch_shapes=[pltpu.SemaphoreType.DMA((6,))],
        compiler_params=pltpu.CompilerParams(vmem_limit_bytes=limit),
        cost_estimate=cost(),
    )(scal, *arrays, *after)


def own_kernel(scal, starts, x, gain, shift, wq, wk, wv, wc, normed, proj, states, held, sems):
    copies = [
        pltpu.make_async_copy(ref, held.at[w], sems.at[w])
        for w, ref in enumerate((wq, wk, wv, wc))
    ]
    for copy in copies:
        copy.start()
    nhat, _ = normalize(x[:, 0, :])
    n = nhat * gain[...] + shift[...]
    normed[...] = n
    for w, copy in enumerate(copies):
        copy.wait()
        full = nn(n, held[w])
        if w == 3:
            full = jnp.exp(full)
        for p in range(2):
            proj[p, :, w * 128 : (w + 1) * 128] = full[:, p * 128 : (p + 1) * 128]
    for p in range(2):
        states[p] = end_state(
            proj[p, :, 128:256], proj[p, :, 256:384], proj[p, :, 384:512], starts, scal[0]
        )


def other_kernel(scal, starts, normed, wa, wb, proj, state):
    core = scal[1]
    full = nn(lane_slice(normed, core, 256), wa[...]) + nn(
        lane_slice(normed, 1 - core, 256), wb[...]
    )
    proj[:, 0:384] = full[:, 0:384]
    proj[:, 384:512] = jnp.exp(full[:, 384:512])
    state[...] = end_state(
        proj[:, 128:256], proj[:, 256:384], proj[:, 384:512], starts, scal[0]
    )


def chunk_masks(starts, first, c):
    begin = first + c * CHUNK
    position = column(begin, CHUNK)
    docs = doc_of(starts, position)
    row = begin + lax.broadcasted_iota(jnp.int32, (1, CHUNK), 1)
    mask = (position >= row) & (docs == doc_of(starts, row))
    before = doc_of(starts, begin - 1)
    last = doc_of(starts, begin + CHUNK - 1)
    entering = (docs == before).astype(F32)
    leaving = (docs == last).astype(F32)
    passing = (before == last).astype(F32)
    return mask, entering, leaving, passing


def halves(x):
    left = left_lanes()
    return jnp.where(left, x, 0.0), jnp.where(left, 0.0, x)


def attention(first, starts, proj, carry, o, lanes, saved):
    left = left_lanes()
    mk, mv, z_in = unpack_state(carry)
    for c in range(proj.shape[0] // CHUNK):
        rows = slice(c * CHUNK, (c + 1) * CHUNK)
        q2, k2 = proj[rows, 0:128], proj[rows, 128:256]
        v2, e2 = proj[rows, 256:384], proj[rows, 384:512]
        mask, entering, leaving, passing = chunk_masks(starts, first, c)
        z = nn(mask.astype(F32), e2) + entering * z_in
        total = entering * nn(q2, mk)
        parts = [nn(jnp.where(mask, nt(qh, k2), 0.0), e2) for qh in halves(q2)]
        total = total + jnp.where(left, parts[0], parts[1])
        s = total / z * 0.125
        top = jnp.where(
            left,
            jnp.max(jnp.where(left, s, -jnp.inf), axis=1, keepdims=True),
            jnp.max(jnp.where(left, -jnp.inf, s), axis=1, keepdims=True),
        )
        p = jnp.exp(s - top)
        pa, pb = halves(p)
        p = p / jnp.where(
            left, jnp.sum(pa, axis=1, keepdims=True), jnp.sum(pb, axis=1, keepdims=True)
        )
        r = p / z
        parts = [nn(jnp.where(mask, nt(rh, e2), 0.0), v2) for rh in halves(r)]
        o[rows, lanes] = jnp.where(left, parts[0], parts[1]) + entering * nn(r, mv)
        saved[rows, 0:128] = z
        saved[rows, 128:256] = s
        saved[rows, 256:384] = p
        if (c + 1) * CHUNK < proj.shape[0]:
            em = e2 * leaving
            mk = blocks_only(tn(k2, em)) + passing * mk
            mv = blocks_only(tn(em, v2)) + passing * mv
            z_in = jnp.sum(em, axis=0, keepdims=True) + passing * z_in


def attention_back(first, starts, proj, carry, saved, d_o, lanes, dproj):
    left = left_lanes()
    chunks = proj.shape[0] // CHUNK
    states = [unpack_state(carry)]
    for c in range(chunks - 1):
        rows = slice(c * CHUNK, (c + 1) * CHUNK)
        k2, v2, e2 = proj[rows, 128:256], proj[rows, 256:384], proj[rows, 384:512]
        _, _, leaving, passing = chunk_masks(starts, first, c)
        mk, mv, z_in = states[c]
        em = e2 * leaving
        states.append(
            (
                blocks_only(tn(k2, em)) + passing * mk,
                blocks_only(tn(em, v2)) + passing * mv,
                jnp.sum(em, axis=0, keepdims=True) + passing * z_in,
            )
        )
    ahead = None
    for c in reversed(range(chunks)):
        rows = slice(c * CHUNK, (c + 1) * CHUNK)
        q2, k2 = proj[rows, 0:128], proj[rows, 128:256]
        v2, e2 = proj[rows, 256:384], proj[rows, 384:512]
        z, s, p = saved[rows, 0:128], saved[rows, 128:256], saved[rows, 256:384]
        do2 = d_o[rows, lanes]
        mask, entering, leaving, passing = chunk_masks(starts, first, c)
        mk, mv, _ = states[c]
        r = p / z
        do_in = entering * do2
        parts_v, parts_r, parts_e = [], [], []
        for rh, doh in zip(halves(r), halves(do2)):
            mixing = jnp.where(mask, nt(rh, e2), 0.0)
            d_mixing = jnp.where(mask, nt(doh, v2), 0.0)
            parts_v.append(tn(mixing, do2))
            parts_r.append(nn(d_mixing, e2))
            parts_e.append(tn(d_mixing, r))
        dv = jnp.where(left, parts_v[0], parts_v[1])
        dr = jnp.where(left, parts_r[0], parts_r[1]) + nt(do_in, mv)
        de = jnp.where(left, parts_e[0], parts_e[1])
        dp = dr / z
        dz = -dp * r
        pdp = p * dp
        pa, pb = halves(pdp)
        inner = jnp.where(
            left, jnp.sum(pa, axis=1, keepdims=True), jnp.sum(pb, axis=1, keepdims=True)
        )
        ds = p * (dp - inner) / z
        w = ds * 0.125
        dz = dz - ds * s
        w_in = entering * w
        parts_q, parts_k, parts_e = [], [], []
        for qh, wh in zip(halves(q2), halves(w)):
            affinity = jnp.where(mask, nt(qh, k2), 0.0)
            d_affinity = jnp.where(mask, nt(wh, e2), 0.0)
            parts_q.append(nn(d_affinity, k2))
            parts_k.append(tn(d_affinity, q2))
            parts_e.append(tn(affinity, w))
        dq = jnp.where(left, parts_q[0], parts_q[1]) + nt(w_in, mk)
        dk = jnp.where(left, parts_k[0], parts_k[1])
        de = de + jnp.where(left, parts_e[0], parts_e[1]) + tn(mask.astype(F32), dz)
        if ahead is not None:
            dmk, dmv, dz_out = ahead
            em = e2 * leaving
            dv = dv + nn(em, dmv)
            dk = dk + nt(em, dmk)
            de = de + leaving * (nn(k2, dmk) + nt(v2, dmv) + dz_out)
        dproj[rows, 0:128] = dq
        dproj[rows, 128:256] = dk
        dproj[rows, 256:384] = dv
        dproj[rows, 384:512] = de
        now = (
            blocks_only(tn(q2, w_in)),
            blocks_only(tn(r, do_in)),
            jnp.sum(entering * dz, axis=0, keepdims=True),
        )
        if ahead is not None:
            now = tuple(a + passing * b for a, b in zip(now, ahead))
        ahead = now
    return pack_state(*ahead)


def own_pair(scal, j):
    return jnp.bitwise_xor(scal[2], j)


def attention_kernel(scal, starts, proj, carry, o, saved, j=None):
    here = proj if j is None else proj.at[own_pair(scal, j)]
    attention(scal[0], starts, here, carry, o, slice(0, 128), saved)


def middle_kernel(
    scal, o0, o1, o2, o3, x, wo, w0, w1, w2, w3, gain, shift, hidden, second, o_all, w_all,
):
    for j, ref in enumerate((o0, o1, o2, o3)):
        o_all[:, j * 128 : (j + 1) * 128] = ref[...]
    for j in range(2):
        which = pl.multiple_of(own_pair(scal, j) * 128, 128)
        w_all[j * 128 : (j + 1) * 128, :] = wo[pl.ds(which, 128), :]
    for k, ref in enumerate((w0, w1, w2, w3)):
        start = 256 + (k >> 1) * 128 + jnp.bitwise_xor(scal[1], k & 1) * 64
        w_all[pl.ds(pl.multiple_of(start, 64), 64), :] = ref[256:320, :]
    h = x[:, 0, :] + nn(o_all[...], w_all[...])
    hidden[...] = h
    nhat, _ = normalize(h)
    second[...] = nhat * gain[...] + shift[...]


def middle_back_kernel(
    scal, hidden, cot, ds0, ds1, ds2, ds3, u0, u1, u2, u3, gain, o_all, w_all,
    outputs, d_hidden, grads, d_o, send, keep, work,
):
    core = scal[1]
    outputs[:, 0, :] = hidden[...] + ((u0[...] + u1[...]) + (u2[...] + u3[...]))
    d_second = (ds0[...] + ds1[...]) + (ds2[...] + ds3[...])
    nhat, r = normalize(hidden[...])
    grads[0:1, :] = jnp.sum(d_second * nhat, axis=0, keepdims=True)
    grads[1:2, :] = jnp.sum(d_second, axis=0, keepdims=True)
    grads[2:8, :] = jnp.zeros((6, grads.shape[1]), F32)
    d = cot[:, 0, :] + norm_back(d_second, nhat, r, gain[...])
    d_hidden[...] = d
    d_o[...] = nt(d, w_all[...])
    work[...] = tn(o_all[...], d)
    for ref, which in ((send, 1 - core), (keep, core)):
        for j in range(4):
            rows = pl.ds(pl.multiple_of(j * 128 + which * 64, 64), 64)
            for b in range(4):
                ref[j, b * 64 : (b + 1) * 64, :] = work[rows, b * 128 : (b + 1) * 128]


def feed_forward_kernel(j, scal, second, cot, up, down, unit, other, packed, out, ds, up_far, down_far):
    where = pl.ds(pl.multiple_of(jnp.bitwise_xor(scal[3], j) * 256, 256), 256)
    for ref, half in ((unit, scal[2]), (other, 1 - scal[2])):
        place = pl.ds(pl.multiple_of(half * 128, 128), 128)
        for b in range(4):
            up_far[b * 128 : (b + 1) * 128, place] = ref[0:128, b * 128 : (b + 1) * 128]
        down_far[place, :] = ref[128:256, :]
    n_left, n_right = second[:, 0:256], second[:, 256:512]
    g = cot[:, 0, :]
    for half in range(2):
        if half == 0:
            up_left, up_right = up[0:256, where], up[256:512, where]
            down_block = down[where, :]
        else:
            up_left, up_right = up_far[0:256, :], up_far[256:512, :]
            down_block = down_far[...]
        u = nn(n_left, up_left) + nn(n_right, up_right)
        inner = GELU_C * (u + GELU_K * u * u * u)
        t = jnp.tanh(inner)
        act = 0.5 * u * (1.0 + t)
        slope = 0.5 * (1.0 + t) + 0.5 * u * (1.0 - t * t) * (
            GELU_C * (1.0 + 3.0 * GELU_K * u * u)
        )
        du = nt(g, down_block) * slope
        packed[2 * half, :, 0:256] = tn(n_left, du)
        packed[2 * half, :, 256:512] = tn(n_right, du)
        packed[2 * half + 1] = tn(act, g)
        out_part = nn(act, down_block)
        ds_left, ds_right = nt(du, up_left), nt(du, up_right)
        if half == 0:
            out[...] = out_part
            ds[:, 0:256] = ds_left
            ds[:, 256:512] = ds_right
        else:
            out[...] = out[...] + out_part
            ds[:, 0:256] = ds[:, 0:256] + ds_left
            ds[:, 256:512] = ds[:, 256:512] + ds_right


def pair_grads(first, starts, core, proj, dstate, normed, dproj, o_send, o_keep, send, keep, final):
    k2, v2, e2 = proj[:, 128:256], proj[:, 256:384], proj[:, 384:512]
    count = k2.shape[0]
    dmk, dmv, dz_out = unpack_state(dstate)
    leaving = (
        doc_of(starts, column(first, count)) == doc_of(starts, first + count - 1)
    ).astype(F32)
    em = e2 * leaving
    final[:, 0:128] = dproj[:, 0:128]
    final[:, 128:256] = dproj[:, 128:256] + nt(em, dmk)
    final[:, 256:384] = dproj[:, 256:384] + nn(em, dmv)
    de = dproj[:, 384:512] + leaving * (nn(k2, dmk) + nt(v2, dmv) + dz_out)
    final[:, 384:512] = e2 * de
    send[:, 0:512] = tn(lane_slice(normed, 1 - core, 256), final[...])
    keep[:, 0:512] = tn(lane_slice(normed, core, 256), final[...])
    send[:, 512:640] = o_send
    keep[:, 512:640] = o_keep


def first_back_kernel(
    scal, x, gain, d_hidden, f0, f1, f2, f3, a0, b0, a1, b1, grads2, wq, wk, wv, wc,
    grad_x, grads, cat, acc, held, sems,
):
    core, pair = scal[1], scal[2]
    copies = [
        pltpu.make_async_copy(ref, held.at[w], sems.at[w])
        for w, ref in enumerate((wq, wk, wv, wc))
    ]
    for copy in copies:
        copy.start()
    for j, ref in enumerate((f0, f1)):
        which = jnp.bitwise_xor(pair, j)
        for w in range(4):
            start = pl.multiple_of(w * 256 + which * 128, 128)
            cat[:, pl.ds(start, 128)] = ref[:, w * 128 : (w + 1) * 128]
    total = None
    for w, copy in enumerate(copies):
        copy.wait()
        part = nt(cat[:, w * 256 : (w + 1) * 256], held[w])
        total = part if total is None else total + part
    acc[...] = total
    for which, refs in ((core, (a0, a1)), (1 - core, (b0, b1))):
        part = nt(f2[...], refs[0][...]) + nt(f3[...], refs[1][...])
        lanes = pl.ds(pl.multiple_of(which * 256, 256), 256)
        acc[:, lanes] = acc[:, lanes] + part
    d_normed = acc[...]
    nhat, r = normalize(x[:, 0, :])
    grads[...] = jnp.zeros(grads.shape, F32)
    grads[0:1, 0:512] = jnp.sum(d_normed * nhat, axis=0, keepdims=True)
    grads[1:2, 0:512] = jnp.sum(d_normed, axis=0, keepdims=True)
    grads[2:4, 0:512] = grads2[0:2, :]
    grad_x[:, 0, :] = d_hidden[...] + norm_back(d_normed, nhat, r, gain[...])


def add(groups, packed=False, after=(), light=True):
    arrays = []
    places = []
    for group in groups:
        places.append([])
        for array, lead in group:
            at = next((i for i, a in enumerate(arrays) if a is array), None)
            if at is None:
                at = len(arrays)
                arrays.append(array)
            places[-1].append((at, lead))
    shapes = [group[0][0].shape[-2:] for group in groups]
    outs = shapes
    if packed:
        outs = [(sum(s[0] for s in shapes), shapes[0][1])]

    def kernel(*refs):
        row = 0
        for g, group in enumerate(places):
            value = None
            for at, lead in group:
                term = refs[at][...] if lead is None else refs[at][lead]
                value = term if value is None else value + term
            if packed:
                refs[len(arrays)][row : row + shapes[g][0], :] = value
                row += shapes[g][0]
            else:
                refs[len(arrays) + g][...] = value

    return run(kernel, outs, (), arrays, after=after, light=light)


def pick(first, second, scal, after=()):
    arrays = []
    places = [[], []]
    for group, place in zip((first, second), places):
        for array, lead in group:
            at = next((i for i, a in enumerate(arrays) if a is array), None)
            if at is None:
                at = len(arrays)
                arrays.append(array)
            place.append((at, lead))

    def kernel(scal, *refs):
        sums = []
        for place in places:
            value = None
            for at, lead in place:
                term = refs[at][...] if lead is None else refs[at][lead]
                value = term if value is None else value + term
            sums.append(value)
        for side in range(2):

            @pl.when(scal[2] == side)
            def _():
                refs[-2][...] = sums[1 - side]
                refs[-1][...] = sums[side]

    shape = first[0][0].shape[-2:]
    return run(kernel, [shape] * 2, (scal,), arrays, after=after, light=True)


def halve(terms, gains, scal, at, tail=8, after=()):
    rows, cols = terms[0][0].shape[-2:]
    rows -= 0 if gains else tail
    arrays = [a for a, _ in terms] + list(gains)
    leads = [lead for _, lead in terms]

    def kernel(scal, *refs):
        ins, extra = refs[: len(leads)], refs[len(leads) : len(arrays)]
        for out, which in ((refs[-2], 1 - scal[at]), (refs[-1], scal[at])):
            block = pl.ds(pl.multiple_of(which * (rows // 2), rows // 2), rows // 2)
            value = None
            for ref, lead in zip(ins, leads):
                term = ref[block, :] if lead is None else ref[lead, block, :]
                value = term if value is None else value + term
            out[0 : rows // 2, :] = value
            if tail:
                last = None
                for ref in extra or ins:
                    term = ref[...] if extra else ref[rows : rows + tail, :]
                    last = term if last is None else last + term
                out[rows // 2 :, :] = last

    return run(kernel, [(rows // 2 + tail, cols)] * 2, (scal,), arrays, after=after, light=True)


def join(here, there, scal, at, tail=8, after=()):
    rows, cols = here.shape
    rows -= tail

    def kernel(scal, here, there, out):
        for ref, which in ((here, scal[at]), (there, 1 - scal[at])):
            block = pl.ds(pl.multiple_of(which * rows, rows), rows)
            out[block, :] = ref[0:rows, :]
        if tail:
            out[2 * rows :, :] = here[rows:, :]

    return run(kernel, [(2 * rows + tail, cols)], (scal,), (here, there), after=after, light=True)[0]


def hidden_assemble_kernel(scal, p0, p1, p2, p3, up, down):
    core, pair = scal[1], scal[2]
    for side in range(2):

        @pl.when(pair == side)
        def _():
            for k, ref in enumerate((p0, p1, p2, p3)):
                for far in range(2):
                    block = jnp.bitwise_xor(scal[3], (2 - 2 * far) + (k & 1))
                    where = pl.ds(pl.multiple_of(block * 256, 256), 256)
                    rows = slice(far * 256, (far + 1) * 256)
                    if (k >> 1) == side:
                        up[0:256, where] = ref[rows, 0:256]
                        up[256:512, where] = ref[rows, 256:512]
                    else:
                        down[where, :] = ref[rows, :]


def qkvc_assemble_kernel(scal, p0, p1, p2, p3, wq, wk, wv, wc, wo, gains):
    core, pair = scal[1], scal[2]
    for j, ref in enumerate((p0, p1, p2, p3)):
        half = jnp.bitwise_xor(core, j & 1)
        which = jnp.bitwise_xor(pair, j >> 1)
        rows = pl.ds(pl.multiple_of(half * 256, 256), 256)
        lanes = pl.ds(pl.multiple_of(which * 128, 128), 128)
        for w, out in enumerate((wq, wk, wv, wc)):
            out[rows, lanes] = ref[0:256, w * 128 : (w + 1) * 128]
        out_rows = pl.ds(pl.multiple_of(which * 128 + half * 64, 64), 64)
        for b in range(4):
            wo[out_rows, b * 128 : (b + 1) * 128] = ref[b * 64 : (b + 1) * 64, 512:640]
    tails = [ref[256:264, 0:512] for ref in (p0, p1, p2, p3)]
    gains[...] = (tails[0] + tails[1]) + (tails[2] + tails[3])


def per_device(
    inputs, doc_starts, query_weight, key_weight, value_weight, control_weight, output_weight,
    up_weight, down_weight, first_gain, first_shift, second_gain, second_shift, cotangent,
):
    rows, _, width = inputs.shape
    devices = lax.axis_size("dp")
    place = lax.axis_index("dp").astype(jnp.int32)
    y = lax.axis_index("head").astype(jnp.int32)
    core = place & 1
    pair = (place >> 1) & 1
    one = lambda *v: jnp.stack([jnp.asarray(a, jnp.int32) for a in v])
    depth = (place >> 2) & 1
    bits = [at for at in range(31) if (1 << at) < devices]
    scal = one(y * rows, core, pair, depth * 2 + core, *((place >> at) & 1 for at in bits))
    gain1, shift1 = first_gain.reshape(1, width), first_shift.reshape(1, width)
    gain2, shift2 = second_gain.reshape(1, width), second_shift.reshape(1, width)
    weights = (query_weight, key_weight, value_weight, control_weight)

    def swap_y(a):
        return lax.ppermute(a, "head", [(0, 1), (1, 0)])

    def swap(a, bits):
        return lax.ppermute(a, "dp", [(i, i ^ bits) for i in range(devices)])

    to_second = lambda a: lax.ppermute(a, "head", [(0, 1)])
    to_first = lambda a: lax.ppermute(a, "head", [(1, 0)])

    tables = (scal, doc_starts)
    (piece,) = cut(cut_first_kernel, [(256, 512)], scal, weights, limit=60 * 2**20, near=True)
    qa0 = swap_y(piece)
    normed, proj_own, states_own = run(
        own_kernel,
        [(rows, width), (2, rows, 512), (2, 136, 128)],
        tables,
        (inputs, gain1, shift1) + weights,
        (pltpu.VMEM((4, width, 256), F32), pltpu.SemaphoreType.DMA((4,))),
        after=(piece,),
        far=4,
    )
    carry_oth = to_second(states_own)
    qa0 = tie(qa0, (carry_oth,))
    qb0 = swap(qa0, 1)
    qa1 = swap(qa0, 2)
    (unit,) = cut(
        cut_second_kernel, [(320, 512)], scal, (output_weight, up_weight, down_weight), (qa0,)
    )
    unit0 = swap_y(unit)

    def project(wa, wb, after):
        return run(
            other_kernel, [(rows, 512), (136, 128)], tables, (normed, wa, wb),
            after=after,
        )

    def attend(proj, carry, j, after=()):
        def kernel(scal, starts, proj, carry, o, saved):
            state = carry[own_pair(scal, j - 2)] if j >= 2 else carry[...]
            attention_kernel(scal, starts, proj, state, o, saved, j if j < 2 else None)

        return run(
            kernel, [(rows, 128), (rows, 384)], tables, (proj, carry), after=after
        )

    proj_oth0, state0 = project(qa0, qb0, (unit,))
    carry_own0 = to_second(state0)
    o2, saved2 = attend(proj_oth0, carry_oth, 2)
    qa1 = tie(qa1, (o2,))
    qb1 = swap(qa1, 1)
    unit0 = tie(unit0, (qa1,))
    unit1, unit2, unit4 = swap(unit0, 1), swap(unit0, 2), swap(unit0, 4)
    proj_oth1, state1 = project(qa1, qb1, ())
    carry_own1 = to_second(state1)
    o3, saved3 = attend(proj_oth1, carry_oth, 3)
    o0, saved0 = attend(proj_own, carry_own0, 0, (o3, carry_own1))
    unit2 = tie(unit2, (o0,))
    unit3, unit6 = swap(unit2, 1), swap(unit2, 4)
    o1, saved1 = attend(proj_own, carry_own1, 1, (unit2,))
    hidden, second, o_all, w_all = run(
        middle_kernel,
        [(rows, width), (rows, width), (rows, 512), (512, width)],
        (scal,),
        (o0, o1, o2, o3, inputs, output_weight, unit0, unit1, unit2, unit3, gain2, shift2),
    )
    saved = (saved0, saved1, saved2, saved3)

    def feed_forward(j, unit, other, after=()):
        return run(
            lambda *refs: feed_forward_kernel(j, *refs),
            [(4, 256, 512), (rows, width), (rows, width)],
            (scal,),
            (second, cotangent, up_weight, down_weight, unit, other),
            (pltpu.VMEM((width, 256), F32), pltpu.VMEM((256, width), F32)),
            after=after,
        )

    part1, out1, ds1 = feed_forward(1, unit1, unit3)
    got1 = swap(part1, 1)
    part0, out0, ds0 = feed_forward(0, unit0, unit2, (ds1,))
    unit4, unit6 = tie(unit4, (ds0,)), tie(unit6, (ds0,))
    unit5, unit7 = swap(unit4, 1), swap(unit6, 1)
    up_send, down_own, down_oth = add(
        [[(part0, 2), (got1, 2)], [(part0, 1), (got1, 1)], [(part0, 3), (got1, 3)]]
    )
    up_got = swap_y(up_send)
    down_own, down_oth = swap(down_own, 4), swap(down_oth, 4)
    part3, out3, ds3 = feed_forward(3, unit5, unit7, (up_send,))
    got3 = swap(part3, 1)
    part2, out2, ds2 = feed_forward(2, unit4, unit6, (ds3,))
    up_send0, up_sum = add(
        [[(part2, 2), (got3, 2)], [(part0, 0), (got1, 0), (up_got, None)]], after=(ds2,)
    )
    up_got0 = swap_y(up_send0)
    up_far = swap(up_sum, 4)
    outputs, d_hidden, grads2, d_o, o_send, o_keep = run(
        middle_back_kernel,
        [inputs.shape, (rows, width), (8, width), (rows, 512), (4, 256, 128), (4, 256, 128)],
        (scal,),
        (hidden, cotangent, ds0, ds1, ds2, ds3, out0, out1, out2, out3, gain2, o_all, w_all),
        (pltpu.VMEM((512, width), F32),),
        after=(up_sum,),
    )
    (down_send0,) = add(
        [[(part2, 3), (got3, 3), (down_oth, None)]], after=(d_hidden,)
    )
    down_got0 = swap_y(down_send0)

    def back(js, after=()):
        arrays = (proj_own, proj_oth0, proj_oth1, carry_oth, carry_own0, carry_own1, d_o) + saved

        def kernel(scal, starts, own, oth0, oth1, c_oth, c_own0, c_own1, d_o, *rest):
            dproj, dstate = rest[4:]
            for k, j in enumerate(js):
                if j < 2:
                    proj = own.at[own_pair(scal, j)]
                    carry = (c_own0, c_own1)[j][...]
                else:
                    proj = (oth0, oth1)[j - 2]
                    carry = c_oth[own_pair(scal, j - 2)]
                dstate[len(js) - 1 - k] = attention_back(
                    scal[0], starts, proj, carry, rest[j], d_o,
                    slice(j * 128, (j + 1) * 128), dproj.at[k],
                )

        return run(
            kernel,
            [(len(js), rows, 512), (len(js), 136, 128)],
            tables,
            arrays,
            after=after,
        )

    def weight_grads(j, dstate, dproj, after=()):
        proj = proj_own if j < 2 else (proj_oth0, proj_oth1)[j - 2]

        def kernel(scal, starts, proj, normed, o_send, o_keep, dstate, dproj, send, keep, final):
            here = proj.at[own_pair(scal, j)] if j < 2 else proj
            pair_grads(
                scal[0], starts, scal[1], here, dstate[0], normed, dproj.at[0],
                o_send[j], o_keep[j], send, keep, final,
            )

        return run(
            kernel,
            [(256, 640), (256, 640), (rows, 512)],
            tables,
            (proj, normed, o_send, o_keep, dstate, dproj),
            after=after,
            light=True,
        )

    dproj1, dstate1 = back((1,), (down_send0,))
    dstate1 = to_first(dstate1)
    dproj3, dstate3 = back((3,), (dproj1,))
    dstate3 = to_first(dstate3)
    ff_bits = [1] + bits[3:]
    ff_send, ff_keep = pick(
        [(part2, 0), (got3, 0), (up_got0, None), (up_far, None)],
        [(part2, 1), (got3, 1), (down_own, None), (down_got0, None)],
        scal, (dproj3,),
    )
    ff_got = swap(ff_send, 2)
    send3, keep3, final3 = weight_grads(3, dstate1, dproj3, (ff_send,))
    got3 = swap(send3, 1)
    send1, keep1, final1 = weight_grads(1, dstate3, dproj1, (final3,))
    got1 = swap(send1, 1)
    (y_send1,) = add([[(keep3, None), (got3, None)]], after=(final1,))
    y_got1 = swap_y(y_send1)
    dproj0, dstate0 = back((0,), (y_send1,))
    dstate0 = to_first(dstate0)
    dproj2, dstate2 = back((2,), (dproj0,))
    dstate2 = to_first(dstate2)
    send2, keep2, final2 = weight_grads(2, dstate0, dproj2, (dproj2,))
    got2 = swap(send2, 1)
    for at in ff_bits[1:]:
        ff_send, ff_keep = halve(
            [(ff_keep, None), (ff_got, None)], (), scal, at + 4, 0, (final2,)
        )
        ff_got = swap(ff_send, 1 << at)
    send0, keep0, final0 = weight_grads(0, dstate2, dproj0, (ff_send,))
    got0 = swap(send0, 1)
    y_send0, x_send1 = add(
        [[(keep2, None), (got2, None)], [(keep1, None), (got1, None), (y_got1, None)]],
        after=(final0,),
    )
    y_got0 = swap_y(y_send0)
    x_got1 = swap(x_send1, 2)
    grad_inputs, grads1 = run(
        first_back_kernel,
        [inputs.shape, (8, 640)],
        (scal,),
        (inputs, gain1, d_hidden, final0, final1, final2, final3, qa0, qb0, qa1, qb1, grads2)
        + weights,
        (
            pltpu.VMEM((rows, 1024), F32),
            pltpu.VMEM((rows, width), F32),
            pltpu.VMEM((4, width, 256), F32),
            pltpu.SemaphoreType.DMA((4,)),
        ),
        after=(y_send0,),
        far=4,
        light=True,
    )
    gains_got = swap_y(grads1)
    (ff_shard,) = add([[(ff_keep, None), (ff_got, None)]], after=(grads1,))
    turn = ff_shard
    ff_steps = list(reversed(ff_bits[1:]))
    ff_there = swap(ff_shard, 1 << ff_steps[0])
    terms = [(keep0, None), (got0, None), (y_got0, None), (x_got1, None)]
    gains = (grads1, gains_got)
    for at in bits[2:]:
        send, keep = halve(terms, gains, scal, at + 4, after=(turn,))
        terms, gains = [(keep, None), (swap(send, 1 << at), None)], ()
        turn = send
        if ff_steps:
            step = ff_steps.pop(0)
            ff_shard = join(ff_shard, ff_there, scal, step + 4, 0, (turn,))
            turn = ff_shard
            ff_there = swap(ff_shard, 1 << (ff_steps[0] if ff_steps else 2))
    (ff_pair,) = add([[(ff_shard, None)], [(ff_there, None)]], packed=True, after=(turn,))
    ff_x = swap(ff_pair, 2)
    ff_core = swap(ff_pair, 1)
    (shard,) = add([terms], after=(ff_pair,))
    steps = list(reversed(bits[2:]))
    for n, at in enumerate(steps):
        shard = join(shard, swap(shard, 1 << at), scal, at + 4)
        if n == 0:
            ff_x = tie(ff_x, (shard,))
            ff_x_core = swap(ff_x, 1)
    far = swap(shard, 2)
    grad_up, grad_down = run(
        hidden_assemble_kernel,
        [up_weight.shape, down_weight.shape],
        (scal,),
        (ff_pair, ff_core, ff_x, ff_x_core),
        after=(shard,),
    )
    grad_query, grad_key, grad_value, grad_control, grad_output, gains = run(
        qkvc_assemble_kernel,
        [w.shape for w in weights] + [output_weight.shape, (8, width)],
        (scal,),
        (shard, swap(shard, 1), far, swap(far, 1)),
        after=(grad_up,),
    )
    return (
        outputs, grad_inputs,
        grad_query, grad_key, grad_value, grad_control, grad_output, grad_up, grad_down,
        gains[0], gains[1], gains[2], gains[3],
    )


def solution(mesh):
    rows = P("head", "dp", None)
    cols = P(None, "head")
    tall = P("head", None)
    flat = P()
    return jax.shard_map(
        per_device,
        mesh=mesh,
        in_specs=(
            rows, P("dp", None), cols, cols, cols, cols, tall, cols, tall,
            flat, flat, flat, flat, rows,
        ),
        out_specs=(
            rows, rows, cols, cols, cols, cols, tall, cols, tall, flat, flat, flat, flat,
        ),
        check_vma=False,
    )
```

```python
import jax
import jax.numpy as jnp
from jax import lax
from jax.experimental import pallas as pl
from jax.experimental.pallas import tpu as pltpu
from jax.sharding import PartitionSpec as P

F32 = jnp.float32
HIGH = lax.Precision.HIGH
CHUNK = 256
EPS = 1e-05
GELU_C = 0.7978845608028654
GELU_K = 0.044715
VMEM_LIMIT = 16 * 2**20


def dot(left, right, dims):
    return lax.dot_general(
        left, right, (dims, ((), ())), precision=HIGH, preferred_element_type=F32
    )


def nn(left, right):
    return dot(left, right, ((1,), (0,)))


def nt(left, right):
    return dot(left, right, ((1,), (1,)))


def tn(left, right):
    return dot(left, right, ((0,), (0,)))


def whole():
    return pl.BlockSpec(memory_space=pltpu.VMEM)


def anywhere():
    return pl.BlockSpec(memory_space=pl.ANY)


def distant():
    return pl.BlockSpec(memory_space=pltpu.HBM)


def scalars():
    return pl.BlockSpec(memory_space=pltpu.SMEM)


FRONT, HEAVY, LATE, SUM = 50.0, 50.0, 50.0, 50.0


def cost(us):
    return pl.CostEstimate(flops=int(us * 1153e6), bytes_accessed=0, transcendentals=0)


def run(kernel, outs, scal, arrays, scratch=(), after=(), far=0, us=HEAVY):
    out_shape = [jax.ShapeDtypeStruct(shape, F32) for shape in outs]
    first, last = len(scal) + len(arrays), len(scal) + len(arrays) + len(after)
    return pl.pallas_call(
        lambda *refs: kernel(*refs[:first], *refs[last:]),
        out_shape=out_shape,
        in_specs=[scalars()] * len(scal)
        + [whole()] * (len(arrays) - far)
        + [distant()] * far
        + [anywhere()] * len(after),
        out_specs=[whole()] * len(outs),
        scratch_shapes=list(scratch),
        compiler_params=pltpu.CompilerParams(vmem_limit_bytes=VMEM_LIMIT),
        cost_estimate=cost(us),
    )(*scal, *arrays, *after)


def tie(array, after):
    count = 1 + len(after)
    return pl.pallas_call(
        lambda *refs: None,
        out_shape=jax.ShapeDtypeStruct(array.shape, F32),
        in_specs=[anywhere()] * count,
        out_specs=anywhere(),
        input_output_aliases={0: 0},
        compiler_params=pltpu.CompilerParams(vmem_limit_bytes=2**20),
        cost_estimate=pl.CostEstimate(flops=0, bytes_accessed=0, transcendentals=0),
    )(array, *after)


def spacer(*after):
    return pl.pallas_call(
        lambda *refs: None,
        out_shape=jax.ShapeDtypeStruct((8, 128), F32),
        in_specs=[anywhere()] * len(after),
        out_specs=anywhere(),
        compiler_params=pltpu.CompilerParams(vmem_limit_bytes=2**20),
        cost_estimate=cost(HEAVY),
    )(*after)


def lane_slice(ref, index, width):
    return ref[:, pl.ds(pl.multiple_of(index * width, width), width)]


def normalize(x):
    centre = x - jnp.mean(x, axis=-1, keepdims=True)
    spread = jnp.mean(centre * centre, axis=-1, keepdims=True)
    r = lax.rsqrt(spread + EPS)
    return centre * r, r


def norm_back(dy, nhat, r, gain):
    dyg = dy * gain
    first = jnp.mean(dyg, axis=-1, keepdims=True)
    second = jnp.mean(dyg * nhat, axis=-1, keepdims=True)
    return r * (dyg - first - nhat * second)


def doc_of(starts, position):
    total = jnp.zeros(jnp.shape(position), jnp.int32)
    for k in range(starts.shape[1]):
        total = total + (position >= starts[0, k]).astype(jnp.int32)
    return total


def column(first, count):
    return first + lax.broadcasted_iota(jnp.int32, (count, 1), 0)


def left_lanes():
    return lax.broadcasted_iota(jnp.int32, (1, 128), 1) < 64


def pack_state(mk, mv, z):
    left = left_lanes()
    return jnp.concatenate(
        [
            jnp.where(left, mk[0:64], mk[64:128]),
            jnp.where(left, mv[0:64], mv[64:128]),
            jnp.broadcast_to(z, (8, 128)),
        ],
        axis=0,
    )


def blocks_only(m):
    diagonal = (lax.broadcasted_iota(jnp.int32, (128, 128), 0) < 64) == (
        lax.broadcasted_iota(jnp.int32, (128, 128), 1) < 64
    )
    return jnp.where(diagonal, m, 0.0)


def unpack_state(state):
    mk = state[0:64]
    mv = state[64:128]
    return (
        blocks_only(jnp.concatenate([mk, mk], axis=0)),
        blocks_only(jnp.concatenate([mv, mv], axis=0)),
        state[128:129],
    )


def end_state(k2, v2, e2, starts, first):
    count = k2.shape[0]
    kept = (doc_of(starts, column(first, count)) == doc_of(starts, first + count - 1)).astype(F32)
    em = e2 * kept
    return pack_state(outer(k2, em), outer(em, v2), jnp.sum(em, axis=0, keepdims=True))


def cut_first_kernel(scal, wq, wk, wv, wc, piece, sems):
    rows = pl.ds(pl.multiple_of(scal[1] * 256, 256), 256)
    lanes = pl.ds(pl.multiple_of(scal[2] * 128, 128), 128)
    copies = [
        pltpu.make_async_copy(
            ref.at[rows, lanes], piece.at[:, w * 128 : (w + 1) * 128], sems.at[w]
        )
        for w, ref in enumerate((wq, wk, wv, wc))
    ]
    for copy in copies:
        copy.start()
    for copy in copies:
        copy.wait()


def cut_second_kernel(scal, wo, up, down, piece, sems):
    unit = pl.ds(pl.multiple_of(scal[3] * 256 + scal[2] * 128, 128), 128)
    thin = pl.ds(pl.multiple_of((scal[2] * 2 + scal[1]) * 64, 64), 64)
    copies = [
        pltpu.make_async_copy(
            up.at[b * 128 : (b + 1) * 128, unit], piece.at[0:128, b * 128 : (b + 1) * 128],
            sems.at[b],
        )
        for b in range(4)
    ]
    copies.append(pltpu.make_async_copy(down.at[unit, :], piece.at[128:256, :], sems.at[4]))
    copies.append(pltpu.make_async_copy(wo.at[thin, :], piece.at[256:320, :], sems.at[5]))
    for copy in copies:
        copy.start()
    for copy in copies:
        copy.wait()


def cut(kernel, shapes, scal, arrays, after=(), limit=2**20, near=False):
    first, last = 1 + len(arrays), 1 + len(arrays) + len(after)
    out_shape = [jax.ShapeDtypeStruct(shape, F32) for shape in shapes]
    return pl.pallas_call(
        lambda *refs: kernel(*refs[:first], *refs[last:]),
        out_shape=out_shape,
        in_specs=[scalars()] + [distant()] * len(arrays) + [anywhere()] * len(after),
        out_specs=[whole() if near else anywhere()] * len(shapes),
        scratch_shapes=[pltpu.SemaphoreType.DMA((6,))],
        compiler_params=pltpu.CompilerParams(vmem_limit_bytes=limit),
        cost_estimate=cost(FRONT),
    )(scal, *arrays, *after)


def own_kernel(scal, starts, x, gain, shift, wq, wk, wv, wc, normed, proj, states, held, sems):
    copies = [
        pltpu.make_async_copy(ref, held.at[w], sems.at[w])
        for w, ref in enumerate((wq, wk, wv, wc))
    ]
    for copy in copies:
        copy.start()
    nhat, _ = normalize(x[:, 0, :])
    n = nhat * gain[...] + shift[...]
    normed[...] = n
    for w, copy in enumerate(copies):
        copy.wait()
        full = nn(n, held[w])
        if w == 3:
            full = jnp.exp(full)
        for p in range(2):
            proj[p, :, w * 128 : (w + 1) * 128] = full[:, p * 128 : (p + 1) * 128]
    for p in range(2):
        states[p] = end_state(
            proj[p, :, 128:256], proj[p, :, 256:384], proj[p, :, 384:512], starts, scal[0]
        )


def other_kernel(scal, starts, normed, wa, wb, proj, states, before=None):
    core = scal[1]
    full = nn(lane_slice(normed, core, 256), wa[...]) + nn(
        lane_slice(normed, 1 - core, 256), wb[...]
    )
    proj[:, 0:384] = full[:, 0:384]
    proj[:, 384:512] = jnp.exp(full[:, 384:512])
    state = end_state(proj[:, 128:256], proj[:, 256:384], proj[:, 384:512], starts, scal[0])
    if before is None:
        states[...] = state
    else:
        states[0] = before[...]
        states[1] = state


def chunk_masks(starts, first, c):
    begin = first + c * CHUNK
    position = column(begin, CHUNK)
    docs = doc_of(starts, position)
    row = begin + lax.broadcasted_iota(jnp.int32, (1, CHUNK), 1)
    mask = (position >= row) & (docs == doc_of(starts, row))
    before = doc_of(starts, begin - 1)
    last = doc_of(starts, begin + CHUNK - 1)
    entering = (docs == before).astype(F32)
    leaving = (docs == last).astype(F32)
    passing = (before == last).astype(F32)
    return mask, entering, leaving, passing


BF16 = jnp.bfloat16


def raw(left, right, dims):
    return lax.dot_general(left, right, (dims, ((), ())), preferred_element_type=F32)


def rest_of(x):
    return x - x.astype(BF16).astype(F32)


def turn(x):
    return pltpu.roll(x, 64, 1)


def beside(a, b):
    return jnp.concatenate([a, b], axis=1).astype(BF16)


def rows_factor(x):
    left = left_lanes()
    low = turn(rest_of(x))
    return (
        beside(jnp.where(left, x, low), jnp.where(left, x, 0.0)),
        beside(jnp.where(left, low, x), jnp.where(left, 0.0, x)),
    )


def columns_factor(x):
    left = left_lanes()
    other = turn(x)
    low = rest_of(x)
    return (
        beside(jnp.where(left, x, other), low),
        beside(jnp.where(left, other, x), low),
    )


def affinity_of(rows, columns, mask):
    result = []
    for r, c in zip(rows, columns):
        value = jnp.where(mask, raw(r, c, ((1,), (1,))), 0.0)
        high = value.astype(BF16)
        result.append((high, (value - high.astype(F32)).astype(BF16)))
    return result


def narrow(x):
    left = left_lanes()
    low = rest_of(x)
    return (
        jnp.where(left, x, turn(low)).astype(BF16),
        jnp.where(left, turn(low), x).astype(BF16),
    )


def gather_heads(first, second):
    left = left_lanes()
    return jnp.where(left, first, second) + turn(jnp.where(left, second, first))


def spread(matrices, x):
    outs = []
    for (high, low), part in zip(matrices, x):
        outs.append(raw(high, part, ((1,), (0,))) + raw(low, part, ((1,), (0,))))
    return gather_heads(*outs)


def spread_back(matrices, x):
    outs = []
    for (high, low), part in zip(matrices, x):
        outs.append(raw(high, part, ((0,), (0,))) + raw(low, part, ((0,), (0,))))
    return gather_heads(*outs)


def fold(x):
    return x[:, 0:128] + x[:, 128:256]


def both_parts(x):
    return beside(x, rest_of(x))


def masked_sum(mask, x):
    return fold(raw(mask, both_parts(x), ((1,), (0,))))


def masked_sum_back(mask, x):
    return fold(raw(mask, both_parts(x), ((0,), (0,))))


def times_state(x, m):
    part = both_parts(m)
    return fold(raw(both_parts(x), jnp.concatenate([part, part], axis=0), ((1,), (0,))))


def times_state_back(x, m):
    low = rest_of(m)
    right = jnp.concatenate([beside(m, m), beside(low, low)], axis=0)
    return fold(raw(both_parts(x), right, ((1,), (1,))))


def outer(x, y):
    full = raw(both_parts(x), both_parts(y), ((0,), (0,)))
    return blocks_only(fold(full[0:128] + full[128:256]))


def slot_sums(x):
    left = left_lanes()
    return jnp.where(
        left,
        jnp.sum(jnp.where(left, x, 0.0), axis=1, keepdims=True),
        jnp.sum(jnp.where(left, 0.0, x), axis=1, keepdims=True),
    )


def next_state(k2, v2, e2, state, leaving, passing):
    mk, mv, z_in = state
    em = e2 * leaving
    return (
        outer(k2, em) + passing * mk,
        outer(em, v2) + passing * mv,
        jnp.sum(em, axis=0, keepdims=True) + passing * z_in,
    )


def attention(first, starts, proj, carry, o, lanes, saved):
    left = left_lanes()
    state = unpack_state(carry)
    chunks = proj.shape[0] // CHUNK
    for c in range(chunks):
        rows = slice(c * CHUNK, (c + 1) * CHUNK)
        q2, k2 = proj[rows, 0:128], proj[rows, 128:256]
        v2, e2 = proj[rows, 256:384], proj[rows, 384:512]
        mask, entering, leaving, passing = chunk_masks(starts, first, c)
        mk, mv, z_in = state
        z = masked_sum(mask.astype(F32).astype(BF16), e2) + entering * z_in
        affinity = affinity_of(rows_factor(q2), columns_factor(k2), mask)
        total = spread(affinity, narrow(e2)) + entering * times_state(q2, mk)
        s = total / z * 0.125
        top = jnp.where(
            left,
            jnp.max(jnp.where(left, s, -jnp.inf), axis=1, keepdims=True),
            jnp.max(jnp.where(left, -jnp.inf, s), axis=1, keepdims=True),
        )
        p = jnp.exp(s - top)
        p = p / slot_sums(p)
        r = p / z
        mixing = affinity_of(rows_factor(r), columns_factor(e2), mask)
        o[rows, lanes] = spread(mixing, narrow(v2)) + entering * times_state(r, mv)
        saved[rows, 0:128] = z
        saved[rows, 128:256] = s
        saved[rows, 256:384] = p
        if c + 1 < chunks:
            state = next_state(k2, v2, e2, state, leaving, passing)


def attention_back(first, starts, proj, carry, saved, d_o, lanes, dproj):
    chunks = proj.shape[0] // CHUNK
    states = [unpack_state(carry)]
    for c in range(chunks - 1):
        rows = slice(c * CHUNK, (c + 1) * CHUNK)
        _, _, leaving, passing = chunk_masks(starts, first, c)
        states.append(
            next_state(
                proj[rows, 128:256], proj[rows, 256:384], proj[rows, 384:512], states[c],
                leaving, passing,
            )
        )
    ahead = None
    for c in reversed(range(chunks)):
        rows = slice(c * CHUNK, (c + 1) * CHUNK)
        q2, k2 = proj[rows, 0:128], proj[rows, 128:256]
        v2, e2 = proj[rows, 256:384], proj[rows, 384:512]
        z, s, p = saved[rows, 0:128], saved[rows, 128:256], saved[rows, 256:384]
        do2 = d_o[rows, lanes]
        mask, entering, leaving, passing = chunk_masks(starts, first, c)
        mk, mv, _ = states[c]
        r = p / z
        do_in = entering * do2
        e_columns, e_narrow = columns_factor(e2), narrow(e2)
        mixing = affinity_of(rows_factor(r), e_columns, mask)
        d_mixing = affinity_of(rows_factor(do2), columns_factor(v2), mask)
        dv = spread_back(mixing, narrow(do2))
        dr = spread(d_mixing, e_narrow) + times_state_back(do_in, mv)
        de = spread_back(d_mixing, narrow(r))
        dp = dr / z
        dz = -dp * r
        ds = p * (dp - slot_sums(p * dp)) / z
        w = ds * 0.125
        dz = dz - ds * s
        w_in = entering * w
        affinity = affinity_of(rows_factor(q2), columns_factor(k2), mask)
        d_affinity = affinity_of(rows_factor(w), e_columns, mask)
        dq = spread(d_affinity, narrow(k2)) + times_state_back(w_in, mk)
        dk = spread_back(d_affinity, narrow(q2))
        de = de + spread_back(affinity, narrow(w))
        de = de + masked_sum_back(mask.astype(F32).astype(BF16), dz)
        if ahead is not None:
            dmk, dmv, dz_out = ahead
            em = e2 * leaving
            dv = dv + times_state(em, dmv)
            dk = dk + times_state_back(em, dmk)
            de = de + leaving * (times_state(k2, dmk) + times_state_back(v2, dmv) + dz_out)
        dproj[rows, 0:128] = dq
        dproj[rows, 128:256] = dk
        dproj[rows, 256:384] = dv
        dproj[rows, 384:512] = de
        now = (
            outer(q2, w_in),
            outer(r, do_in),
            jnp.sum(entering * dz, axis=0, keepdims=True),
        )
        if ahead is not None:
            now = tuple(a + passing * b for a, b in zip(now, ahead))
        ahead = now
    return pack_state(*ahead)


def own_pair(scal, j):
    return jnp.bitwise_xor(scal[2], j)


def attention_kernel(scal, starts, proj, carry, o, saved, j=None):
    here = proj if j is None else proj.at[own_pair(scal, j)]
    attention(scal[0], starts, here, carry, o, slice(0, 128), saved)


def middle_kernel(
    scal, o0, o1, o2, o3, x, wo, w0, w1, w2, w3, gain, shift, hidden, second, o_all, w_all,
):
    for j, ref in enumerate((o0, o1, o2, o3)):
        o_all[:, j * 128 : (j + 1) * 128] = ref[...]
    for j in range(2):
        which = pl.multiple_of(own_pair(scal, j) * 128, 128)
        w_all[j * 128 : (j + 1) * 128, :] = wo[pl.ds(which, 128), :]
    for k, ref in enumerate((w0, w1, w2, w3)):
        start = 256 + (k >> 1) * 128 + jnp.bitwise_xor(scal[1], k & 1) * 64
        w_all[pl.ds(pl.multiple_of(start, 64), 64), :] = ref[256:320, :]
    h = x[:, 0, :] + nn(o_all[...], w_all[...])
    hidden[...] = h
    nhat, _ = normalize(h)
    second[...] = nhat * gain[...] + shift[...]


def middle_back_kernel(
    scal, hidden, cot, ds0, ds1, ds2, ds3, u0, u1, u2, u3, gain, o_all, w_all,
    outputs, d_hidden, grads, d_o, send, keep, work,
):
    core = scal[1]
    outputs[:, 0, :] = hidden[...] + ((u0[...] + u1[...]) + (u2[...] + u3[...]))
    d_second = (ds0[...] + ds1[...]) + (ds2[...] + ds3[...])
    nhat, r = normalize(hidden[...])
    grads[0:1, :] = jnp.sum(d_second * nhat, axis=0, keepdims=True)
    grads[1:2, :] = jnp.sum(d_second, axis=0, keepdims=True)
    grads[2:8, :] = jnp.zeros((6, grads.shape[1]), F32)
    d = cot[:, 0, :] + norm_back(d_second, nhat, r, gain[...])
    d_hidden[...] = d
    d_o[...] = nt(d, w_all[...])
    work[...] = tn(o_all[...], d)
    for ref, which in ((send, 1 - core), (keep, core)):
        for j in range(4):
            rows = pl.ds(pl.multiple_of(j * 128 + which * 64, 64), 64)
            for b in range(4):
                ref[j, b * 64 : (b + 1) * 64, :] = work[rows, b * 128 : (b + 1) * 128]


def feed_forward_kernel(j, scal, second, cot, up, down, unit, other, packed, out, ds, up_far, down_far):
    where = pl.ds(pl.multiple_of(jnp.bitwise_xor(scal[3], j) * 256, 256), 256)
    for ref, half in ((unit, scal[2]), (other, 1 - scal[2])):
        place = pl.ds(pl.multiple_of(half * 128, 128), 128)
        for b in range(4):
            up_far[b * 128 : (b + 1) * 128, place] = ref[0:128, b * 128 : (b + 1) * 128]
        down_far[place, :] = ref[128:256, :]
    n_left, n_right = second[:, 0:256], second[:, 256:512]
    g = cot[:, 0, :]
    for half in range(2):
        if half == 0:
            up_left, up_right = up[0:256, where], up[256:512, where]
            down_block = down[where, :]
        else:
            up_left, up_right = up_far[0:256, :], up_far[256:512, :]
            down_block = down_far[...]
        u = nn(n_left, up_left) + nn(n_right, up_right)
        inner = GELU_C * (u + GELU_K * u * u * u)
        t = jnp.tanh(inner)
        act = 0.5 * u * (1.0 + t)
        slope = 0.5 * (1.0 + t) + 0.5 * u * (1.0 - t * t) * (
            GELU_C * (1.0 + 3.0 * GELU_K * u * u)
        )
        du = nt(g, down_block) * slope
        packed[2 * half, :, 0:256] = tn(n_left, du)
        packed[2 * half, :, 256:512] = tn(n_right, du)
        packed[2 * half + 1] = tn(act, g)
        out_part = nn(act, down_block)
        ds_left, ds_right = nt(du, up_left), nt(du, up_right)
        if half == 0:
            out[...] = out_part
            ds[:, 0:256] = ds_left
            ds[:, 256:512] = ds_right
        else:
            out[...] = out[...] + out_part
            ds[:, 0:256] = ds[:, 0:256] + ds_left
            ds[:, 256:512] = ds[:, 256:512] + ds_right


def pair_grads(first, starts, core, proj, dstate, normed, dproj, o_send, o_keep, send, keep, final):
    k2, v2, e2 = proj[:, 128:256], proj[:, 256:384], proj[:, 384:512]
    count = k2.shape[0]
    dmk, dmv, dz_out = unpack_state(dstate)
    leaving = (
        doc_of(starts, column(first, count)) == doc_of(starts, first + count - 1)
    ).astype(F32)
    em = e2 * leaving
    final[:, 0:128] = dproj[:, 0:128]
    final[:, 128:256] = dproj[:, 128:256] + times_state_back(em, dmk)
    final[:, 256:384] = dproj[:, 256:384] + times_state(em, dmv)
    de = dproj[:, 384:512] + leaving * (
        times_state(k2, dmk) + times_state_back(v2, dmv) + dz_out
    )
    final[:, 384:512] = e2 * de
    send[:, 0:512] = tn(lane_slice(normed, 1 - core, 256), final[...])
    keep[:, 0:512] = tn(lane_slice(normed, core, 256), final[...])
    send[:, 512:640] = o_send
    keep[:, 512:640] = o_keep


def first_back_kernel(
    scal, x, gain, d_hidden, f0, f1, f2, f3, a0, b0, a1, b1, grads2, wq, wk, wv, wc,
    grad_x, grads, cat, acc, held, sems,
):
    core, pair = scal[1], scal[2]
    copies = [
        pltpu.make_async_copy(ref, held.at[w], sems.at[w])
        for w, ref in enumerate((wq, wk, wv, wc))
    ]
    for copy in copies:
        copy.start()
    for j, ref in enumerate((f0, f1)):
        which = jnp.bitwise_xor(pair, j)
        for w in range(4):
            start = pl.multiple_of(w * 256 + which * 128, 128)
            cat[:, pl.ds(start, 128)] = ref[:, w * 128 : (w + 1) * 128]
    total = None
    for w, copy in enumerate(copies):
        copy.wait()
        part = nt(cat[:, w * 256 : (w + 1) * 256], held[w])
        total = part if total is None else total + part
    acc[...] = total
    for which, refs in ((core, (a0, a1)), (1 - core, (b0, b1))):
        part = nt(f2[...], refs[0][...]) + nt(f3[...], refs[1][...])
        lanes = pl.ds(pl.multiple_of(which * 256, 256), 256)
        acc[:, lanes] = acc[:, lanes] + part
    d_normed = acc[...]
    nhat, r = normalize(x[:, 0, :])
    grads[...] = jnp.zeros(grads.shape, F32)
    grads[0:1, 0:512] = jnp.sum(d_normed * nhat, axis=0, keepdims=True)
    grads[1:2, 0:512] = jnp.sum(d_normed, axis=0, keepdims=True)
    grads[2:4, 0:512] = grads2[0:2, :]
    grad_x[:, 0, :] = d_hidden[...] + norm_back(d_normed, nhat, r, gain[...])


def table_of(groups):
    arrays, places = [], []
    for group in groups:
        places.append([])
        for array, lead, part in group:
            at = next((i for i, a in enumerate(arrays) if a is array), None)
            if at is None:
                at = len(arrays)
                arrays.append(array)
            places[-1].append((at, lead, part))
    return arrays, places


def total(scal, refs, place):
    value = None
    for at, lead, part in place:
        ref = refs[at] if lead is None else refs[at].at[lead]
        if part is None:
            term = ref[...]
        else:
            rows = ref.shape[0] // 2
            which = jnp.bitwise_xor(scal[2], part) * rows
            term = ref[pl.ds(pl.multiple_of(which, rows), rows), :]
        value = term if value is None else value + term
    return value


def shape_of(group):
    array, _, part = group[0]
    rows, cols = array.shape[-2:]
    return (rows if part is None else rows // 2, cols)


def sums(outs, scal, after=(), rows=False):
    arrays, places = table_of([group for out in outs for group in out])
    shapes = []
    for out in outs:
        h, w = shape_of(out[0])
        if rows:
            shapes.append((sum(shape_of(g)[0] for g in out), w))
        else:
            shapes.append((h, w) if len(out) == 1 else (len(out), h, w))

    def kernel(scal, *refs):
        at = 0
        for n, out in enumerate(outs):
            target = refs[len(arrays) + n]
            row = 0
            for k in range(len(out)):
                value = total(scal, refs, places[at])
                at += 1
                if rows:
                    target[row : row + value.shape[0], :] = value
                    row += value.shape[0]
                elif len(out) == 1:
                    target[...] = value
                else:
                    target[k] = value

    return run(kernel, shapes, (scal,), arrays, after=after, us=SUM)


def choose(first, second, scal, at, after=()):
    arrays, places = table_of([first, second])

    def kernel(scal, *refs):
        values = [total(scal, refs, place) for place in places]
        for side in range(2):

            @pl.when(scal[at] == side)
            def _():
                refs[-2][...] = values[1 - side]
                refs[-1][...] = values[side]

    return run(kernel, [shape_of(first)] * 2, (scal,), arrays, after=after, us=SUM)


def halve(terms, gains, scal, at, tail=8, after=()):
    rows, cols = terms[0][0].shape[-2:]
    rows -= 0 if gains else tail
    arrays = [a for a, _ in terms] + list(gains)
    leads = [lead for _, lead in terms]

    def kernel(scal, *refs):
        ins, extra = refs[: len(leads)], refs[len(leads) : len(arrays)]
        for out, which in ((refs[-2], 1 - scal[at]), (refs[-1], scal[at])):
            block = pl.ds(pl.multiple_of(which * (rows // 2), rows // 2), rows // 2)
            value = None
            for ref, lead in zip(ins, leads):
                term = ref[block, :] if lead is None else ref[lead, block, :]
                value = term if value is None else value + term
            out[0 : rows // 2, :] = value
            if tail:
                last = None
                for ref in ins + extra:
                    if ref.shape[-2] == rows:
                        continue
                    first = 0 if ref.shape[-2] == tail else rows
                    term = ref[first : first + tail, :]
                    last = term if last is None else last + term
                out[rows // 2 :, :] = last

    return run(
        kernel, [(rows // 2 + tail, cols)] * 2, (scal,), arrays, after=after, us=SUM
    )


def join(here, there, scal, at, tail=8, after=()):
    rows, cols = here.shape
    rows -= tail

    def kernel(scal, here, there, out):
        for ref, which in ((here, scal[at]), (there, 1 - scal[at])):
            block = pl.ds(pl.multiple_of(which * rows, rows), rows)
            out[block, :] = ref[0:rows, :]
        if tail:
            out[2 * rows :, :] = here[rows:, :]

    return run(kernel, [(2 * rows + tail, cols)], (scal,), (here, there), after=after, us=SUM)[0]


def hidden_assemble_kernel(scal, p0, p1, p2, p3, up, down):
    for k, ref in enumerate((p0, p1, p2, p3)):
        half = jnp.bitwise_xor(scal[2], k >> 1) * 128
        for far in range(2):
            block = jnp.bitwise_xor(scal[3], (k & 1) + 2 - 2 * far)
            lanes = pl.ds(pl.multiple_of(block * 256, 256), 256)
            rows = slice(far * 256, far * 256 + 128)
            up[pl.ds(pl.multiple_of(half, 128), 128), lanes] = ref[rows, 0:256]
            up[pl.ds(pl.multiple_of(half + 256, 128), 128), lanes] = ref[rows, 256:512]
            where = pl.ds(pl.multiple_of(block * 256 + half, 128), 128)
            down[where, :] = ref[far * 256 + 128 : far * 256 + 256, :]


def qkvc_assemble_kernel(scal, *refs):
    (here, there), (wq, wk, wv, wc, wo, gains) = refs[:2], refs[2:]
    pieces = [ref.at[k] for ref in (here, there) for k in range(4)]
    size = here.shape[1] - 8
    tails = None
    for k, ref in enumerate(pieces):
        half = jnp.bitwise_xor(scal[1], k >> 2)
        which = jnp.bitwise_xor(scal[2], k & 1)
        first = jnp.bitwise_xor(scal[6], (k >> 1) & 1) * size
        rows = pl.ds(pl.multiple_of(half * 256 + first, size), size)
        lanes = pl.ds(pl.multiple_of(which * 128, 128), 128)
        for w, out in enumerate((wq, wk, wv, wc)):
            out[rows, lanes] = ref[0:size, w * 128 : (w + 1) * 128]
        for b in range(size // 64):
            start = pl.multiple_of(first // 64 * 128 + b * 128, 128)
            out_rows = pl.ds(pl.multiple_of(which * 128 + half * 64, 64), 64)
            wo[out_rows, pl.ds(start, 128)] = ref[b * 64 : (b + 1) * 64, 512:640]
        tail = ref[size : size + 8, 0:512]
        tails = tail if tails is None else tails + tail
    gains[...] = 0.5 * tails


def per_device(
    inputs, doc_starts, query_weight, key_weight, value_weight, control_weight, output_weight,
    up_weight, down_weight, first_gain, first_shift, second_gain, second_shift, cotangent,
):
    rows, _, width = inputs.shape
    devices = lax.axis_size("dp")
    place = lax.axis_index("dp").astype(jnp.int32)
    y = lax.axis_index("head").astype(jnp.int32)
    core = place & 1
    pair = (place >> 1) & 1
    one = lambda *v: jnp.stack([jnp.asarray(a, jnp.int32) for a in v])
    depth = (place >> 2) & 1
    bits = [at for at in range(31) if (1 << at) < devices]
    scal = one(y * rows, core, pair, depth * 2 + core, *((place >> at) & 1 for at in bits))
    gain1, shift1 = first_gain.reshape(1, width), first_shift.reshape(1, width)
    gain2, shift2 = second_gain.reshape(1, width), second_shift.reshape(1, width)
    weights = (query_weight, key_weight, value_weight, control_weight)

    def swap_y(a):
        return lax.ppermute(a, "head", [(0, 1), (1, 0)])

    def swap(a, bits):
        return lax.ppermute(a, "dp", [(i, i ^ bits) for i in range(devices)])

    to_second = lambda a: lax.ppermute(a, "head", [(0, 1)])
    to_first = lambda a: lax.ppermute(a, "head", [(1, 0)])

    tables = (scal, doc_starts)
    (piece,) = cut(cut_first_kernel, [(256, 512)], scal, weights, limit=60 * 2**20, near=True)
    qa0 = swap_y(piece)
    normed, proj_own, states_own = run(
        own_kernel,
        [(rows, width), (2, rows, 512), (2, 136, 128)],
        tables,
        (inputs, gain1, shift1) + weights,
        (pltpu.VMEM((4, width, 256), F32), pltpu.SemaphoreType.DMA((4,))),
        after=(piece,),
        far=4,
        us=FRONT,
    )
    carry_oth = to_second(states_own)
    qa0 = tie(qa0, (carry_oth,))
    qb0 = swap(qa0, 1)
    qa1 = swap(qa0, 2)
    (unit,) = cut(
        cut_second_kernel, [(320, 512)], scal, (output_weight, up_weight, down_weight), (qa0,)
    )
    unit0 = swap_y(unit)

    proj_oth0, state0 = run(
        other_kernel, [(rows, 512), (136, 128)], tables, (normed, qa0, qb0),
        after=(unit,), us=FRONT,
    )

    def attend(proj, carry, j, after=()):
        def kernel(scal, starts, proj, carry, o, saved):
            state = carry[own_pair(scal, j - 2)] if j >= 2 else carry[j]
            attention_kernel(scal, starts, proj, state, o, saved, j if j < 2 else None)

        return run(
            kernel, [(rows, 128), (rows, 384)], tables, (proj, carry), after=after, us=FRONT
        )

    qa1 = tie(qa1, (proj_oth0,))
    qb1 = swap(qa1, 1)
    o2, saved2 = attend(proj_oth0, carry_oth, 2, (qa1,))
    proj_oth1, states_oth = run(
        lambda scal, starts, normed, wa, wb, before, proj, states: other_kernel(
            scal, starts, normed, wa, wb, proj, states, before
        ),
        [(rows, 512), (2, 136, 128)], tables, (normed, qa1, qb1, state0),
        after=(o2,), us=FRONT,
    )
    unit0 = tie(unit0, (states_oth,))
    unit1, unit2, unit4 = swap(unit0, 1), swap(unit0, 2), swap(unit0, 4)
    carry_own = to_second(states_oth)
    o3, saved3 = attend(proj_oth1, carry_oth, 3, (unit0,))
    o0, saved0 = attend(proj_own, carry_own, 0, (o3,))
    o1, saved1 = attend(proj_own, carry_own, 1, (o0, unit1))
    unit2 = tie(unit2, (o1,))
    unit3, unit6 = swap(unit2, 1), swap(unit2, 4)
    hidden, second, o_all, w_all = run(
        middle_kernel,
        [(rows, width), (rows, width), (rows, 512), (512, width)],
        (scal,),
        (o0, o1, o2, o3, inputs, output_weight, unit0, unit1, unit2, unit3, gain2, shift2),
        after=(spacer(unit2),),
        us=FRONT,
    )
    saved = (saved0, saved1, saved2, saved3)

    def feed_forward(j, unit, other, after=()):
        return run(
            lambda *refs: feed_forward_kernel(j, *refs),
            [(4, 256, 512), (rows, width), (rows, width)],
            (scal,),
            (second, cotangent, up_weight, down_weight, unit, other),
            (pltpu.VMEM((width, 256), F32), pltpu.VMEM((256, width), F32)),
            after=after,
        )

    part1, out1, ds1 = feed_forward(1, unit1, unit3)
    got1 = swap(part1, 1)
    part0, out0, ds0 = feed_forward(0, unit0, unit2, (ds1,))
    unit4, unit6 = tie(unit4, (ds0,)), tie(unit6, (ds0,))
    unit5, unit7 = swap(unit4, 1), swap(unit6, 1)
    def block0(k, part=None):
        return [(part0, k, part), (got1, k, part)]

    def block2(k, part=None):
        return [(part2, k, part), (got3, k, part)]

    u0, d0 = sums([[block0(2)], [block0(1, 1), block0(3, 1)]], scal)
    u0_y = swap_y(u0)
    d0_x = swap(d0, 2)
    part3, out3, ds3 = feed_forward(3, unit5, unit7, (u0,))
    got3 = swap(part3, 1)
    part2, out2, ds2 = feed_forward(2, unit4, unit6, (ds3,))
    u2, u0, d0, d2 = sums(
        [
            [block2(2)],
            [block0(0) + [(u0_y, None, None)]],
            [block0(k, 0) + [(d0_x, n, None)] for n, k in enumerate((1, 3))],
            [block2(1, 1), block2(3, 1)],
        ],
        scal, (ds2,),
    )
    u2_y = swap_y(u2)
    d0_z = swap(d0, 4)
    d2_x = swap(d2, 2)
    u0_z = swap(u0, 4)
    outputs, d_hidden, grads2, d_o, o_send, o_keep = run(
        middle_back_kernel,
        [inputs.shape, (rows, width), (8, width), (rows, 512), (4, 256, 128), (4, 256, 128)],
        (scal,),
        (hidden, cotangent, ds0, ds1, ds2, ds3, out0, out1, out2, out3, gain2, o_all, w_all),
        (pltpu.VMEM((512, width), F32),),
        after=(u2,),
    )

    def back(js, after=()):
        arrays = (proj_own, proj_oth0, proj_oth1, carry_oth, carry_own, d_o) + saved

        def kernel(scal, starts, own, oth0, oth1, c_oth, c_own, d_o, *rest):
            dproj, dstate = rest[4:]
            for k, j in enumerate(js):
                if j < 2:
                    proj = own.at[own_pair(scal, j)]
                    carry = c_own[j]
                else:
                    proj = (oth0, oth1)[j - 2]
                    carry = c_oth[own_pair(scal, j - 2)]
                dstate[len(js) - 1 - k] = attention_back(
                    scal[0], starts, proj, carry, rest[j], d_o,
                    slice(j * 128, (j + 1) * 128), dproj.at[k],
                )

        return run(
            kernel,
            [(len(js), rows, 512), (len(js), 136, 128)],
            tables,
            arrays,
            after=after,
        )

    def weight_grads(j, dstate, dproj, after=(), extra=()):
        proj = proj_own if j < 2 else (proj_oth0, proj_oth1)[j - 2]

        def kernel(scal, starts, proj, normed, o_send, o_keep, dstate, dproj, *rest):
            send, keep, final = rest[len(extra) : len(extra) + 3]
            here = proj.at[own_pair(scal, j)] if j < 2 else proj
            pair_grads(
                scal[0], starts, scal[1], here, dstate[0], normed, dproj.at[0],
                o_send[j], o_keep[j], send, keep, final,
            )
            if extra:
                rest[-1][...] = rest[0][...] + rest[1][...]

        return run(
            kernel,
            [(256, 640), (256, 640), (rows, 512)] + [a.shape for a in extra[:1]],
            tables,
            (proj, normed, o_send, o_keep, dstate, dproj) + extra,
            after=after,
            us=LATE,
        )

    dproj1, dstate1 = back((1,))
    dstate1 = to_first(dstate1)
    (d2,) = sums([[block2(3, 0) + [(d2_x, 1, None), (d0_z, 1, None)]]], scal, (dproj1,))
    d2_y = swap_y(d2)
    dproj3, dstate3 = back((3,), (d2,))
    dstate3 = to_first(dstate3)
    dproj0, dstate0 = back((0,), (dproj3,))
    dstate0 = to_first(dstate0)
    up_terms = lambda part: block2(0, part) + [(u2_y, None, part), (u0_z, None, part)]
    (u2,) = sums([[up_terms(1)]], scal, (dproj0,))
    u2_x = swap(u2, 2)
    send3, keep3, final3 = weight_grads(3, dstate1, dproj3, (u2,))
    got3q = swap(send3, 1)
    send1, keep1, final1 = weight_grads(1, dstate3, dproj1, (final3,))
    got1q = swap(send1, 1)
    (y_send1,) = sums([[[(keep3, None, None), (got3q, None, None)]]], scal, (final1,))
    y_got1 = swap_y(y_send1)
    dproj2, dstate2 = back((2,), (y_send1,))
    dstate2 = to_first(dstate2)
    send2, keep2, final2, own_sum1 = weight_grads(
        2, dstate0, dproj2, (dproj2,), (keep1, got1q)
    )
    got2 = swap(send2, 1)
    ff_send, ff_keep = choose(
        up_terms(0) + [(u2_x, None, None)],
        block2(1, 0) + [(d2_x, 0, None), (d0_z, 0, None), (d2_y, None, None)],
        scal, 7, (final2,),
    )
    ff_got = swap(ff_send, 8)
    send0, keep0, final0 = weight_grads(0, dstate2, dproj0, (ff_send,))
    got0 = swap(send0, 1)
    grad_inputs, grads1 = run(
        first_back_kernel,
        [inputs.shape, (8, 640)],
        (scal,),
        (inputs, gain1, d_hidden, final0, final1, final2, final3, qa0, qb0, qa1, qb1, grads2)
        + weights,
        (
            pltpu.VMEM((rows, 1024), F32),
            pltpu.VMEM((rows, width), F32),
            pltpu.VMEM((4, width, 256), F32),
            pltpu.SemaphoreType.DMA((4,)),
        ),
        after=(final0,),
        far=4,
        us=LATE,
    )
    y_send0, x_send1, own_sum, ff_shard = sums(
        [
            [[(keep2, None, None), (got2, None, None)], [(grads1, None, None)]],
            [[(own_sum1, None, None), (y_got1, None, None)]],
            [[(keep0, None, None), (got0, None, None)]],
            [[(ff_keep, None, None), (ff_got, None, None)]],
        ],
        scal, (grads1,), rows=True,
    )
    y_got0 = swap_y(y_send0)
    x_got1 = swap(x_send1, 2)
    step = spacer(y_send0)
    for at in bits[4:]:
        ff_send, ff_keep = halve([(ff_shard, None)], (), scal, at + 4, 0, (step,))
        ff_got = swap(ff_send, 1 << at)
        (ff_shard,) = sums(
            [[[(ff_keep, None, None), (ff_got, None, None)]]], scal, (spacer(ff_send),)
        )
        step = spacer(ff_shard)
    ff_steps = list(reversed(bits[3:]))
    ff_there = swap(ff_shard, 1 << ff_steps[0])
    terms = [(own_sum, None), (y_got0, None), (x_got1, None)]
    pending = list(bits[2:])
    gains = (grads1,)
    while pending or ff_there is not None:
        if ff_steps:
            to = ff_steps.pop(0)
            ff_shard = join(ff_shard, ff_there, scal, to + 4, 0, (step,))
            ff_there = swap(ff_shard, 1 << (ff_steps[0] if ff_steps else 2))
            step = spacer(ff_shard)
        elif ff_there is not None:
            (ff_pair,) = sums(
                [[[(ff_shard, None, None)], [(ff_there, None, None)]]], scal, (step,), rows=True
            )
            ff_there = None
            ff_x = swap(ff_pair, 2)
            step = spacer(ff_pair)
        if pending:
            at = pending.pop(0)
            send, keep = halve(terms, gains, scal, at + 4, 8, (step,))
            terms, gains = [(keep, None), (swap(send, 1 << at), None)], ()
            step = spacer(send)
    (shard,) = sums([[[(a, None, None) for a, _ in terms]]], scal, (step,))
    for n, at in enumerate(reversed(bits[3:])):
        there = swap(shard, 1 << at)
        step = spacer(shard)
        if n == 0:
            ff_x = tie(ff_x, (step,))
            ff_core, ff_x_core = swap(ff_pair, 1), swap(ff_x, 1)
            step = spacer(ff_x)
        shard = join(shard, there, scal, at + 4, after=(step,))
    quarters = [shard] + [swap(shard, 2 * k) for k in (1, 2, 3)]
    grad_up, grad_down = run(
        hidden_assemble_kernel,
        [up_weight.shape, down_weight.shape],
        (scal,),
        (ff_pair, ff_core, ff_x, ff_x_core),
        after=(spacer(shard),),
    )
    (quarters,) = sums([[[(a, None, None)] for a in quarters]], scal, (grad_up,))
    grad_query, grad_key, grad_value, grad_control, grad_output, gains = run(
        qkvc_assemble_kernel,
        [w.shape for w in weights] + [output_weight.shape, (8, width)],
        (scal,),
        (quarters, swap(quarters, 1)),
        after=(spacer(quarters),),
    )
    return (
        outputs, grad_inputs,
        grad_query, grad_key, grad_value, grad_control, grad_output, grad_up, grad_down,
        gains[0], gains[1], gains[2], gains[3],
    )


def solution(mesh):
    rows = P("head", "dp", None)
    cols = P(None, "head")
    tall = P("head", None)
    flat = P()
    return jax.shard_map(
        per_device,
        mesh=mesh,
        in_specs=(
            rows, P("dp", None), cols, cols, cols, cols, tall, cols, tall,
            flat, flat, flat, flat, rows,
        ),
        out_specs=(
            rows, rows, cols, cols, cols, cols, tall, cols, tall, flat, flat, flat, flat,
        ),
        check_vma=False,
    )
```

```python
import jax
import jax.numpy as jnp
from jax import lax
from jax.experimental import pallas as pl
from jax.experimental.pallas import tpu as pltpu
from jax.sharding import PartitionSpec as P

F32 = jnp.float32
HIGH = lax.Precision.HIGH
CHUNK = 256
EPS = 1e-05
GELU_C = 0.7978845608028654
GELU_K = 0.044715
VMEM_LIMIT = 16 * 2**20


def dot(left, right, dims):
    return lax.dot_general(
        left, right, (dims, ((), ())), precision=HIGH, preferred_element_type=F32
    )


def nn(left, right):
    return dot(left, right, ((1,), (0,)))


def nt(left, right):
    return dot(left, right, ((1,), (1,)))


def tn(left, right):
    return dot(left, right, ((0,), (0,)))


def whole():
    return pl.BlockSpec(memory_space=pltpu.VMEM)


def anywhere():
    return pl.BlockSpec(memory_space=pl.ANY)


def distant():
    return pl.BlockSpec(memory_space=pltpu.HBM)


def scalars():
    return pl.BlockSpec(memory_space=pltpu.SMEM)


FRONT, HEAVY, LATE, SUM = 50.0, 50.0, 50.0, 50.0


def cost(us):
    return pl.CostEstimate(flops=int(us * 1153e6), bytes_accessed=0, transcendentals=0)


def run(kernel, outs, scal, arrays, scratch=(), after=(), far=0, us=HEAVY, away=False):
    out_shape = [jax.ShapeDtypeStruct(shape, F32) for shape in outs]
    first, last = len(scal) + len(arrays), len(scal) + len(arrays) + len(after)
    return pl.pallas_call(
        lambda *refs: kernel(*refs[:first], *refs[last:]),
        out_shape=out_shape,
        in_specs=[scalars()] * len(scal)
        + [whole()] * (len(arrays) - far)
        + [distant()] * far
        + [anywhere()] * len(after),
        out_specs=[anywhere() if away else whole()] * len(outs),
        scratch_shapes=list(scratch),
        compiler_params=pltpu.CompilerParams(vmem_limit_bytes=VMEM_LIMIT),
        cost_estimate=cost(us),
    )(*scal, *arrays, *after)


def tie(array, after):
    count = 1 + len(after)
    return pl.pallas_call(
        lambda *refs: None,
        out_shape=jax.ShapeDtypeStruct(array.shape, F32),
        in_specs=[anywhere()] * count,
        out_specs=anywhere(),
        input_output_aliases={0: 0},
        compiler_params=pltpu.CompilerParams(vmem_limit_bytes=2**20),
        cost_estimate=pl.CostEstimate(flops=0, bytes_accessed=0, transcendentals=0),
    )(array, *after)


def spacer(*after):
    return pl.pallas_call(
        lambda *refs: None,
        out_shape=jax.ShapeDtypeStruct((8, 128), F32),
        in_specs=[anywhere()] * len(after),
        out_specs=anywhere(),
        compiler_params=pltpu.CompilerParams(vmem_limit_bytes=2**20),
        cost_estimate=cost(HEAVY),
    )(*after)


def lane_slice(ref, index, width):
    return ref[:, pl.ds(pl.multiple_of(index * width, width), width)]


def normalize(x):
    centre = x - jnp.mean(x, axis=-1, keepdims=True)
    spread = jnp.mean(centre * centre, axis=-1, keepdims=True)
    r = lax.rsqrt(spread + EPS)
    return centre * r, r


def norm_back(dy, nhat, r, gain):
    dyg = dy * gain
    first = jnp.mean(dyg, axis=-1, keepdims=True)
    second = jnp.mean(dyg * nhat, axis=-1, keepdims=True)
    return r * (dyg - first - nhat * second)


def doc_of(starts, position):
    total = jnp.zeros(jnp.shape(position), jnp.int32)
    for k in range(starts.shape[1]):
        total = total + (position >= starts[0, k]).astype(jnp.int32)
    return total


def column(first, count):
    return first + lax.broadcasted_iota(jnp.int32, (count, 1), 0)


def left_lanes():
    return lax.broadcasted_iota(jnp.int32, (1, 128), 1) < 64


def pack_state(mk, mv, z):
    left = left_lanes()
    return jnp.concatenate(
        [
            jnp.where(left, mk[0:64], mk[64:128]),
            jnp.where(left, mv[0:64], mv[64:128]),
            jnp.broadcast_to(z, (8, 128)),
        ],
        axis=0,
    )


def blocks_only(m):
    diagonal = (lax.broadcasted_iota(jnp.int32, (128, 128), 0) < 64) == (
        lax.broadcasted_iota(jnp.int32, (128, 128), 1) < 64
    )
    return jnp.where(diagonal, m, 0.0)


def unpack_state(state):
    mk = state[0:64]
    mv = state[64:128]
    return (
        blocks_only(jnp.concatenate([mk, mk], axis=0)),
        blocks_only(jnp.concatenate([mv, mv], axis=0)),
        state[128:129],
    )


def end_state(k2, v2, e2, starts, first):
    count = k2.shape[0]
    kept = (doc_of(starts, column(first, count)) == doc_of(starts, first + count - 1)).astype(F32)
    em = e2 * kept
    return pack_state(outer(k2, em), outer(em, v2), jnp.sum(em, axis=0, keepdims=True))


def cut_first_kernel(scal, wq, wk, wv, wc, piece, sems):
    rows = pl.ds(pl.multiple_of(scal[1] * 256, 256), 256)
    lanes = pl.ds(pl.multiple_of(scal[2] * 128, 128), 128)
    copies = [
        pltpu.make_async_copy(
            ref.at[rows, lanes], piece.at[:, w * 128 : (w + 1) * 128], sems.at[w]
        )
        for w, ref in enumerate((wq, wk, wv, wc))
    ]
    for copy in copies:
        copy.start()
    for copy in copies:
        copy.wait()


def cut_second_kernel(scal, wo, up, down, piece, sems):
    unit = pl.ds(pl.multiple_of(scal[3] * 256 + scal[2] * 128, 128), 128)
    thin = pl.ds(pl.multiple_of((scal[2] * 2 + scal[1]) * 64, 64), 64)
    copies = [
        pltpu.make_async_copy(
            up.at[b * 128 : (b + 1) * 128, unit], piece.at[0:128, b * 128 : (b + 1) * 128],
            sems.at[b],
        )
        for b in range(4)
    ]
    copies.append(pltpu.make_async_copy(down.at[unit, :], piece.at[128:256, :], sems.at[4]))
    copies.append(pltpu.make_async_copy(wo.at[thin, :], piece.at[256:320, :], sems.at[5]))
    for copy in copies:
        copy.start()
    for copy in copies:
        copy.wait()


def cut(kernel, shapes, scal, arrays, after=(), limit=2**20, near=False):
    first, last = 1 + len(arrays), 1 + len(arrays) + len(after)
    out_shape = [jax.ShapeDtypeStruct(shape, F32) for shape in shapes]
    return pl.pallas_call(
        lambda *refs: kernel(*refs[:first], *refs[last:]),
        out_shape=out_shape,
        in_specs=[scalars()] + [distant()] * len(arrays) + [anywhere()] * len(after),
        out_specs=[whole() if near else anywhere()] * len(shapes),
        scratch_shapes=[pltpu.SemaphoreType.DMA((6,))],
        compiler_params=pltpu.CompilerParams(vmem_limit_bytes=limit),
        cost_estimate=cost(FRONT),
    )(scal, *arrays, *after)


def own_kernel(scal, starts, x, gain, shift, wq, wk, wv, wc, normed, proj, states, held, sems):
    copies = [
        pltpu.make_async_copy(ref, held.at[w], sems.at[w])
        for w, ref in enumerate((wq, wk, wv, wc))
    ]
    for copy in copies:
        copy.start()
    nhat, _ = normalize(x[:, 0, :])
    n = nhat * gain[...] + shift[...]
    normed[...] = n
    for w, copy in enumerate(copies):
        copy.wait()
        full = nn(n, held[w])
        if w == 3:
            full = jnp.exp(full)
        for p in range(2):
            proj[p, :, w * 128 : (w + 1) * 128] = full[:, p * 128 : (p + 1) * 128]
    for p in range(2):
        states[p] = end_state(
            proj[p, :, 128:256], proj[p, :, 256:384], proj[p, :, 384:512], starts, scal[0]
        )


def other_kernel(scal, starts, normed, wa, wb, proj, states, before=None):
    core = scal[1]
    full = nn(lane_slice(normed, core, 256), wa[...]) + nn(
        lane_slice(normed, 1 - core, 256), wb[...]
    )
    proj[:, 0:384] = full[:, 0:384]
    proj[:, 384:512] = jnp.exp(full[:, 384:512])
    state = end_state(proj[:, 128:256], proj[:, 256:384], proj[:, 384:512], starts, scal[0])
    if before is None:
        states[...] = state
    else:
        states[0] = before[...]
        states[1] = state


def chunk_masks(starts, first, c):
    begin = first + c * CHUNK
    position = column(begin, CHUNK)
    docs = doc_of(starts, position)
    row = begin + lax.broadcasted_iota(jnp.int32, (1, CHUNK), 1)
    mask = (position >= row) & (docs == doc_of(starts, row))
    before = doc_of(starts, begin - 1)
    last = doc_of(starts, begin + CHUNK - 1)
    entering = (docs == before).astype(F32)
    leaving = (docs == last).astype(F32)
    passing = (before == last).astype(F32)
    return mask, entering, leaving, passing


BF16 = jnp.bfloat16


def raw(left, right, dims):
    return lax.dot_general(left, right, (dims, ((), ())), preferred_element_type=F32)


def rest_of(x):
    return x - x.astype(BF16).astype(F32)


def turn(x):
    return pltpu.roll(x, 64, 1)


def beside(a, b):
    return jnp.concatenate([a, b], axis=1).astype(BF16)


def rows_factor(x):
    left = left_lanes()
    low = turn(rest_of(x))
    return (
        beside(jnp.where(left, x, low), jnp.where(left, x, 0.0)),
        beside(jnp.where(left, low, x), jnp.where(left, 0.0, x)),
    )


def columns_factor(x):
    left = left_lanes()
    other = turn(x)
    low = rest_of(x)
    return (
        beside(jnp.where(left, x, other), low),
        beside(jnp.where(left, other, x), low),
    )


def affinity_of(rows, columns, mask):
    result = []
    for r, c in zip(rows, columns):
        value = jnp.where(mask, raw(r, c, ((1,), (1,))), 0.0)
        high = value.astype(BF16)
        result.append((high, (value - high.astype(F32)).astype(BF16)))
    return result


def narrow(x):
    left = left_lanes()
    low = rest_of(x)
    return (
        jnp.where(left, x, turn(low)).astype(BF16),
        jnp.where(left, turn(low), x).astype(BF16),
    )


def gather_heads(first, second):
    left = left_lanes()
    return jnp.where(left, first, second) + turn(jnp.where(left, second, first))


def spread(matrices, x):
    outs = []
    for (high, low), part in zip(matrices, x):
        outs.append(raw(high, part, ((1,), (0,))) + raw(low, part, ((1,), (0,))))
    return gather_heads(*outs)


def spread_back(matrices, x):
    outs = []
    for (high, low), part in zip(matrices, x):
        outs.append(raw(high, part, ((0,), (0,))) + raw(low, part, ((0,), (0,))))
    return gather_heads(*outs)


def fold(x):
    return x[:, 0:128] + x[:, 128:256]


def both_parts(x):
    return beside(x, rest_of(x))


def masked_sum(mask, x):
    return fold(raw(mask, both_parts(x), ((1,), (0,))))


def masked_sum_back(mask, x):
    return fold(raw(mask, both_parts(x), ((0,), (0,))))


def times_state(x, m):
    part = both_parts(m)
    return fold(raw(both_parts(x), jnp.concatenate([part, part], axis=0), ((1,), (0,))))


def times_state_back(x, m):
    low = rest_of(m)
    right = jnp.concatenate([beside(m, m), beside(low, low)], axis=0)
    return fold(raw(both_parts(x), right, ((1,), (1,))))


def outer(x, y):
    full = raw(both_parts(x), both_parts(y), ((0,), (0,)))
    return blocks_only(fold(full[0:128] + full[128:256]))


def slot_sums(x):
    left = left_lanes()
    return jnp.where(
        left,
        jnp.sum(jnp.where(left, x, 0.0), axis=1, keepdims=True),
        jnp.sum(jnp.where(left, 0.0, x), axis=1, keepdims=True),
    )


def next_state(k2, v2, e2, state, leaving, passing):
    mk, mv, z_in = state
    em = e2 * leaving
    return (
        outer(k2, em) + passing * mk,
        outer(em, v2) + passing * mv,
        jnp.sum(em, axis=0, keepdims=True) + passing * z_in,
    )


def attention(first, starts, proj, carry, o, lanes, saved):
    left = left_lanes()
    state = unpack_state(carry)
    chunks = proj.shape[0] // CHUNK
    for c in range(chunks):
        rows = slice(c * CHUNK, (c + 1) * CHUNK)
        q2, k2 = proj[rows, 0:128], proj[rows, 128:256]
        v2, e2 = proj[rows, 256:384], proj[rows, 384:512]
        mask, entering, leaving, passing = chunk_masks(starts, first, c)
        mk, mv, z_in = state
        z = masked_sum(mask.astype(F32).astype(BF16), e2) + entering * z_in
        affinity = affinity_of(rows_factor(q2), columns_factor(k2), mask)
        total = spread(affinity, narrow(e2)) + entering * times_state(q2, mk)
        s = total / z * 0.125
        top = jnp.where(
            left,
            jnp.max(jnp.where(left, s, -jnp.inf), axis=1, keepdims=True),
            jnp.max(jnp.where(left, -jnp.inf, s), axis=1, keepdims=True),
        )
        p = jnp.exp(s - top)
        p = p / slot_sums(p)
        r = p / z
        mixing = affinity_of(rows_factor(r), columns_factor(e2), mask)
        o[rows, lanes] = spread(mixing, narrow(v2)) + entering * times_state(r, mv)
        saved[rows, 0:128] = z
        saved[rows, 128:256] = s
        saved[rows, 256:384] = p
        if c + 1 < chunks:
            state = next_state(k2, v2, e2, state, leaving, passing)


def attention_back(first, starts, proj, carry, saved, d_o, lanes, dproj):
    chunks = proj.shape[0] // CHUNK
    states = [unpack_state(carry)]
    for c in range(chunks - 1):
        rows = slice(c * CHUNK, (c + 1) * CHUNK)
        _, _, leaving, passing = chunk_masks(starts, first, c)
        states.append(
            next_state(
                proj[rows, 128:256], proj[rows, 256:384], proj[rows, 384:512], states[c],
                leaving, passing,
            )
        )
    ahead = None
    for c in reversed(range(chunks)):
        rows = slice(c * CHUNK, (c + 1) * CHUNK)
        q2, k2 = proj[rows, 0:128], proj[rows, 128:256]
        v2, e2 = proj[rows, 256:384], proj[rows, 384:512]
        z, s, p = saved[rows, 0:128], saved[rows, 128:256], saved[rows, 256:384]
        do2 = d_o[rows, lanes]
        mask, entering, leaving, passing = chunk_masks(starts, first, c)
        mk, mv, _ = states[c]
        r = p / z
        do_in = entering * do2
        e_columns, e_narrow = columns_factor(e2), narrow(e2)
        mixing = affinity_of(rows_factor(r), e_columns, mask)
        d_mixing = affinity_of(rows_factor(do2), columns_factor(v2), mask)
        dv = spread_back(mixing, narrow(do2))
        dr = spread(d_mixing, e_narrow) + times_state_back(do_in, mv)
        de = spread_back(d_mixing, narrow(r))
        dp = dr / z
        dz = -dp * r
        ds = p * (dp - slot_sums(p * dp)) / z
        w = ds * 0.125
        dz = dz - ds * s
        w_in = entering * w
        affinity = affinity_of(rows_factor(q2), columns_factor(k2), mask)
        d_affinity = affinity_of(rows_factor(w), e_columns, mask)
        dq = spread(d_affinity, narrow(k2)) + times_state_back(w_in, mk)
        dk = spread_back(d_affinity, narrow(q2))
        de = de + spread_back(affinity, narrow(w))
        de = de + masked_sum_back(mask.astype(F32).astype(BF16), dz)
        if ahead is not None:
            dmk, dmv, dz_out = ahead
            em = e2 * leaving
            dv = dv + times_state(em, dmv)
            dk = dk + times_state_back(em, dmk)
            de = de + leaving * (times_state(k2, dmk) + times_state_back(v2, dmv) + dz_out)
        dproj[rows, 0:128] = dq
        dproj[rows, 128:256] = dk
        dproj[rows, 256:384] = dv
        dproj[rows, 384:512] = de
        now = (
            outer(q2, w_in),
            outer(r, do_in),
            jnp.sum(entering * dz, axis=0, keepdims=True),
        )
        if ahead is not None:
            now = tuple(a + passing * b for a, b in zip(now, ahead))
        ahead = now
    return pack_state(*ahead)


def own_pair(scal, j):
    return jnp.bitwise_xor(scal[2], j)


def attention_kernel(scal, starts, proj, carry, o, saved, j=None):
    here = proj if j is None else proj.at[own_pair(scal, j)]
    attention(scal[0], starts, here, carry, o, slice(0, 128), saved)


def middle_kernel(
    scal, o0, o1, o2, o3, x, wo, w0, w1, w2, w3, gain, shift, hidden, second, o_all, w_all,
):
    for j, ref in enumerate((o0, o1, o2, o3)):
        o_all[:, j * 128 : (j + 1) * 128] = ref[...]
    for j in range(2):
        which = pl.multiple_of(own_pair(scal, j) * 128, 128)
        w_all[j * 128 : (j + 1) * 128, :] = wo[pl.ds(which, 128), :]
    for k, ref in enumerate((w0, w1, w2, w3)):
        start = 256 + (k >> 1) * 128 + jnp.bitwise_xor(scal[1], k & 1) * 64
        w_all[pl.ds(pl.multiple_of(start, 64), 64), :] = ref[256:320, :]
    h = x[:, 0, :] + nn(o_all[...], w_all[...])
    hidden[...] = h
    nhat, _ = normalize(h)
    second[...] = nhat * gain[...] + shift[...]


def middle_back_kernel(
    scal, hidden, cot, ds0, ds1, ds2, ds3, u0, u1, u2, u3, gain, o_all, w_all,
    outputs, d_hidden, grads, d_o, send, keep, work,
):
    core = scal[1]
    outputs[:, 0, :] = hidden[...] + ((u0[...] + u1[...]) + (u2[...] + u3[...]))
    d_second = (ds0[...] + ds1[...]) + (ds2[...] + ds3[...])
    nhat, r = normalize(hidden[...])
    grads[0:1, :] = jnp.sum(d_second * nhat, axis=0, keepdims=True)
    grads[1:2, :] = jnp.sum(d_second, axis=0, keepdims=True)
    grads[2:8, :] = jnp.zeros((6, grads.shape[1]), F32)
    d = cot[:, 0, :] + norm_back(d_second, nhat, r, gain[...])
    d_hidden[...] = d
    d_o[...] = nt(d, w_all[...])
    work[...] = tn(o_all[...], d)
    for ref, which in ((send, 1 - core), (keep, core)):
        for j in range(4):
            rows = pl.ds(pl.multiple_of(j * 128 + which * 64, 64), 64)
            for b in range(4):
                ref[j, b * 64 : (b + 1) * 64, :] = work[rows, b * 128 : (b + 1) * 128]


def feed_forward_kernel(j, scal, second, cot, up, down, unit, other, packed, out, ds, up_far, down_far):
    where = pl.ds(pl.multiple_of(jnp.bitwise_xor(scal[3], j) * 256, 256), 256)
    for ref, half in ((unit, scal[2]), (other, 1 - scal[2])):
        place = pl.ds(pl.multiple_of(half * 128, 128), 128)
        for b in range(4):
            up_far[b * 128 : (b + 1) * 128, place] = ref[0:128, b * 128 : (b + 1) * 128]
        down_far[place, :] = ref[128:256, :]
    n_left, n_right = second[:, 0:256], second[:, 256:512]
    g = cot[:, 0, :]
    for half in range(2):
        if half == 0:
            up_left, up_right = up[0:256, where], up[256:512, where]
            down_block = down[where, :]
        else:
            up_left, up_right = up_far[0:256, :], up_far[256:512, :]
            down_block = down_far[...]
        u = nn(n_left, up_left) + nn(n_right, up_right)
        inner = GELU_C * (u + GELU_K * u * u * u)
        t = jnp.tanh(inner)
        act = 0.5 * u * (1.0 + t)
        slope = 0.5 * (1.0 + t) + 0.5 * u * (1.0 - t * t) * (
            GELU_C * (1.0 + 3.0 * GELU_K * u * u)
        )
        du = nt(g, down_block) * slope
        packed[2 * half, :, 0:256] = tn(n_left, du)
        packed[2 * half, :, 256:512] = tn(n_right, du)
        packed[2 * half + 1] = tn(act, g)
        out_part = nn(act, down_block)
        ds_left, ds_right = nt(du, up_left), nt(du, up_right)
        if half == 0:
            out[...] = out_part
            ds[:, 0:256] = ds_left
            ds[:, 256:512] = ds_right
        else:
            out[...] = out[...] + out_part
            ds[:, 0:256] = ds[:, 0:256] + ds_left
            ds[:, 256:512] = ds[:, 256:512] + ds_right


def pair_grads(first, starts, core, proj, dstate, normed, dproj, o_send, o_keep, send, keep, final):
    k2, v2, e2 = proj[:, 128:256], proj[:, 256:384], proj[:, 384:512]
    count = k2.shape[0]
    dmk, dmv, dz_out = unpack_state(dstate)
    leaving = (
        doc_of(starts, column(first, count)) == doc_of(starts, first + count - 1)
    ).astype(F32)
    em = e2 * leaving
    final[:, 0:128] = dproj[:, 0:128]
    final[:, 128:256] = dproj[:, 128:256] + times_state_back(em, dmk)
    final[:, 256:384] = dproj[:, 256:384] + times_state(em, dmv)
    de = dproj[:, 384:512] + leaving * (
        times_state(k2, dmk) + times_state_back(v2, dmv) + dz_out
    )
    final[:, 384:512] = e2 * de
    send[:, 0:512] = tn(lane_slice(normed, 1 - core, 256), final[...])
    keep[:, 0:512] = tn(lane_slice(normed, core, 256), final[...])
    send[:, 512:640] = o_send
    keep[:, 512:640] = o_keep


def first_back_kernel(
    scal, x, gain, d_hidden, f0, f31, f2, a0, b0, a1, b1, grads2, wq, wk, wv, wc,
    grad_x, grads, cat, acc, held, sems,
):
    core, pair = scal[1], scal[2]
    copies = [
        pltpu.make_async_copy(ref, held.at[w], sems.at[w])
        for w, ref in enumerate((wq, wk, wv, wc))
    ]
    for copy in copies:
        copy.start()
    for j, ref in enumerate((f0.at[0], f31.at[1])):
        which = jnp.bitwise_xor(pair, j)
        for w in range(4):
            start = pl.multiple_of(w * 256 + which * 128, 128)
            cat[:, pl.ds(start, 128)] = ref[:, w * 128 : (w + 1) * 128]
    total = None
    for w, copy in enumerate(copies):
        copy.wait()
        part = nt(cat[:, w * 256 : (w + 1) * 256], held[w])
        total = part if total is None else total + part
    acc[...] = total
    for which, refs in ((core, (a0, a1)), (1 - core, (b0, b1))):
        part = nt(f2[0], refs[0][...]) + nt(f31[0], refs[1][...])
        lanes = pl.ds(pl.multiple_of(which * 256, 256), 256)
        acc[:, lanes] = acc[:, lanes] + part
    d_normed = acc[...]
    nhat, r = normalize(x[:, 0, :])
    grads[...] = jnp.zeros(grads.shape, F32)
    grads[0:1, 0:512] = jnp.sum(d_normed * nhat, axis=0, keepdims=True)
    grads[1:2, 0:512] = jnp.sum(d_normed, axis=0, keepdims=True)
    grads[2:4, 0:512] = grads2[0:2, :]
    grad_x[:, 0, :] = d_hidden[...] + norm_back(d_normed, nhat, r, gain[...])


def table_of(groups):
    arrays, places = [], []
    for group in groups:
        places.append([])
        for array, lead, part in group:
            at = next((i for i, a in enumerate(arrays) if a is array), None)
            if at is None:
                at = len(arrays)
                arrays.append(array)
            places[-1].append((at, lead, part))
    return arrays, places


def total(scal, refs, place):
    value = None
    for at, lead, part in place:
        ref = refs[at] if lead is None else refs[at].at[lead]
        if part is None:
            term = ref[...]
        else:
            rows = ref.shape[0] // 2
            which = jnp.bitwise_xor(scal[2], part) * rows
            term = ref[pl.ds(pl.multiple_of(which, rows), rows), :]
        value = term if value is None else value + term
    return value


def shape_of(group):
    array, _, part = group[0]
    rows, cols = array.shape[-2:]
    return (rows if part is None else rows // 2, cols)


def sums(outs, scal, after=(), rows=False):
    arrays, places = table_of([group for out in outs for group in out])
    shapes = []
    for out in outs:
        h, w = shape_of(out[0])
        if rows:
            shapes.append((sum(shape_of(g)[0] for g in out), w))
        else:
            shapes.append((h, w) if len(out) == 1 else (len(out), h, w))

    def kernel(scal, *refs):
        at = 0
        for n, out in enumerate(outs):
            target = refs[len(arrays) + n]
            row = 0
            for k in range(len(out)):
                value = total(scal, refs, places[at])
                at += 1
                if rows:
                    target[row : row + value.shape[0], :] = value
                    row += value.shape[0]
                elif len(out) == 1:
                    target[...] = value
                else:
                    target[k] = value

    return run(kernel, shapes, (scal,), arrays, after=after, us=SUM)


def choose(first, second, scal, at, after=()):
    arrays, places = table_of([first, second])

    def kernel(scal, *refs):
        values = [total(scal, refs, place) for place in places]
        for side in range(2):

            @pl.when(scal[at] == side)
            def _():
                refs[-2][...] = values[1 - side]
                refs[-1][...] = values[side]

    return run(kernel, [shape_of(first)] * 2, (scal,), arrays, after=after, us=SUM)


def halve(terms, scal, at, after=()):
    rows, cols = terms[0][0].shape[-2:]
    rows //= 2
    leads = [lead for _, lead in terms]

    def kernel(scal, *refs):
        for out, which in ((refs[-2], 1 - scal[at]), (refs[-1], scal[at])):
            block = pl.ds(pl.multiple_of(which * rows, rows), rows)
            value = None
            for ref, lead in zip(refs, leads):
                term = ref[block, :] if lead is None else ref[lead, block, :]
                value = term if value is None else value + term
            out[...] = value

    return run(
        kernel, [(rows, cols)] * 2, (scal,), [a for a, _ in terms], after=after, us=SUM
    )


def join(here, there, scal, at, tail=8, after=()):
    rows, cols = here.shape
    rows -= tail

    def kernel(scal, here, there, out):
        for ref, which in ((here, scal[at]), (there, 1 - scal[at])):
            block = pl.ds(pl.multiple_of(which * rows, rows), rows)
            out[block, :] = ref[0:rows, :]
        if tail:
            out[2 * rows :, :] = here[rows:, :] + there[rows:, :]

    return run(kernel, [(2 * rows + tail, cols)], (scal,), (here, there), after=after, us=SUM)[0]


def hidden_assemble_kernel(scal, p0, p1, p2, p3, up, down, token, sem):
    copies = []
    for k, ref in enumerate((p0, p1, p2, p3)):
        half = jnp.bitwise_xor(scal[2], k >> 1) * 128
        for far in range(2):
            block = jnp.bitwise_xor(scal[3], (k & 1) + 2 - 2 * far)
            lanes = pl.ds(pl.multiple_of(block * 256, 256), 256)
            first = far * 256
            upper = pl.ds(pl.multiple_of(half, 128), 128)
            lower = pl.ds(pl.multiple_of(half + 256, 128), 128)
            where = pl.ds(pl.multiple_of(block * 256 + half, 128), 128)
            rows = ref.at[first : first + 128, :]
            copies += [
                (rows.at[:, 0:256], up.at[upper, lanes]),
                (rows.at[:, 256:512], up.at[lower, lanes]),
                (ref.at[first + 128 : first + 256, :], down.at[where, :]),
            ]
    copies = [
        pltpu.make_async_copy(source, target, sem.at[n])
        for n, (source, target) in enumerate(copies)
    ]
    for copy in copies:
        copy.start()
    for copy in copies:
        copy.wait()


def qkvc_assemble_kernel(scal, *refs):
    (here, there), (wq, wk, wv, wc, wo), gains = refs[:2], refs[2:7], refs[7:]
    pieces = [ref.at[k] for ref in (here, there) for k in range(4)]
    size = here.shape[1] - 8
    tails = None
    for k, ref in enumerate(pieces):
        half = jnp.bitwise_xor(scal[1], k >> 2)
        which = jnp.bitwise_xor(scal[2], k & 1)
        first = jnp.bitwise_xor(scal[6], (k >> 1) & 1) * size
        rows = pl.ds(pl.multiple_of(half * 256 + first, size), size)
        lanes = pl.ds(pl.multiple_of(which * 128, 128), 128)
        for w, out in enumerate((wq, wk, wv, wc)):
            out[rows, lanes] = ref[0:size, w * 128 : (w + 1) * 128]
        for b in range(size // 64):
            start = pl.multiple_of(first // 64 * 128 + b * 128, 128)
            out_rows = pl.ds(pl.multiple_of(which * 128 + half * 64, 64), 64)
            wo[out_rows, pl.ds(start, 128)] = ref[b * 64 : (b + 1) * 64, 512:640]
        tail = ref[size : size + 8, 0:512]
        tails = tail if tails is None else tails + tail
    for k, ref in enumerate(gains):
        ref[...] = tails[k : k + 1, :]


def per_device(
    inputs, doc_starts, query_weight, key_weight, value_weight, control_weight, output_weight,
    up_weight, down_weight, first_gain, first_shift, second_gain, second_shift, cotangent,
):
    rows, _, width = inputs.shape
    devices = lax.axis_size("dp")
    place = lax.axis_index("dp").astype(jnp.int32)
    y = lax.axis_index("head").astype(jnp.int32)
    core = place & 1
    pair = (place >> 1) & 1
    one = lambda *v: jnp.stack([jnp.asarray(a, jnp.int32) for a in v])
    depth = (place >> 2) & 1
    bits = [at for at in range(31) if (1 << at) < devices]
    scal = one(y * rows, core, pair, depth * 2 + core, *((place >> at) & 1 for at in bits))
    gain1, shift1 = first_gain.reshape(1, width), first_shift.reshape(1, width)
    gain2, shift2 = second_gain.reshape(1, width), second_shift.reshape(1, width)
    weights = (query_weight, key_weight, value_weight, control_weight)

    def swap_y(a):
        return lax.ppermute(a, "head", [(0, 1), (1, 0)])

    def swap(a, bits):
        return lax.ppermute(a, "dp", [(i, i ^ bits) for i in range(devices)])

    to_second = lambda a: lax.ppermute(a, "head", [(0, 1)])
    to_first = lambda a: lax.ppermute(a, "head", [(1, 0)])

    tables = (scal, doc_starts)
    (piece,) = cut(cut_first_kernel, [(256, 512)], scal, weights, limit=60 * 2**20, near=True)
    qa0 = swap_y(piece)
    normed, proj_own, states_own = run(
        own_kernel,
        [(rows, width), (2, rows, 512), (2, 136, 128)],
        tables,
        (inputs, gain1, shift1) + weights,
        (pltpu.VMEM((4, width, 256), F32), pltpu.SemaphoreType.DMA((4,))),
        after=(piece,),
        far=4,
        us=FRONT,
    )
    carry_oth = to_second(states_own)
    qa0 = tie(qa0, (carry_oth,))
    qb0 = swap(qa0, 1)
    qa1 = swap(qa0, 2)
    (unit,) = cut(
        cut_second_kernel, [(320, 512)], scal, (output_weight, up_weight, down_weight), (qa0,)
    )
    unit0 = swap_y(unit)

    proj_oth0, state0 = run(
        other_kernel, [(rows, 512), (136, 128)], tables, (normed, qa0, qb0),
        after=(unit,), us=FRONT,
    )

    def attend(proj, carry, j, after=()):
        def kernel(scal, starts, proj, carry, o, saved):
            state = carry[own_pair(scal, j - 2)] if j >= 2 else carry[j]
            attention_kernel(scal, starts, proj, state, o, saved, j if j < 2 else None)

        return run(
            kernel, [(rows, 128), (rows, 384)], tables, (proj, carry), after=after, us=FRONT
        )

    qa1 = tie(qa1, (proj_oth0,))
    qb1 = swap(qa1, 1)
    o2, saved2 = attend(proj_oth0, carry_oth, 2, (qa1,))
    unit0 = tie(unit0, (o2,))
    unit1, unit2, unit4 = swap(unit0, 1), swap(unit0, 2), swap(unit0, 4)
    proj_oth1, states_oth = run(
        lambda scal, starts, normed, wa, wb, before, proj, states: other_kernel(
            scal, starts, normed, wa, wb, proj, states, before
        ),
        [(rows, 512), (2, 136, 128)], tables, (normed, qa1, qb1, state0),
        after=(unit0,), us=FRONT,
    )
    carry_own = to_second(states_oth)
    o3, saved3 = attend(proj_oth1, carry_oth, 3, (unit0,))
    o0, saved0 = attend(proj_own, carry_own, 0, (o3,))
    o1, saved1 = attend(proj_own, carry_own, 1, (o0, unit1))
    unit2 = tie(unit2, (o1,))
    unit3, unit6 = swap(unit2, 1), swap(unit2, 4)
    hidden, second, o_all, w_all = run(
        middle_kernel,
        [(rows, width), (rows, width), (rows, 512), (512, width)],
        (scal,),
        (o0, o1, o2, o3, inputs, output_weight, unit0, unit1, unit2, unit3, gain2, shift2),
        after=(spacer(unit2),),
        us=FRONT,
    )
    saved = (saved0, saved1, saved2, saved3)

    def feed_forward(j, unit, other, after=()):
        return run(
            lambda *refs: feed_forward_kernel(j, *refs),
            [(4, 256, 512), (rows, width), (rows, width)],
            (scal,),
            (second, cotangent, up_weight, down_weight, unit, other),
            (pltpu.VMEM((width, 256), F32), pltpu.VMEM((256, width), F32)),
            after=after,
        )

    part1, out1, ds1 = feed_forward(1, unit1, unit3)
    got1 = swap(part1, 1)
    part0, out0, ds0 = feed_forward(0, unit0, unit2, (ds1,))
    unit4, unit6 = tie(unit4, (ds0,)), tie(unit6, (ds0,))
    unit5, unit7 = swap(unit4, 1), swap(unit6, 1)
    def block0(k, part=None):
        return [(part0, k, part), (got1, k, part)]

    def block2(k, part=None):
        return [(part2, k, part), (got3, k, part)]

    u0, d0 = sums([[block0(2)], [block0(1, 1), block0(3, 1)]], scal)
    u0_y = swap_y(u0)
    d0_x = swap(d0, 2)
    part3, out3, ds3 = feed_forward(3, unit5, unit7, (u0,))
    got3 = swap(part3, 1)
    part2, out2, ds2 = feed_forward(2, unit4, unit6, (ds3,))
    u2, u0, d0, d2 = sums(
        [
            [block2(2)],
            [block0(0) + [(u0_y, None, None)]],
            [block0(k, 0) + [(d0_x, n, None)] for n, k in enumerate((1, 3))],
            [block2(1, 1), block2(3, 1)],
        ],
        scal, (ds2,),
    )
    u2_y = swap_y(u2)
    d0_z = swap(d0, 4)
    d2_x = swap(d2, 2)
    u0_z = swap(u0, 4)
    outputs, d_hidden, grads2, d_o, o_send, o_keep = run(
        middle_back_kernel,
        [inputs.shape, (rows, width), (8, width), (rows, 512), (4, 256, 128), (4, 256, 128)],
        (scal,),
        (hidden, cotangent, ds0, ds1, ds2, ds3, out0, out1, out2, out3, gain2, o_all, w_all),
        (pltpu.VMEM((512, width), F32),),
        after=(u2,),
    )

    def back(js, after=()):
        arrays = (proj_own, proj_oth0, proj_oth1, carry_oth, carry_own, d_o) + saved

        def kernel(scal, starts, own, oth0, oth1, c_oth, c_own, d_o, *rest):
            dproj, dstate = rest[4:]
            for k, j in enumerate(js):
                if j < 2:
                    proj = own.at[own_pair(scal, j)]
                    carry = c_own[j]
                else:
                    proj = (oth0, oth1)[j - 2]
                    carry = c_oth[own_pair(scal, j - 2)]
                dstate[len(js) - 1 - k] = attention_back(
                    scal[0], starts, proj, carry, rest[j], d_o,
                    slice(j * 128, (j + 1) * 128), dproj.at[k],
                )

        return run(
            kernel,
            [(len(js), rows, 512), (len(js), 136, 128)],
            tables,
            arrays,
            after=after,
        )

    def weight_grads(js, dstates, dprojs, after=(), extra=()):
        n = len(js)
        arrays = (proj_own, proj_oth0, proj_oth1, normed, o_send, o_keep)
        arrays += tuple(a for a, _ in dstates) + tuple(a for a, _ in dprojs)
        arrays += tuple(a for a, _ in extra)

        def kernel(scal, starts, own, oth0, oth1, normed, o_send, o_keep, *rest):
            states, grads, rest = rest[:n], rest[n : 2 * n], rest[2 * n :]
            send, keep, final = rest[len(extra) : len(extra) + 3]
            for k, j in enumerate(js):
                here = own.at[own_pair(scal, j)] if j < 2 else (oth0, oth1)[j - 2]
                pair_grads(
                    scal[0], starts, scal[1], here, states[k][dstates[k][1]], normed,
                    grads[k].at[dprojs[k][1]], o_send[j], o_keep[j],
                    send.at[k], keep.at[k], final.at[k],
                )
            if extra:
                value = None
                for ref, (_, lead) in zip(rest, extra):
                    term = ref[lead]
                    value = term if value is None else value + term
                rest[-1][...] = value

        outs = [(n, 256, 640), (n, 256, 640), (n, rows, 512)]
        return run(
            kernel, outs + [(256, 640)] * bool(extra), tables, arrays, after=after, us=LATE
        )

    dproj13, dstate13 = back((1, 3))
    dstate13 = to_first(dstate13)
    dproj0, dstate0 = back((0,), (dproj13,))
    dstate0 = to_first(dstate0)
    up_terms = lambda part: block2(0, part) + [(u2_y, None, part), (u0_z, None, part)]
    d2, u2 = sums(
        [
            [block2(3, 0) + [(d2_x, 1, None), (d0_z, 1, None)]],
            [up_terms(1)],
        ],
        scal, (dproj0,),
    )
    d2_y = swap_y(d2)
    u2_x = swap(u2, 2)
    send31, keep31, final31 = weight_grads(
        (3, 1), ((dstate13, 1), (dstate13, 0)), ((dproj13, 1), (dproj13, 0)), (d2,)
    )
    got31 = swap(send31, 1)
    ff_send, ff_keep = choose(
        up_terms(0) + [(u2_x, None, None)],
        block2(1, 0) + [(d2_x, 0, None), (d0_z, 0, None), (d2_y, None, None)],
        scal, 7, (final31,),
    )
    ff_got = swap(ff_send, 8)
    (y_send1,) = sums([[[(keep31, 0, None), (got31, 0, None)]]], scal, (ff_send,))
    y_got1 = swap_y(y_send1)
    dproj2, dstate2 = back((2,), (y_send1,))
    dstate2 = to_first(dstate2)
    send2, keep2, final2, own_sum1 = weight_grads(
        (2,), ((dstate0, 0),), ((dproj2, 0),), (dproj2,), ((keep31, 1), (got31, 1))
    )
    got2 = swap(send2, 1)
    (ff_shard,) = sums(
        [[[(ff_keep, None, None), (ff_got, None, None)]]], scal, (final2,)
    )
    step = ff_shard
    for at in bits[4:]:
        ff_send, ff_keep = halve([(ff_shard, None)], scal, at + 4, (step,))
        ff_got = swap(ff_send, 1 << at)
        (ff_shard,) = sums(
            [[[(ff_keep, None, None), (ff_got, None, None)]]], scal, (spacer(ff_send),)
        )
        step = ff_shard
    ff_steps = list(reversed(bits[3:]))
    ff_there = swap(ff_shard, 1 << ff_steps[0])
    send0, keep0, final0 = weight_grads((0,), ((dstate2, 0),), ((dproj0, 0),), (ff_shard,))
    got0 = swap(send0, 1)
    y_send0, x_send1 = sums(
        [
            [[(keep2, 0, None), (got2, 0, None)]],
            [[(own_sum1, None, None), (y_got1, None, None)]],
        ],
        scal, (final0,),
    )
    y_got0 = swap_y(y_send0)
    x_got1 = swap(x_send1, 2)
    step = spacer(y_send0)
    terms = [(keep0, 0), (got0, 0), (y_got0, None), (x_got1, None)]
    pending = list(bits[2:])
    while pending or ff_there is not None:
        if ff_steps:
            to = ff_steps.pop(0)
            ff_shard = join(ff_shard, ff_there, scal, to + 4, 0, (step,))
            ff_there = swap(ff_shard, 1 << (ff_steps[0] if ff_steps else 2))
            step = spacer(ff_shard)
        elif ff_there is not None:
            ff_pair, gains = sums(
                [[[(ff_shard, None, None)], [(ff_there, None, None)]], [[(grads1, None, None)]]],
                scal, (step,), rows=True,
            )
            gains_got = swap_y(gains)
            ff_there = None
            ff_x = swap(ff_pair, 2)
            step = spacer(ff_pair)
        if pending:
            at = pending.pop(0)
            if at == 2:
                send, keep = halve(terms, scal, at + 4, (step,))
                there = swap(send, 1 << at)
                step = spacer(send)
                grad_inputs, grads1 = run(
                    first_back_kernel,
                    [inputs.shape, (8, 640)],
                    (scal,),
                    (inputs, gain1, d_hidden, final0, final31, final2, qa0, qb0, qa1, qb1, grads2)
                    + weights,
                    (
                        pltpu.VMEM((rows, 1024), F32),
                        pltpu.VMEM((rows, width), F32),
                        pltpu.VMEM((4, width, 256), F32),
                        pltpu.SemaphoreType.DMA((4,)),
                    ),
                    after=(step,),
                    far=4,
                    us=LATE,
                )
                step = spacer(grads1)
            else:
                send, keep = halve(terms, scal, at + 4, (step,))
                there = swap(send, 1 << at)
                step = spacer(send)
            terms = [(keep, None), (there, None)]
    (shard,) = sums(
        [
            [
                [(a, None, None) for a, _ in terms],
                [(grads1, None, None), (gains_got, None, None)],
            ]
        ],
        scal, (step,), rows=True,
    )
    for n, at in enumerate(reversed(bits[3:])):
        there = swap(shard, 1 << at)
        step = spacer(shard)
        if n == 0:
            ff_x = tie(ff_x, (step,))
            ff_core, ff_x_core = swap(ff_pair, 1), swap(ff_x, 1)
            step = spacer(ff_x)
        shard = join(shard, there, scal, at + 4, after=(step,))
    quarters = [shard] + [swap(shard, 2 * k) for k in (1, 2, 3)]
    grad_up, grad_down, token = run(
        hidden_assemble_kernel,
        [up_weight.shape, down_weight.shape, (8, 128)],
        (scal,),
        (ff_pair, ff_core, ff_x, ff_x_core),
        (pltpu.SemaphoreType.DMA((24,)),),
        after=(spacer(shard),),
        away=True,
    )
    (quarters,) = sums([[[(a, None, None)] for a in quarters]], scal, (token,))
    *weight_grad, gain_a, gain_b, gain_c, gain_d = run(
        qkvc_assemble_kernel,
        [w.shape for w in weights] + [output_weight.shape] + [(1, width)] * 4,
        (scal,),
        (quarters, swap(quarters, 1)),
        after=(spacer(quarters),),
    )
    return (
        outputs, grad_inputs,
        *weight_grad, grad_up, grad_down,
        gain_a[0], gain_b[0], gain_c[0], gain_d[0],
    )


def solution(mesh):
    rows = P("head", "dp", None)
    cols = P(None, "head")
    tall = P("head", None)
    flat = P()
    return jax.shard_map(
        per_device,
        mesh=mesh,
        in_specs=(
            rows, P("dp", None), cols, cols, cols, cols, tall, cols, tall,
            flat, flat, flat, flat, rows,
        ),
        out_specs=(
            rows, rows, cols, cols, cols, cols, tall, cols, tall, flat, flat, flat, flat,
        ),
        check_vma=False,
    )
```

```python
import jax
import jax.numpy as jnp
from jax import lax
from jax.experimental import pallas as pl
from jax.experimental.pallas import tpu as pltpu
from jax.sharding import PartitionSpec as P

F32 = jnp.float32
HIGH = lax.Precision.HIGH
CHUNK = 256
EPS = 1e-05
GELU_C = 0.7978845608028654
GELU_K = 0.044715
VMEM_LIMIT = 16 * 2**20


def dot(left, right, dims):
    return lax.dot_general(
        left, right, (dims, ((), ())), precision=HIGH, preferred_element_type=F32
    )


def nn(left, right):
    return dot(left, right, ((1,), (0,)))


def nt(left, right):
    return dot(left, right, ((1,), (1,)))


def tn(left, right):
    return dot(left, right, ((0,), (0,)))


def whole():
    return pl.BlockSpec(memory_space=pltpu.VMEM)


def anywhere():
    return pl.BlockSpec(memory_space=pl.ANY)


def distant():
    return pl.BlockSpec(memory_space=pltpu.HBM)


def scalars():
    return pl.BlockSpec(memory_space=pltpu.SMEM)


FRONT, HEAVY, LATE, SUM = 20.0, 20.0, 20.0, 20.0


def cost(us):
    return pl.CostEstimate(flops=int(us * 1153e6), bytes_accessed=0, transcendentals=0)


def run(kernel, outs, scal, arrays, scratch=(), after=(), far=0, us=HEAVY, away=False):
    out_shape = [jax.ShapeDtypeStruct(shape, F32) for shape in outs]
    first, last = len(scal) + len(arrays), len(scal) + len(arrays) + len(after)
    return pl.pallas_call(
        lambda *refs: kernel(*refs[:first], *refs[last:]),
        out_shape=out_shape,
        in_specs=[scalars()] * len(scal)
        + [whole()] * (len(arrays) - far)
        + [distant()] * far
        + [anywhere()] * len(after),
        out_specs=[anywhere() if away else whole()] * len(outs),
        scratch_shapes=list(scratch),
        compiler_params=pltpu.CompilerParams(vmem_limit_bytes=VMEM_LIMIT),
        cost_estimate=cost(us),
    )(*scal, *arrays, *after)


def tie(array, after):
    count = 1 + len(after)
    return pl.pallas_call(
        lambda *refs: None,
        out_shape=jax.ShapeDtypeStruct(array.shape, F32),
        in_specs=[anywhere()] * count,
        out_specs=anywhere(),
        input_output_aliases={0: 0},
        compiler_params=pltpu.CompilerParams(vmem_limit_bytes=2**20),
        cost_estimate=pl.CostEstimate(flops=0, bytes_accessed=0, transcendentals=0),
    )(array, *after)


def spacer(*after):
    return pl.pallas_call(
        lambda *refs: None,
        out_shape=jax.ShapeDtypeStruct((8, 128), F32),
        in_specs=[anywhere()] * len(after),
        out_specs=anywhere(),
        compiler_params=pltpu.CompilerParams(vmem_limit_bytes=2**20),
        cost_estimate=cost(HEAVY),
    )(*after)


def lane_slice(ref, index, width):
    return ref[:, pl.ds(pl.multiple_of(index * width, width), width)]


def normalize(x):
    centre = x - jnp.mean(x, axis=-1, keepdims=True)
    spread = jnp.mean(centre * centre, axis=-1, keepdims=True)
    r = lax.rsqrt(spread + EPS)
    return centre * r, r


def norm_back(dy, nhat, r, gain):
    dyg = dy * gain
    first = jnp.mean(dyg, axis=-1, keepdims=True)
    second = jnp.mean(dyg * nhat, axis=-1, keepdims=True)
    return r * (dyg - first - nhat * second)


def doc_of(starts, position):
    total = jnp.zeros(jnp.shape(position), jnp.int32)
    for k in range(starts.shape[1]):
        total = total + (position >= starts[0, k]).astype(jnp.int32)
    return total


def column(first, count):
    return first + lax.broadcasted_iota(jnp.int32, (count, 1), 0)


def left_lanes():
    return lax.broadcasted_iota(jnp.int32, (1, 128), 1) < 64


def pack_state(mk, mv, z):
    left = left_lanes()
    return jnp.concatenate(
        [
            jnp.where(left, mk[0:64], mk[64:128]),
            jnp.where(left, mv[0:64], mv[64:128]),
            jnp.broadcast_to(z, (8, 128)),
        ],
        axis=0,
    )


def blocks_only(m):
    diagonal = (lax.broadcasted_iota(jnp.int32, (128, 128), 0) < 64) == (
        lax.broadcasted_iota(jnp.int32, (128, 128), 1) < 64
    )
    return jnp.where(diagonal, m, 0.0)


def unpack_state(state):
    mk = state[0:64]
    mv = state[64:128]
    return (
        blocks_only(jnp.concatenate([mk, mk], axis=0)),
        blocks_only(jnp.concatenate([mv, mv], axis=0)),
        state[128:129],
    )


def end_state(k2, v2, e2, starts, first):
    count = k2.shape[0]
    kept = (doc_of(starts, column(first, count)) == doc_of(starts, first + count - 1)).astype(F32)
    em = e2 * kept
    return pack_state(outer(k2, em), outer(em, v2), jnp.sum(em, axis=0, keepdims=True))


def cut_first_kernel(scal, wq, wk, wv, wc, piece, sems):
    rows = pl.ds(pl.multiple_of(scal[1] * 256, 256), 256)
    lanes = pl.ds(pl.multiple_of(scal[2] * 128, 128), 128)
    copies = [
        pltpu.make_async_copy(
            ref.at[rows, lanes], piece.at[:, w * 128 : (w + 1) * 128], sems.at[w]
        )
        for w, ref in enumerate((wq, wk, wv, wc))
    ]
    for copy in copies:
        copy.start()
    for copy in copies:
        copy.wait()


def cut_second_kernel(scal, wo, up, down, piece, sems):
    unit = pl.ds(pl.multiple_of(scal[3] * 256 + scal[2] * 128, 128), 128)
    thin = pl.ds(pl.multiple_of((scal[2] * 2 + scal[1]) * 64, 64), 64)
    copies = [
        pltpu.make_async_copy(
            up.at[b * 128 : (b + 1) * 128, unit], piece.at[0:128, b * 128 : (b + 1) * 128],
            sems.at[b],
        )
        for b in range(4)
    ]
    copies.append(pltpu.make_async_copy(down.at[unit, :], piece.at[128:256, :], sems.at[4]))
    copies.append(pltpu.make_async_copy(wo.at[thin, :], piece.at[256:320, :], sems.at[5]))
    for copy in copies:
        copy.start()
    for copy in copies:
        copy.wait()


def cut(kernel, shapes, scal, arrays, after=(), limit=2**20, near=False):
    first, last = 1 + len(arrays), 1 + len(arrays) + len(after)
    out_shape = [jax.ShapeDtypeStruct(shape, F32) for shape in shapes]
    return pl.pallas_call(
        lambda *refs: kernel(*refs[:first], *refs[last:]),
        out_shape=out_shape,
        in_specs=[scalars()] + [distant()] * len(arrays) + [anywhere()] * len(after),
        out_specs=[whole() if near else anywhere()] * len(shapes),
        scratch_shapes=[pltpu.SemaphoreType.DMA((6,))],
        compiler_params=pltpu.CompilerParams(vmem_limit_bytes=limit),
        cost_estimate=cost(FRONT),
    )(scal, *arrays, *after)


def own_kernel(scal, starts, x, gain, shift, wq, wk, wv, wc, normed, proj, states, held, sems):
    copies = [
        pltpu.make_async_copy(ref, held.at[w], sems.at[w])
        for w, ref in enumerate((wq, wk, wv, wc))
    ]
    for copy in copies:
        copy.start()
    nhat, _ = normalize(x[:, 0, :])
    n = nhat * gain[...] + shift[...]
    normed[...] = n
    for w, copy in enumerate(copies):
        copy.wait()
        full = nn(n, held[w])
        if w == 3:
            full = jnp.exp(full)
        for p in range(2):
            proj[p, :, w * 128 : (w + 1) * 128] = full[:, p * 128 : (p + 1) * 128]
    for p in range(2):
        states[p] = end_state(
            proj[p, :, 128:256], proj[p, :, 256:384], proj[p, :, 384:512], starts, scal[0]
        )


def other_kernel(scal, starts, normed, wa, wb, proj, states, before=None):
    core = scal[1]
    full = nn(lane_slice(normed, core, 256), wa[...]) + nn(
        lane_slice(normed, 1 - core, 256), wb[...]
    )
    proj[:, 0:384] = full[:, 0:384]
    proj[:, 384:512] = jnp.exp(full[:, 384:512])
    state = end_state(proj[:, 128:256], proj[:, 256:384], proj[:, 384:512], starts, scal[0])
    if before is None:
        states[...] = state
    else:
        states[0] = before[...]
        states[1] = state


def chunk_masks(starts, first, c):
    begin = first + c * CHUNK
    position = column(begin, CHUNK)
    docs = doc_of(starts, position)
    row = begin + lax.broadcasted_iota(jnp.int32, (1, CHUNK), 1)
    mask = (position >= row) & (docs == doc_of(starts, row))
    before = doc_of(starts, begin - 1)
    last = doc_of(starts, begin + CHUNK - 1)
    entering = (docs == before).astype(F32)
    leaving = (docs == last).astype(F32)
    passing = (before == last).astype(F32)
    return mask, entering, leaving, passing


BF16 = jnp.bfloat16


def raw(left, right, dims):
    return lax.dot_general(left, right, (dims, ((), ())), preferred_element_type=F32)


def rest_of(x):
    return x - x.astype(BF16).astype(F32)


def turn(x):
    return pltpu.roll(x, 64, 1)


def beside(a, b):
    return jnp.concatenate([a, b], axis=1).astype(BF16)


def rows_factor(x):
    left = left_lanes()
    low = turn(rest_of(x))
    return (
        beside(jnp.where(left, x, low), jnp.where(left, x, 0.0)),
        beside(jnp.where(left, low, x), jnp.where(left, 0.0, x)),
    )


def columns_factor(x):
    left = left_lanes()
    other = turn(x)
    low = rest_of(x)
    return (
        beside(jnp.where(left, x, other), low),
        beside(jnp.where(left, other, x), low),
    )


def affinity_of(rows, columns, mask):
    result = []
    for r, c in zip(rows, columns):
        value = jnp.where(mask, raw(r, c, ((1,), (1,))), 0.0)
        high = value.astype(BF16)
        result.append((high, (value - high.astype(F32)).astype(BF16)))
    return result


def narrow(x):
    left = left_lanes()
    low = rest_of(x)
    return (
        jnp.where(left, x, turn(low)).astype(BF16),
        jnp.where(left, turn(low), x).astype(BF16),
    )


def gather_heads(first, second):
    left = left_lanes()
    return jnp.where(left, first, second) + turn(jnp.where(left, second, first))


def spread(matrices, x):
    outs = []
    for (high, low), part in zip(matrices, x):
        outs.append(raw(high, part, ((1,), (0,))) + raw(low, part, ((1,), (0,))))
    return gather_heads(*outs)


def spread_back(matrices, x):
    outs = []
    for (high, low), part in zip(matrices, x):
        outs.append(raw(high, part, ((0,), (0,))) + raw(low, part, ((0,), (0,))))
    return gather_heads(*outs)


def fold(x):
    return x[:, 0:128] + x[:, 128:256]


def both_parts(x):
    return beside(x, rest_of(x))


def masked_sum(mask, x):
    return fold(raw(mask, both_parts(x), ((1,), (0,))))


def masked_sum_back(mask, x):
    return fold(raw(mask, both_parts(x), ((0,), (0,))))


def times_state(x, m):
    part = both_parts(m)
    return fold(raw(both_parts(x), jnp.concatenate([part, part], axis=0), ((1,), (0,))))


def times_state_back(x, m):
    low = rest_of(m)
    right = jnp.concatenate([beside(m, m), beside(low, low)], axis=0)
    return fold(raw(both_parts(x), right, ((1,), (1,))))


def outer(x, y):
    full = raw(both_parts(x), both_parts(y), ((0,), (0,)))
    return blocks_only(fold(full[0:128] + full[128:256]))


def slot_sums(x):
    left = left_lanes()
    return jnp.where(
        left,
        jnp.sum(jnp.where(left, x, 0.0), axis=1, keepdims=True),
        jnp.sum(jnp.where(left, 0.0, x), axis=1, keepdims=True),
    )


def next_state(k2, v2, e2, state, leaving, passing):
    mk, mv, z_in = state
    em = e2 * leaving
    return (
        outer(k2, em) + passing * mk,
        outer(em, v2) + passing * mv,
        jnp.sum(em, axis=0, keepdims=True) + passing * z_in,
    )


def attention(first, starts, proj, carry, o, lanes, saved):
    left = left_lanes()
    state = unpack_state(carry)
    chunks = proj.shape[0] // CHUNK
    for c in range(chunks):
        rows = slice(c * CHUNK, (c + 1) * CHUNK)
        q2, k2 = proj[rows, 0:128], proj[rows, 128:256]
        v2, e2 = proj[rows, 256:384], proj[rows, 384:512]
        mask, entering, leaving, passing = chunk_masks(starts, first, c)
        mk, mv, z_in = state
        z = masked_sum(mask.astype(F32).astype(BF16), e2) + entering * z_in
        affinity = affinity_of(rows_factor(q2), columns_factor(k2), mask)
        total = spread(affinity, narrow(e2)) + entering * times_state(q2, mk)
        s = total / z * 0.125
        top = jnp.where(
            left,
            jnp.max(jnp.where(left, s, -jnp.inf), axis=1, keepdims=True),
            jnp.max(jnp.where(left, -jnp.inf, s), axis=1, keepdims=True),
        )
        p = jnp.exp(s - top)
        p = p / slot_sums(p)
        r = p / z
        mixing = affinity_of(rows_factor(r), columns_factor(e2), mask)
        o[rows, lanes] = spread(mixing, narrow(v2)) + entering * times_state(r, mv)
        saved[rows, 0:128] = z
        saved[rows, 128:256] = s
        saved[rows, 256:384] = p
        if c + 1 < chunks:
            state = next_state(k2, v2, e2, state, leaving, passing)


def attention_back(first, starts, proj, carry, saved, d_o, lanes, dproj):
    chunks = proj.shape[0] // CHUNK
    states = [unpack_state(carry)]
    for c in range(chunks - 1):
        rows = slice(c * CHUNK, (c + 1) * CHUNK)
        _, _, leaving, passing = chunk_masks(starts, first, c)
        states.append(
            next_state(
                proj[rows, 128:256], proj[rows, 256:384], proj[rows, 384:512], states[c],
                leaving, passing,
            )
        )
    ahead = None
    for c in reversed(range(chunks)):
        rows = slice(c * CHUNK, (c + 1) * CHUNK)
        q2, k2 = proj[rows, 0:128], proj[rows, 128:256]
        v2, e2 = proj[rows, 256:384], proj[rows, 384:512]
        z, s, p = saved[rows, 0:128], saved[rows, 128:256], saved[rows, 256:384]
        do2 = d_o[rows, lanes]
        mask, entering, leaving, passing = chunk_masks(starts, first, c)
        mk, mv, _ = states[c]
        r = p / z
        do_in = entering * do2
        e_columns, e_narrow = columns_factor(e2), narrow(e2)
        mixing = affinity_of(rows_factor(r), e_columns, mask)
        d_mixing = affinity_of(rows_factor(do2), columns_factor(v2), mask)
        dv = spread_back(mixing, narrow(do2))
        dr = spread(d_mixing, e_narrow) + times_state_back(do_in, mv)
        de = spread_back(d_mixing, narrow(r))
        dp = dr / z
        dz = -dp * r
        ds = p * (dp - slot_sums(p * dp)) / z
        w = ds * 0.125
        dz = dz - ds * s
        w_in = entering * w
        affinity = affinity_of(rows_factor(q2), columns_factor(k2), mask)
        d_affinity = affinity_of(rows_factor(w), e_columns, mask)
        dq = spread(d_affinity, narrow(k2)) + times_state_back(w_in, mk)
        dk = spread_back(d_affinity, narrow(q2))
        de = de + spread_back(affinity, narrow(w))
        de = de + masked_sum_back(mask.astype(F32).astype(BF16), dz)
        if ahead is not None:
            dmk, dmv, dz_out = ahead
            em = e2 * leaving
            dv = dv + times_state(em, dmv)
            dk = dk + times_state_back(em, dmk)
            de = de + leaving * (times_state(k2, dmk) + times_state_back(v2, dmv) + dz_out)
        dproj[rows, 0:128] = dq
        dproj[rows, 128:256] = dk
        dproj[rows, 256:384] = dv
        dproj[rows, 384:512] = de
        now = (
            outer(q2, w_in),
            outer(r, do_in),
            jnp.sum(entering * dz, axis=0, keepdims=True),
        )
        if ahead is not None:
            now = tuple(a + passing * b for a, b in zip(now, ahead))
        ahead = now
    return pack_state(*ahead)


def own_pair(scal, j):
    return jnp.bitwise_xor(scal[2], j)


def attention_kernel(scal, starts, proj, carry, o, saved, j=None):
    here = proj if j is None else proj.at[own_pair(scal, j)]
    attention(scal[0], starts, here, carry, o, slice(0, 128), saved)


def middle_kernel(
    scal, o0, o1, o2, o3, x, wo, w0, w1, w2, w3, gain, shift, hidden, second, o_all, w_all,
):
    for j, ref in enumerate((o0, o1, o2, o3)):
        o_all[:, j * 128 : (j + 1) * 128] = ref[...]
    for j in range(2):
        which = pl.multiple_of(own_pair(scal, j) * 128, 128)
        w_all[j * 128 : (j + 1) * 128, :] = wo[pl.ds(which, 128), :]
    for k, ref in enumerate((w0, w1, w2, w3)):
        start = 256 + (k >> 1) * 128 + jnp.bitwise_xor(scal[1], k & 1) * 64
        w_all[pl.ds(pl.multiple_of(start, 64), 64), :] = ref[256:320, :]
    h = x[:, 0, :] + nn(o_all[...], w_all[...])
    hidden[...] = h
    nhat, _ = normalize(h)
    second[...] = nhat * gain[...] + shift[...]


def middle_back_kernel(
    scal, hidden, cot, ds0, ds1, ds2, ds3, u0, u1, u2, u3, gain, o_all, w_all,
    outputs, d_hidden, grads, d_o, send, keep, work,
):
    core = scal[1]
    outputs[:, 0, :] = hidden[...] + ((u0[...] + u1[...]) + (u2[...] + u3[...]))
    d_second = (ds0[...] + ds1[...]) + (ds2[...] + ds3[...])
    nhat, r = normalize(hidden[...])
    grads[0:1, :] = jnp.sum(d_second * nhat, axis=0, keepdims=True)
    grads[1:2, :] = jnp.sum(d_second, axis=0, keepdims=True)
    grads[2:8, :] = jnp.zeros((6, grads.shape[1]), F32)
    d = cot[:, 0, :] + norm_back(d_second, nhat, r, gain[...])
    d_hidden[...] = d
    d_o[...] = nt(d, w_all[...])
    work[...] = tn(o_all[...], d)
    for ref, which in ((send, 1 - core), (keep, core)):
        for j in range(4):
            rows = pl.ds(pl.multiple_of(j * 128 + which * 64, 64), 64)
            for b in range(4):
                ref[j, b * 64 : (b + 1) * 64, :] = work[rows, b * 128 : (b + 1) * 128]


def feed_forward_kernel(j, scal, second, cot, up, down, unit, other, packed, out, ds, up_far, down_far):
    where = pl.ds(pl.multiple_of(jnp.bitwise_xor(scal[3], j) * 256, 256), 256)
    for ref, half in ((unit, scal[2]), (other, 1 - scal[2])):
        place = pl.ds(pl.multiple_of(half * 128, 128), 128)
        for b in range(4):
            up_far[b * 128 : (b + 1) * 128, place] = ref[0:128, b * 128 : (b + 1) * 128]
        down_far[place, :] = ref[128:256, :]
    n_left, n_right = second[:, 0:256], second[:, 256:512]
    g = cot[:, 0, :]
    for half in range(2):
        if half == 0:
            up_left, up_right = up[0:256, where], up[256:512, where]
            down_block = down[where, :]
        else:
            up_left, up_right = up_far[0:256, :], up_far[256:512, :]
            down_block = down_far[...]
        u = nn(n_left, up_left) + nn(n_right, up_right)
        inner = GELU_C * (u + GELU_K * u * u * u)
        t = jnp.tanh(inner)
        act = 0.5 * u * (1.0 + t)
        slope = 0.5 * (1.0 + t) + 0.5 * u * (1.0 - t * t) * (
            GELU_C * (1.0 + 3.0 * GELU_K * u * u)
        )
        du = nt(g, down_block) * slope
        packed[2 * half, :, 0:256] = tn(n_left, du)
        packed[2 * half, :, 256:512] = tn(n_right, du)
        packed[2 * half + 1] = tn(act, g)
        out_part = nn(act, down_block)
        ds_left, ds_right = nt(du, up_left), nt(du, up_right)
        if half == 0:
            out[...] = out_part
            ds[:, 0:256] = ds_left
            ds[:, 256:512] = ds_right
        else:
            out[...] = out[...] + out_part
            ds[:, 0:256] = ds[:, 0:256] + ds_left
            ds[:, 256:512] = ds[:, 256:512] + ds_right


def pair_grads(first, starts, core, proj, dstate, normed, dproj, o_send, o_keep, send, keep, final):
    k2, v2, e2 = proj[:, 128:256], proj[:, 256:384], proj[:, 384:512]
    count = k2.shape[0]
    dmk, dmv, dz_out = unpack_state(dstate)
    leaving = (
        doc_of(starts, column(first, count)) == doc_of(starts, first + count - 1)
    ).astype(F32)
    em = e2 * leaving
    final[:, 0:128] = dproj[:, 0:128]
    final[:, 128:256] = dproj[:, 128:256] + times_state_back(em, dmk)
    final[:, 256:384] = dproj[:, 256:384] + times_state(em, dmv)
    de = dproj[:, 384:512] + leaving * (
        times_state(k2, dmk) + times_state_back(v2, dmv) + dz_out
    )
    final[:, 384:512] = e2 * de
    send[:, 0:512] = tn(lane_slice(normed, 1 - core, 256), final[...])
    keep[:, 0:512] = tn(lane_slice(normed, core, 256), final[...])
    send[:, 512:640] = o_send
    keep[:, 512:640] = o_keep


def first_back_kernel(
    scal, x, gain, d_hidden, f0, f31, f2, a0, b0, a1, b1, grads2, wq, wk, wv, wc,
    grad_x, grads, cat, acc, held, sems,
):
    core, pair = scal[1], scal[2]
    copies = [
        pltpu.make_async_copy(ref, held.at[w], sems.at[w])
        for w, ref in enumerate((wq, wk, wv, wc))
    ]
    for copy in copies:
        copy.start()
    for j, ref in enumerate((f0.at[0], f31.at[1])):
        which = jnp.bitwise_xor(pair, j)
        for w in range(4):
            start = pl.multiple_of(w * 256 + which * 128, 128)
            cat[:, pl.ds(start, 128)] = ref[:, w * 128 : (w + 1) * 128]
    total = None
    for w, copy in enumerate(copies):
        copy.wait()
        part = nt(cat[:, w * 256 : (w + 1) * 256], held[w])
        total = part if total is None else total + part
    acc[...] = total
    for which, refs in ((core, (a0, a1)), (1 - core, (b0, b1))):
        part = nt(f2[0], refs[0][...]) + nt(f31[0], refs[1][...])
        lanes = pl.ds(pl.multiple_of(which * 256, 256), 256)
        acc[:, lanes] = acc[:, lanes] + part
    d_normed = acc[...]
    nhat, r = normalize(x[:, 0, :])
    grads[...] = jnp.zeros(grads.shape, F32)
    grads[0:1, 0:512] = jnp.sum(d_normed * nhat, axis=0, keepdims=True)
    grads[1:2, 0:512] = jnp.sum(d_normed, axis=0, keepdims=True)
    grads[2:4, 0:512] = grads2[0:2, :]
    grad_x[:, 0, :] = d_hidden[...] + norm_back(d_normed, nhat, r, gain[...])


def table_of(groups):
    arrays, places = [], []
    for group in groups:
        places.append([])
        for array, lead, part in group:
            at = next((i for i, a in enumerate(arrays) if a is array), None)
            if at is None:
                at = len(arrays)
                arrays.append(array)
            places[-1].append((at, lead, part))
    return arrays, places


def total(scal, refs, place):
    value = None
    for at, lead, part in place:
        if isinstance(lead, tuple):
            ref = refs[at].at[lead[0] : lead[1], :]
        else:
            ref = refs[at] if lead is None else refs[at].at[lead]
        if part is None:
            term = ref[...]
        else:
            rows = ref.shape[0] // 2
            which = jnp.bitwise_xor(scal[2 if part < 2 else 6], part & 1) * rows
            term = ref[pl.ds(pl.multiple_of(which, rows), rows), :]
        value = term if value is None else value + term
    return value


def shape_of(group):
    array, lead, part = group[0]
    rows, cols = array.shape[-2:]
    if isinstance(lead, tuple):
        rows = lead[1] - lead[0]
    return (rows if part is None else rows // 2, cols)


def sums(outs, scal, after=(), rows=False):
    arrays, places = table_of([group for out in outs for group in out])
    shapes = []
    for out in outs:
        h, w = shape_of(out[0])
        if rows:
            shapes.append((sum(shape_of(g)[0] for g in out), w))
        else:
            shapes.append((h, w) if len(out) == 1 else (len(out), h, w))

    def kernel(scal, *refs):
        at = 0
        for n, out in enumerate(outs):
            target = refs[len(arrays) + n]
            row = 0
            for k in range(len(out)):
                value = total(scal, refs, places[at])
                at += 1
                if rows:
                    target[row : row + value.shape[0], :] = value
                    row += value.shape[0]
                elif len(out) == 1:
                    target[...] = value
                else:
                    target[k] = value

    return run(kernel, shapes, (scal,), arrays, after=after, us=SUM)


def choose(first, second, scal, at, after=()):
    arrays, places = table_of([first, second])

    def kernel(scal, *refs):
        values = [total(scal, refs, place) for place in places]
        for side in range(2):

            @pl.when(scal[at] == side)
            def _():
                refs[-2][...] = values[1 - side]
                refs[-1][...] = values[side]

    return run(kernel, [shape_of(first)] * 2, (scal,), arrays, after=after, us=SUM)


def halve(terms, scal, at, after=()):
    rows, cols = terms[0][0].shape[-2:]
    rows //= 2
    leads = [lead for _, lead in terms]

    def kernel(scal, *refs):
        for out, which in ((refs[-2], 1 - scal[at]), (refs[-1], scal[at])):
            block = pl.ds(pl.multiple_of(which * rows, rows), rows)
            value = None
            for ref, lead in zip(refs, leads):
                term = ref[block, :] if lead is None else ref[lead, block, :]
                value = term if value is None else value + term
            out[...] = value

    return run(
        kernel, [(rows, cols)] * 2, (scal,), [a for a, _ in terms], after=after, us=SUM
    )


def join(here, there, scal, at, tail=8, after=()):
    rows, cols = here.shape
    rows -= tail

    def kernel(scal, here, there, out):
        for ref, which in ((here, scal[at]), (there, 1 - scal[at])):
            block = pl.ds(pl.multiple_of(which * rows, rows), rows)
            out[block, :] = ref[0:rows, :]
        if tail:
            out[2 * rows :, :] = here[rows:, :] + there[rows:, :]

    return run(kernel, [(2 * rows + tail, cols)], (scal,), (here, there), after=after, us=SUM)[0]


def hidden_assemble_kernel(scal, p0, p1, p2, p3, up, down, token, sem):
    copies = []
    for k, ref in enumerate((p0, p1, p2, p3)):
        half = jnp.bitwise_xor(scal[2], k >> 1) * 128
        for far in range(2):
            block = jnp.bitwise_xor(scal[3], (k & 1) + 2 - 2 * far)
            lanes = pl.ds(pl.multiple_of(block * 256, 256), 256)
            first = far * 256
            upper = pl.ds(pl.multiple_of(half, 128), 128)
            lower = pl.ds(pl.multiple_of(half + 256, 128), 128)
            where = pl.ds(pl.multiple_of(block * 256 + half, 128), 128)
            rows = ref.at[first : first + 128, :]
            copies += [
                (rows.at[:, 0:256], up.at[upper, lanes]),
                (rows.at[:, 256:512], up.at[lower, lanes]),
                (ref.at[first + 128 : first + 256, :], down.at[where, :]),
            ]
    copies = [
        pltpu.make_async_copy(source, target, sem.at[n])
        for n, (source, target) in enumerate(copies)
    ]
    for copy in copies:
        copy.start()
    for copy in copies:
        copy.wait()


def qkvc_assemble_kernel(scal, *refs):
    (here, there), (wq, wk, wv, wc, wo), gains = refs[:2], refs[2:7], refs[7:]
    pieces = [ref.at[k] for ref in (here, there) for k in range(4)]
    size = here.shape[1] - 8
    tails = None
    for k, ref in enumerate(pieces):
        half = jnp.bitwise_xor(scal[1], k >> 2)
        which = jnp.bitwise_xor(scal[2], k & 1)
        first = jnp.bitwise_xor(scal[6], (k >> 1) & 1) * size
        rows = pl.ds(pl.multiple_of(half * 256 + first, size), size)
        lanes = pl.ds(pl.multiple_of(which * 128, 128), 128)
        for w, out in enumerate((wq, wk, wv, wc)):
            out[rows, lanes] = ref[0:size, w * 128 : (w + 1) * 128]
        for b in range(size // 64):
            start = pl.multiple_of(first // 64 * 128 + b * 128, 128)
            out_rows = pl.ds(pl.multiple_of(which * 128 + half * 64, 64), 64)
            wo[out_rows, pl.ds(start, 128)] = ref[b * 64 : (b + 1) * 64, 512:640]
        tail = ref[size : size + 8, 0:512]
        tails = tail if tails is None else tails + tail
    for k, ref in enumerate(gains):
        ref[...] = tails[k : k + 1, :]


def per_device(
    inputs, doc_starts, query_weight, key_weight, value_weight, control_weight, output_weight,
    up_weight, down_weight, first_gain, first_shift, second_gain, second_shift, cotangent,
):
    rows, _, width = inputs.shape
    devices = lax.axis_size("dp")
    place = lax.axis_index("dp").astype(jnp.int32)
    y = lax.axis_index("head").astype(jnp.int32)
    core = place & 1
    pair = (place >> 1) & 1
    one = lambda *v: jnp.stack([jnp.asarray(a, jnp.int32) for a in v])
    depth = (place >> 2) & 1
    bits = [at for at in range(31) if (1 << at) < devices]
    scal = one(y * rows, core, pair, depth * 2 + core, *((place >> at) & 1 for at in bits))
    gain1, shift1 = first_gain.reshape(1, width), first_shift.reshape(1, width)
    gain2, shift2 = second_gain.reshape(1, width), second_shift.reshape(1, width)
    weights = (query_weight, key_weight, value_weight, control_weight)

    def swap_y(a):
        return lax.ppermute(a, "head", [(0, 1), (1, 0)])

    def swap(a, bits):
        return lax.ppermute(a, "dp", [(i, i ^ bits) for i in range(devices)])

    to_second = lambda a: lax.ppermute(a, "head", [(0, 1)])
    to_first = lambda a: lax.ppermute(a, "head", [(1, 0)])

    tables = (scal, doc_starts)
    (piece,) = cut(cut_first_kernel, [(256, 512)], scal, weights, limit=60 * 2**20, near=True)
    qa0 = swap_y(piece)
    normed, proj_own, states_own = run(
        own_kernel,
        [(rows, width), (2, rows, 512), (2, 136, 128)],
        tables,
        (inputs, gain1, shift1) + weights,
        (pltpu.VMEM((4, width, 256), F32), pltpu.SemaphoreType.DMA((4,))),
        after=(piece,),
        far=4,
        us=FRONT,
    )
    carry_oth = to_second(states_own)
    qa0 = tie(qa0, (carry_oth,))
    qb0 = swap(qa0, 1)
    qa1 = swap(qa0, 2)
    (unit,) = cut(
        cut_second_kernel, [(320, 512)], scal, (output_weight, up_weight, down_weight), (qa0,)
    )
    unit0 = swap_y(unit)

    proj_oth0, state0 = run(
        other_kernel, [(rows, 512), (136, 128)], tables, (normed, qa0, qb0),
        after=(unit,), us=FRONT,
    )

    def attend(proj, carry, j, after=()):
        def kernel(scal, starts, proj, carry, o, saved):
            state = carry[own_pair(scal, j - 2)] if j >= 2 else carry[j]
            attention_kernel(scal, starts, proj, state, o, saved, j if j < 2 else None)

        return run(
            kernel, [(rows, 128), (rows, 384)], tables, (proj, carry), after=after, us=FRONT
        )

    qa1 = tie(qa1, (proj_oth0,))
    qb1 = swap(qa1, 1)
    o2, saved2 = attend(proj_oth0, carry_oth, 2, (qa1,))
    unit0 = tie(unit0, (o2,))
    unit1, unit2, unit4 = swap(unit0, 1), swap(unit0, 2), swap(unit0, 4)
    proj_oth1, states_oth = run(
        lambda scal, starts, normed, wa, wb, before, proj, states: other_kernel(
            scal, starts, normed, wa, wb, proj, states, before
        ),
        [(rows, 512), (2, 136, 128)], tables, (normed, qa1, qb1, state0),
        after=(unit0,), us=FRONT,
    )
    carry_own = to_second(states_oth)
    o3, saved3 = attend(proj_oth1, carry_oth, 3, (unit0,))
    o0, saved0 = attend(proj_own, carry_own, 0, (o3,))
    o1, saved1 = attend(proj_own, carry_own, 1, (o0, unit1))
    unit2 = tie(unit2, (o1,))
    unit3, unit6 = swap(unit2, 1), swap(unit2, 4)
    hidden, second, o_all, w_all = run(
        middle_kernel,
        [(rows, width), (rows, width), (rows, 512), (512, width)],
        (scal,),
        (o0, o1, o2, o3, inputs, output_weight, unit0, unit1, unit2, unit3, gain2, shift2),
        after=(spacer(unit2),),
        us=FRONT,
    )
    saved = (saved0, saved1, saved2, saved3)

    def feed_forward(j, unit, other, after=()):
        return run(
            lambda *refs: feed_forward_kernel(j, *refs),
            [(4, 256, 512), (rows, width), (rows, width)],
            (scal,),
            (second, cotangent, up_weight, down_weight, unit, other),
            (pltpu.VMEM((width, 256), F32), pltpu.VMEM((256, width), F32)),
            after=after,
        )

    part1, out1, ds1 = feed_forward(1, unit1, unit3)
    got1 = swap(part1, 1)
    part0, out0, ds0 = feed_forward(0, unit0, unit2, (ds1,))
    unit4, unit6 = tie(unit4, (ds0,)), tie(unit6, (ds0,))
    unit5, unit7 = swap(unit4, 1), swap(unit6, 1)
    def block0(k, part=None):
        return [(part0, k, part), (got1, k, part)]

    def block2(k, part=None):
        return [(part2, k, part), (got3, k, part)]

    u0, d0 = sums([[block0(2)], [block0(1, 1), block0(3, 1)]], scal)
    u0_y = swap_y(u0)
    d0_x = swap(d0, 2)
    part3, out3, ds3 = feed_forward(3, unit5, unit7, (u0,))
    got3 = swap(part3, 1)
    part2, out2, ds2 = feed_forward(2, unit4, unit6, (ds3,))
    u2, z_send, d2 = sums(
        [
            [block2(2)],
            [block0(0) + [(u0_y, None, None)]]
            + [block0(k, 0) + [(d0_x, n, None)] for n, k in enumerate((1, 3))],
            [block2(1, 1), block2(3, 1)],
        ],
        scal, (ds2,), rows=True,
    )
    u2_y = swap_y(u2)
    d2_x = swap(d2, 2)
    z_got = swap(z_send, 4)
    u0_z, d0_z = (0, 256), ((256, 384), (384, 512))
    outputs, d_hidden, grads2, d_o, o_send, o_keep = run(
        middle_back_kernel,
        [inputs.shape, (rows, width), (8, width), (rows, 512), (4, 256, 128), (4, 256, 128)],
        (scal,),
        (hidden, cotangent, ds0, ds1, ds2, ds3, out0, out1, out2, out3, gain2, o_all, w_all),
        (pltpu.VMEM((512, width), F32),),
        after=(u2,),
    )

    def back(js, after=()):
        arrays = (proj_own, proj_oth0, proj_oth1, carry_oth, carry_own, d_o) + saved

        def kernel(scal, starts, own, oth0, oth1, c_oth, c_own, d_o, *rest):
            dproj, dstate = rest[4:]
            for k, j in enumerate(js):
                if j < 2:
                    proj = own.at[own_pair(scal, j)]
                    carry = c_own[j]
                else:
                    proj = (oth0, oth1)[j - 2]
                    carry = c_oth[own_pair(scal, j - 2)]
                dstate[k] = attention_back(
                    scal[0], starts, proj, carry, rest[j], d_o,
                    slice(j * 128, (j + 1) * 128), dproj.at[k],
                )

        return run(
            kernel,
            [(len(js), rows, 512), (len(js), 136, 128)],
            tables,
            arrays,
            after=after,
        )

    def weight_grads(js, dstates, dprojs, after=(), extra=()):
        n = len(js)
        arrays = (proj_own, proj_oth0, proj_oth1, normed, o_send, o_keep)
        arrays += tuple(a for a, _ in dstates) + tuple(a for a, _ in dprojs)
        arrays += tuple(a for a, _ in extra)

        def kernel(scal, starts, own, oth0, oth1, normed, o_send, o_keep, *rest):
            states, grads, rest = rest[:n], rest[n : 2 * n], rest[2 * n :]
            send, keep, final = rest[len(extra) : len(extra) + 3]
            for k, j in enumerate(js):
                here = own.at[own_pair(scal, j)] if j < 2 else (oth0, oth1)[j - 2]
                pair_grads(
                    scal[0], starts, scal[1], here, states[k][dstates[k][1]], normed,
                    grads[k].at[dprojs[k][1]], o_send[j], o_keep[j],
                    send.at[k], keep.at[k], final.at[k],
                )
            if extra:
                value = None
                for ref, (_, lead) in zip(rest, extra):
                    term = ref[lead]
                    value = term if value is None else value + term
                rest[-1][...] = value

        outs = [(n, 256, 640), (n, 256, 640), (n, rows, 512)]
        return run(
            kernel, outs + [(256, 640)] * bool(extra), tables, arrays, after=after, us=LATE
        )

    dproj, dstate = back((1, 3, 0))
    dstate = to_first(dstate)
    up_terms = lambda part: block2(0, part) + [(u2_y, None, part), (z_got, u0_z, part)]
    d2, u2 = sums(
        [
            [block2(3, 0) + [(d2_x, (128, 256), None), (z_got, d0_z[1], None)]],
            [up_terms(1)],
        ],
        scal, (dproj,),
    )
    d2_y = swap_y(d2)
    u2_x = swap(u2, 2)
    send31, keep31, final31 = weight_grads(
        (3, 1), ((dstate, 0), (dstate, 1)), ((dproj, 1), (dproj, 0)), (d2,)
    )
    got31 = swap(send31, 1)
    ff_send, ff_keep = choose(
        up_terms(0) + [(u2_x, None, None)],
        block2(1, 0) + [(d2_x, (0, 128), None), (z_got, d0_z[0], None), (d2_y, None, None)],
        scal, 7, (final31,),
    )
    ff_got = swap(ff_send, 8)
    (y_send1,) = sums([[[(keep31, 0, None), (got31, 0, None)]]], scal, (ff_send,))
    y_got1 = swap_y(y_send1)
    dproj2, dstate2 = back((2,), (y_send1,))
    dstate2 = to_first(dstate2)
    send2, keep2, final2, own_sum1 = weight_grads(
        (2,), ((dstate, 2),), ((dproj2, 0),), (dproj2,), ((keep31, 1), (got31, 1))
    )
    got2 = swap(send2, 1)
    (ff_shard,) = sums(
        [[[(ff_keep, None, None), (ff_got, None, None)]]], scal, (final2,)
    )
    step = ff_shard
    for at in bits[4:]:
        ff_send, ff_keep = halve([(ff_shard, None)], scal, at + 4, (step,))
        ff_got = swap(ff_send, 1 << at)
        (ff_shard,) = sums(
            [[[(ff_keep, None, None), (ff_got, None, None)]]], scal, (spacer(ff_send),)
        )
        step = ff_shard
    ff_steps = list(reversed(bits[3:]))
    ff_there = swap(ff_shard, 1 << ff_steps[0])
    y_far, x_far = sums(
        [
            [[(keep2, 0, 3), (got2, 0, 3)]],
            [[(own_sum1, None, 3), (y_got1, None, 3)]],
        ],
        scal, (ff_shard,),
    )
    y_far_got = swap_y(y_far)
    x_far_got = swap(x_far, 2)
    send0, keep0, final0 = weight_grads((0,), ((dstate2, 0),), ((dproj, 2),), (y_far,))
    step = spacer(final0)
    grad_inputs, grads1 = run(
        first_back_kernel,
        [inputs.shape, (8, 640)],
        (scal,),
        (inputs, gain1, d_hidden, final0, final31, final2, qa0, qb0, qa1, qb1, grads2)
        + weights,
        (
            pltpu.VMEM((rows, 1024), F32),
            pltpu.VMEM((rows, width), F32),
            pltpu.VMEM((4, width, 256), F32),
            pltpu.SemaphoreType.DMA((4,)),
        ),
        after=(step,),
        far=4,
        us=LATE,
    )
    step = grads1
    while ff_steps:
        to = ff_steps.pop(0)
        ff_shard = join(ff_shard, ff_there, scal, to + 4, 0, (step,))
        ff_there = swap(ff_shard, 1 << (ff_steps[0] if ff_steps else 2))
        step = spacer(ff_shard)
    got0 = swap(tie(send0, (ff_shard,)), 1)
    q_send, y_near, x_near = sums(
        [
            [[(keep0, 0, 3), (got0, 0, 3), (y_far_got, None, None), (x_far_got, None, None)]],
            [[(keep2, 0, 2), (got2, 0, 2)]],
            [[(own_sum1, None, 2), (y_got1, None, 2)]],
        ],
        scal, (step,),
    )
    q_got = swap(q_send, 4)
    y_near_got = swap_y(y_near)
    x_near_got = swap(x_near, 2)
    step = spacer(q_send)
    ff_pair, gains = sums(
        [[[(ff_shard, None, None)], [(ff_there, None, None)]], [[(grads1, None, None)]]],
        scal, (step,), rows=True,
    )
    gains_got = swap_y(gains)
    ff_x = swap(ff_pair, 2)
    step = spacer(ff_pair)
    (part,) = sums(
        [
            [
                [
                    (keep0, 0, 2), (got0, 0, 2), (y_near_got, None, None),
                    (x_near_got, None, None), (q_got, None, None),
                ]
            ]
        ],
        scal, (step,),
    )
    part_got = swap(part, 8)
    step = spacer(part)
    (gains,) = sums([[[(gains, None, None), (gains_got, None, None)]]], scal, (step,))
    for at in bits[3:]:
        gains_got = swap(gains, 1 << at)
        step = spacer(gains)
        terms = [
            [(part, None, None), (part_got, None, None)],
            [(gains, None, None), (gains_got, None, None)],
        ]
        if at == bits[-1]:
            (shard,) = sums([terms], scal, (step,), rows=True)
        else:
            part, gains = sums([terms[:1], terms[1:]], scal, (step,))
            part_got = swap(part, 2 << at)
    quarters = [shard] + [swap(shard, 2 * k) for k in (1, 2, 3)]
    ff_x = tie(ff_x, (quarters[2],))
    ff_core, ff_x_core = swap(ff_pair, 1), swap(ff_x, 1)
    grad_up, grad_down, token = run(
        hidden_assemble_kernel,
        [up_weight.shape, down_weight.shape, (8, 128)],
        (scal,),
        (ff_pair, ff_core, ff_x, ff_x_core),
        (pltpu.SemaphoreType.DMA((24,)),),
        after=(spacer(ff_x),),
        away=True,
    )
    (quarters,) = sums([[[(a, None, None)] for a in quarters]], scal, (token,))
    *weight_grad, gain_a, gain_b, gain_c, gain_d = run(
        qkvc_assemble_kernel,
        [w.shape for w in weights] + [output_weight.shape] + [(1, width)] * 4,
        (scal,),
        (quarters, swap(quarters, 1)),
        after=(spacer(quarters),),
    )
    return (
        outputs, grad_inputs,
        *weight_grad, grad_up, grad_down,
        gain_a[0], gain_b[0], gain_c[0], gain_d[0],
    )


def solution(mesh):
    rows = P("head", "dp", None)
    cols = P(None, "head")
    tall = P("head", None)
    flat = P()
    return jax.shard_map(
        per_device,
        mesh=mesh,
        in_specs=(
            rows, P("dp", None), cols, cols, cols, cols, tall, cols, tall,
            flat, flat, flat, flat, rows,
        ),
        out_specs=(
            rows, rows, cols, cols, cols, cols, tall, cols, tall, flat, flat, flat, flat,
        ),
        check_vma=False,
    )
```

```python
import jax
import jax.numpy as jnp
from jax import lax
from jax.experimental import pallas as pl
from jax.experimental.pallas import tpu as pltpu
from jax.sharding import PartitionSpec as P

F32 = jnp.float32
HIGH = lax.Precision.HIGH
CHUNK = 256
EPS = 1e-05
GELU_C = 0.7978845608028654
GELU_K = 0.044715
VMEM_LIMIT = 16 * 2**20


def dot(left, right, dims):
    return lax.dot_general(
        left, right, (dims, ((), ())), precision=HIGH, preferred_element_type=F32
    )


def nn(left, right):
    return dot(left, right, ((1,), (0,)))


def nt(left, right):
    return dot(left, right, ((1,), (1,)))


def tn(left, right):
    return dot(left, right, ((0,), (0,)))


def whole():
    return pl.BlockSpec(memory_space=pltpu.VMEM)


def anywhere():
    return pl.BlockSpec(memory_space=pl.ANY)


def distant():
    return pl.BlockSpec(memory_space=pltpu.HBM)


def scalars():
    return pl.BlockSpec(memory_space=pltpu.SMEM)


FRONT, HEAVY, LATE, SUM = 20.0, 20.0, 20.0, 20.0


def cost(us):
    return pl.CostEstimate(flops=int(us * 1153e6), bytes_accessed=0, transcendentals=0)


def run(kernel, outs, scal, arrays, scratch=(), after=(), far=0, us=HEAVY, away=False):
    out_shape = [jax.ShapeDtypeStruct(shape, F32) for shape in outs]
    first, last = len(scal) + len(arrays), len(scal) + len(arrays) + len(after)
    return pl.pallas_call(
        lambda *refs: kernel(*refs[:first], *refs[last:]),
        out_shape=out_shape,
        in_specs=[scalars()] * len(scal)
        + [whole()] * (len(arrays) - far)
        + [distant()] * far
        + [anywhere()] * len(after),
        out_specs=[anywhere() if away else whole()] * len(outs),
        scratch_shapes=list(scratch),
        compiler_params=pltpu.CompilerParams(vmem_limit_bytes=VMEM_LIMIT),
        cost_estimate=cost(us),
    )(*scal, *arrays, *after)


def tie(array, after):
    count = 1 + len(after)
    return pl.pallas_call(
        lambda *refs: None,
        out_shape=jax.ShapeDtypeStruct(array.shape, F32),
        in_specs=[anywhere()] * count,
        out_specs=anywhere(),
        input_output_aliases={0: 0},
        compiler_params=pltpu.CompilerParams(vmem_limit_bytes=2**20),
        cost_estimate=pl.CostEstimate(flops=0, bytes_accessed=0, transcendentals=0),
    )(array, *after)


def spacer(*after):
    return pl.pallas_call(
        lambda *refs: None,
        out_shape=jax.ShapeDtypeStruct((8, 128), F32),
        in_specs=[anywhere()] * len(after),
        out_specs=anywhere(),
        compiler_params=pltpu.CompilerParams(vmem_limit_bytes=2**20),
        cost_estimate=cost(HEAVY),
    )(*after)


def lane_slice(ref, index, width):
    return ref[:, pl.ds(pl.multiple_of(index * width, width), width)]


def normalize(x):
    centre = x - jnp.mean(x, axis=-1, keepdims=True)
    spread = jnp.mean(centre * centre, axis=-1, keepdims=True)
    r = lax.rsqrt(spread + EPS)
    return centre * r, r


def norm_back(dy, nhat, r, gain):
    dyg = dy * gain
    first = jnp.mean(dyg, axis=-1, keepdims=True)
    second = jnp.mean(dyg * nhat, axis=-1, keepdims=True)
    return r * (dyg - first - nhat * second)


def doc_of(starts, position):
    total = jnp.zeros(jnp.shape(position), jnp.int32)
    for k in range(starts.shape[1]):
        total = total + (position >= starts[0, k]).astype(jnp.int32)
    return total


def column(first, count):
    return first + lax.broadcasted_iota(jnp.int32, (count, 1), 0)


def left_lanes():
    return lax.broadcasted_iota(jnp.int32, (1, 128), 1) < 64


def pack_state(mk, mv, z):
    left = left_lanes()
    return jnp.concatenate(
        [
            jnp.where(left, mk[0:64], mk[64:128]),
            jnp.where(left, mv[0:64], mv[64:128]),
            jnp.broadcast_to(z, (8, 128)),
        ],
        axis=0,
    )


def blocks_only(m):
    diagonal = (lax.broadcasted_iota(jnp.int32, (128, 128), 0) < 64) == (
        lax.broadcasted_iota(jnp.int32, (128, 128), 1) < 64
    )
    return jnp.where(diagonal, m, 0.0)


def unpack_state(state):
    mk = state[0:64]
    mv = state[64:128]
    return (
        blocks_only(jnp.concatenate([mk, mk], axis=0)),
        blocks_only(jnp.concatenate([mv, mv], axis=0)),
        state[128:129],
    )


def end_state(k2, v2, e2, starts, first):
    count = k2.shape[0]
    kept = (doc_of(starts, column(first, count)) == doc_of(starts, first + count - 1)).astype(F32)
    em = e2 * kept
    return pack_state(outer(k2, em), outer(em, v2), jnp.sum(em, axis=0, keepdims=True))


def cut_first_kernel(scal, wq, wk, wv, wc, piece, sems):
    rows = pl.ds(pl.multiple_of(scal[1] * 256, 256), 256)
    lanes = pl.ds(pl.multiple_of(scal[2] * 128, 128), 128)
    copies = [
        pltpu.make_async_copy(
            ref.at[rows, lanes], piece.at[:, w * 128 : (w + 1) * 128], sems.at[w]
        )
        for w, ref in enumerate((wq, wk, wv, wc))
    ]
    for copy in copies:
        copy.start()
    for copy in copies:
        copy.wait()


def cut_second_kernel(scal, wo, up, down, piece, sems):
    unit = pl.ds(pl.multiple_of(scal[3] * 256 + scal[2] * 128, 128), 128)
    thin = pl.ds(pl.multiple_of((scal[2] * 2 + scal[1]) * 64, 64), 64)
    copies = [
        pltpu.make_async_copy(
            up.at[b * 128 : (b + 1) * 128, unit], piece.at[0:128, b * 128 : (b + 1) * 128],
            sems.at[b],
        )
        for b in range(4)
    ]
    copies.append(pltpu.make_async_copy(down.at[unit, :], piece.at[128:256, :], sems.at[4]))
    copies.append(pltpu.make_async_copy(wo.at[thin, :], piece.at[256:320, :], sems.at[5]))
    for copy in copies:
        copy.start()
    for copy in copies:
        copy.wait()


def cut(kernel, shapes, scal, arrays, after=(), limit=2**20, near=False):
    first, last = 1 + len(arrays), 1 + len(arrays) + len(after)
    out_shape = [jax.ShapeDtypeStruct(shape, F32) for shape in shapes]
    return pl.pallas_call(
        lambda *refs: kernel(*refs[:first], *refs[last:]),
        out_shape=out_shape,
        in_specs=[scalars()] + [distant()] * len(arrays) + [anywhere()] * len(after),
        out_specs=[whole() if near else anywhere()] * len(shapes),
        scratch_shapes=[pltpu.SemaphoreType.DMA((6,))],
        compiler_params=pltpu.CompilerParams(vmem_limit_bytes=limit),
        cost_estimate=cost(FRONT),
    )(scal, *arrays, *after)


def own_kernel(scal, starts, x, gain, shift, wq, wk, wv, wc, normed, proj, states, held, sems):
    copies = [
        pltpu.make_async_copy(ref, held.at[w], sems.at[w])
        for w, ref in enumerate((wq, wk, wv, wc))
    ]
    for copy in copies:
        copy.start()
    nhat, _ = normalize(x[:, 0, :])
    n = nhat * gain[...] + shift[...]
    normed[...] = n
    for w, copy in enumerate(copies):
        copy.wait()
        full = nn(n, held[w])
        if w == 3:
            full = jnp.exp(full)
        for p in range(2):
            proj[p, :, w * 128 : (w + 1) * 128] = full[:, p * 128 : (p + 1) * 128]
    for p in range(2):
        states[p] = end_state(
            proj[p, :, 128:256], proj[p, :, 256:384], proj[p, :, 384:512], starts, scal[0]
        )


def other_kernel(scal, starts, normed, wa, wb, proj, states, before=None):
    core = scal[1]
    full = nn(lane_slice(normed, core, 256), wa[...]) + nn(
        lane_slice(normed, 1 - core, 256), wb[...]
    )
    proj[:, 0:384] = full[:, 0:384]
    proj[:, 384:512] = jnp.exp(full[:, 384:512])
    state = end_state(proj[:, 128:256], proj[:, 256:384], proj[:, 384:512], starts, scal[0])
    if before is None:
        states[...] = state
    else:
        states[0] = before[...]
        states[1] = state


def chunk_masks(starts, first, c):
    begin = first + c * CHUNK
    position = column(begin, CHUNK)
    docs = doc_of(starts, position)
    row = begin + lax.broadcasted_iota(jnp.int32, (1, CHUNK), 1)
    mask = (position >= row) & (docs == doc_of(starts, row))
    before = doc_of(starts, begin - 1)
    last = doc_of(starts, begin + CHUNK - 1)
    entering = (docs == before).astype(F32)
    leaving = (docs == last).astype(F32)
    passing = (before == last).astype(F32)
    return mask, entering, leaving, passing


BF16 = jnp.bfloat16


def raw(left, right, dims):
    return lax.dot_general(left, right, (dims, ((), ())), preferred_element_type=F32)


def rest_of(x):
    return x - x.astype(BF16).astype(F32)


def turn(x):
    return pltpu.roll(x, 64, 1)


def beside(a, b):
    return jnp.concatenate([a, b], axis=1).astype(BF16)


def rows_factor(x):
    left = left_lanes()
    low = turn(rest_of(x))
    return (
        beside(jnp.where(left, x, low), jnp.where(left, x, 0.0)),
        beside(jnp.where(left, low, x), jnp.where(left, 0.0, x)),
    )


def columns_factor(x):
    left = left_lanes()
    other = turn(x)
    low = rest_of(x)
    return (
        beside(jnp.where(left, x, other), low),
        beside(jnp.where(left, other, x), low),
    )


def affinity_of(rows, columns, mask):
    result = []
    for r, c in zip(rows, columns):
        value = jnp.where(mask, raw(r, c, ((1,), (1,))), 0.0)
        high = value.astype(BF16)
        result.append((high, (value - high.astype(F32)).astype(BF16)))
    return result


def narrow(x):
    left = left_lanes()
    low = rest_of(x)
    return (
        jnp.where(left, x, turn(low)).astype(BF16),
        jnp.where(left, turn(low), x).astype(BF16),
    )


def gather_heads(first, second):
    left = left_lanes()
    return jnp.where(left, first, second) + turn(jnp.where(left, second, first))


def spread(matrices, x):
    outs = []
    for (high, low), part in zip(matrices, x):
        outs.append(raw(high, part, ((1,), (0,))) + raw(low, part, ((1,), (0,))))
    return gather_heads(*outs)


def spread_back(matrices, x):
    outs = []
    for (high, low), part in zip(matrices, x):
        outs.append(raw(high, part, ((0,), (0,))) + raw(low, part, ((0,), (0,))))
    return gather_heads(*outs)


def fold(x):
    return x[:, 0:128] + x[:, 128:256]


def both_parts(x):
    return beside(x, rest_of(x))


def masked_sum(mask, x):
    return fold(raw(mask, both_parts(x), ((1,), (0,))))


def masked_sum_back(mask, x):
    return fold(raw(mask, both_parts(x), ((0,), (0,))))


def times_state(x, m):
    part = both_parts(m)
    return fold(raw(both_parts(x), jnp.concatenate([part, part], axis=0), ((1,), (0,))))


def times_state_back(x, m):
    low = rest_of(m)
    right = jnp.concatenate([beside(m, m), beside(low, low)], axis=0)
    return fold(raw(both_parts(x), right, ((1,), (1,))))


def outer(x, y):
    full = raw(both_parts(x), both_parts(y), ((0,), (0,)))
    return blocks_only(fold(full[0:128] + full[128:256]))


def slot_sums(x):
    left = left_lanes()
    return jnp.where(
        left,
        jnp.sum(jnp.where(left, x, 0.0), axis=1, keepdims=True),
        jnp.sum(jnp.where(left, 0.0, x), axis=1, keepdims=True),
    )


def next_state(k2, v2, e2, state, leaving, passing):
    mk, mv, z_in = state
    em = e2 * leaving
    return (
        outer(k2, em) + passing * mk,
        outer(em, v2) + passing * mv,
        jnp.sum(em, axis=0, keepdims=True) + passing * z_in,
    )


def attention(first, starts, proj, carry, o, lanes, saved):
    left = left_lanes()
    state = unpack_state(carry)
    chunks = proj.shape[0] // CHUNK
    for c in range(chunks):
        rows = slice(c * CHUNK, (c + 1) * CHUNK)
        q2, k2 = proj[rows, 0:128], proj[rows, 128:256]
        v2, e2 = proj[rows, 256:384], proj[rows, 384:512]
        mask, entering, leaving, passing = chunk_masks(starts, first, c)
        mk, mv, z_in = state
        z = masked_sum(mask.astype(F32).astype(BF16), e2) + entering * z_in
        affinity = affinity_of(rows_factor(q2), columns_factor(k2), mask)
        total = spread(affinity, narrow(e2)) + entering * times_state(q2, mk)
        s = total / z * 0.125
        top = jnp.where(
            left,
            jnp.max(jnp.where(left, s, -jnp.inf), axis=1, keepdims=True),
            jnp.max(jnp.where(left, -jnp.inf, s), axis=1, keepdims=True),
        )
        p = jnp.exp(s - top)
        p = p / slot_sums(p)
        r = p / z
        mixing = affinity_of(rows_factor(r), columns_factor(e2), mask)
        o[rows, lanes] = spread(mixing, narrow(v2)) + entering * times_state(r, mv)
        saved[rows, 0:128] = z
        saved[rows, 128:256] = s
        saved[rows, 256:384] = p
        if c + 1 < chunks:
            state = next_state(k2, v2, e2, state, leaving, passing)


def attention_back(first, starts, proj, carry, saved, d_o, lanes, dproj):
    chunks = proj.shape[0] // CHUNK
    states = [unpack_state(carry)]
    for c in range(chunks - 1):
        rows = slice(c * CHUNK, (c + 1) * CHUNK)
        _, _, leaving, passing = chunk_masks(starts, first, c)
        states.append(
            next_state(
                proj[rows, 128:256], proj[rows, 256:384], proj[rows, 384:512], states[c],
                leaving, passing,
            )
        )
    ahead = None
    for c in reversed(range(chunks)):
        rows = slice(c * CHUNK, (c + 1) * CHUNK)
        q2, k2 = proj[rows, 0:128], proj[rows, 128:256]
        v2, e2 = proj[rows, 256:384], proj[rows, 384:512]
        z, s, p = saved[rows, 0:128], saved[rows, 128:256], saved[rows, 256:384]
        do2 = d_o[rows, lanes]
        mask, entering, leaving, passing = chunk_masks(starts, first, c)
        mk, mv, _ = states[c]
        r = p / z
        do_in = entering * do2
        e_columns, e_narrow = columns_factor(e2), narrow(e2)
        mixing = affinity_of(rows_factor(r), e_columns, mask)
        d_mixing = affinity_of(rows_factor(do2), columns_factor(v2), mask)
        dv = spread_back(mixing, narrow(do2))
        dr = spread(d_mixing, e_narrow) + times_state_back(do_in, mv)
        de = spread_back(d_mixing, narrow(r))
        dp = dr / z
        dz = -dp * r
        ds = p * (dp - slot_sums(p * dp)) / z
        w = ds * 0.125
        dz = dz - ds * s
        w_in = entering * w
        affinity = affinity_of(rows_factor(q2), columns_factor(k2), mask)
        d_affinity = affinity_of(rows_factor(w), e_columns, mask)
        dq = spread(d_affinity, narrow(k2)) + times_state_back(w_in, mk)
        dk = spread_back(d_affinity, narrow(q2))
        de = de + spread_back(affinity, narrow(w))
        de = de + masked_sum_back(mask.astype(F32).astype(BF16), dz)
        if ahead is not None:
            dmk, dmv, dz_out = ahead
            em = e2 * leaving
            dv = dv + times_state(em, dmv)
            dk = dk + times_state_back(em, dmk)
            de = de + leaving * (times_state(k2, dmk) + times_state_back(v2, dmv) + dz_out)
        dproj[rows, 0:128] = dq
        dproj[rows, 128:256] = dk
        dproj[rows, 256:384] = dv
        dproj[rows, 384:512] = de
        now = (
            outer(q2, w_in),
            outer(r, do_in),
            jnp.sum(entering * dz, axis=0, keepdims=True),
        )
        if ahead is not None:
            now = tuple(a + passing * b for a, b in zip(now, ahead))
        ahead = now
    return pack_state(*ahead)


def own_pair(scal, j):
    return jnp.bitwise_xor(scal[2], j)


def attention_kernel(scal, starts, proj, carry, o, saved, j=None):
    here = proj if j is None else proj.at[own_pair(scal, j)]
    attention(scal[0], starts, here, carry, o, slice(0, 128), saved)


def middle_kernel(
    scal, o0, o1, o2, o3, x, wo, w0, w1, w2, w3, gain, shift, hidden, second, o_all, w_all,
):
    for j, ref in enumerate((o0, o1, o2, o3)):
        o_all[:, j * 128 : (j + 1) * 128] = ref[...]
    for j in range(2):
        which = pl.multiple_of(own_pair(scal, j) * 128, 128)
        w_all[j * 128 : (j + 1) * 128, :] = wo[pl.ds(which, 128), :]
    for k, ref in enumerate((w0, w1, w2, w3)):
        start = 256 + (k >> 1) * 128 + jnp.bitwise_xor(scal[1], k & 1) * 64
        w_all[pl.ds(pl.multiple_of(start, 64), 64), :] = ref[256:320, :]
    h = x[:, 0, :] + nn(o_all[...], w_all[...])
    hidden[...] = h
    nhat, _ = normalize(h)
    second[...] = nhat * gain[...] + shift[...]


def middle_back_kernel(
    scal, hidden, cot, ds0, ds1, ds2, ds3, u0, u1, u2, u3, gain, o_all, w_all,
    outputs, d_hidden, grads, d_o, send, keep, work,
):
    core = scal[1]
    outputs[:, 0, :] = hidden[...] + ((u0[...] + u1[...]) + (u2[...] + u3[...]))
    d_second = (ds0[...] + ds1[...]) + (ds2[...] + ds3[...])
    nhat, r = normalize(hidden[...])
    grads[0:1, :] = jnp.sum(d_second * nhat, axis=0, keepdims=True)
    grads[1:2, :] = jnp.sum(d_second, axis=0, keepdims=True)
    grads[2:8, :] = jnp.zeros((6, grads.shape[1]), F32)
    d = cot[:, 0, :] + norm_back(d_second, nhat, r, gain[...])
    d_hidden[...] = d
    d_o[...] = nt(d, w_all[...])
    work[...] = tn(o_all[...], d)
    for ref, which in ((send, 1 - core), (keep, core)):
        for j in range(4):
            rows = pl.ds(pl.multiple_of(j * 128 + which * 64, 64), 64)
            for b in range(4):
                ref[j, b * 64 : (b + 1) * 64, :] = work[rows, b * 128 : (b + 1) * 128]


def feed_forward_kernel(j, scal, second, cot, up, down, unit, other, packed, out, ds, up_far, down_far):
    where = pl.ds(pl.multiple_of(jnp.bitwise_xor(scal[3], j) * 256, 256), 256)
    for ref, half in ((unit, scal[2]), (other, 1 - scal[2])):
        place = pl.ds(pl.multiple_of(half * 128, 128), 128)
        for b in range(4):
            up_far[b * 128 : (b + 1) * 128, place] = ref[0:128, b * 128 : (b + 1) * 128]
        down_far[place, :] = ref[128:256, :]
    n_left, n_right = second[:, 0:256], second[:, 256:512]
    g = cot[:, 0, :]
    for half in range(2):
        if half == 0:
            up_left, up_right = up[0:256, where], up[256:512, where]
            down_block = down[where, :]
        else:
            up_left, up_right = up_far[0:256, :], up_far[256:512, :]
            down_block = down_far[...]
        u = nn(n_left, up_left) + nn(n_right, up_right)
        inner = GELU_C * (u + GELU_K * u * u * u)
        t = jnp.tanh(inner)
        act = 0.5 * u * (1.0 + t)
        slope = 0.5 * (1.0 + t) + 0.5 * u * (1.0 - t * t) * (
            GELU_C * (1.0 + 3.0 * GELU_K * u * u)
        )
        du = nt(g, down_block) * slope
        packed[2 * half, :, 0:256] = tn(n_left, du)
        packed[2 * half, :, 256:512] = tn(n_right, du)
        packed[2 * half + 1] = tn(act, g)
        out_part = nn(act, down_block)
        ds_left, ds_right = nt(du, up_left), nt(du, up_right)
        if half == 0:
            out[...] = out_part
            ds[:, 0:256] = ds_left
            ds[:, 256:512] = ds_right
        else:
            out[...] = out[...] + out_part
            ds[:, 0:256] = ds[:, 0:256] + ds_left
            ds[:, 256:512] = ds[:, 256:512] + ds_right


def pair_grads(first, starts, core, proj, dstate, normed, dproj, o_send, o_keep, send, keep, final):
    k2, v2, e2 = proj[:, 128:256], proj[:, 256:384], proj[:, 384:512]
    count = k2.shape[0]
    dmk, dmv, dz_out = unpack_state(dstate)
    leaving = (
        doc_of(starts, column(first, count)) == doc_of(starts, first + count - 1)
    ).astype(F32)
    em = e2 * leaving
    final[:, 0:128] = dproj[:, 0:128]
    final[:, 128:256] = dproj[:, 128:256] + times_state_back(em, dmk)
    final[:, 256:384] = dproj[:, 256:384] + times_state(em, dmv)
    de = dproj[:, 384:512] + leaving * (
        times_state(k2, dmk) + times_state_back(v2, dmv) + dz_out
    )
    final[:, 384:512] = e2 * de
    send[:, 0:512] = tn(lane_slice(normed, 1 - core, 256), final[...])
    keep[:, 0:512] = tn(lane_slice(normed, core, 256), final[...])
    send[:, 512:640] = o_send
    keep[:, 512:640] = o_keep


def first_back_kernel(
    scal, x, gain, d_hidden, f0, f31, f2, a0, b0, a1, b1, grads2, wq, wk, wv, wc,
    grad_x, grads, cat, acc, held, sems,
):
    core, pair = scal[1], scal[2]
    copies = [
        pltpu.make_async_copy(ref, held.at[w], sems.at[w])
        for w, ref in enumerate((wq, wk, wv, wc))
    ]
    for copy in copies:
        copy.start()
    for j, ref in enumerate((f0.at[0], f31.at[1])):
        which = jnp.bitwise_xor(pair, j)
        for w in range(4):
            start = pl.multiple_of(w * 256 + which * 128, 128)
            cat[:, pl.ds(start, 128)] = ref[:, w * 128 : (w + 1) * 128]
    total = None
    for w, copy in enumerate(copies):
        copy.wait()
        part = nt(cat[:, w * 256 : (w + 1) * 256], held[w])
        total = part if total is None else total + part
    acc[...] = total
    for which, refs in ((core, (a0, a1)), (1 - core, (b0, b1))):
        part = nt(f2[0], refs[0][...]) + nt(f31[0], refs[1][...])
        lanes = pl.ds(pl.multiple_of(which * 256, 256), 256)
        acc[:, lanes] = acc[:, lanes] + part
    d_normed = acc[...]
    nhat, r = normalize(x[:, 0, :])
    grads[...] = jnp.zeros(grads.shape, F32)
    grads[0:1, 0:512] = jnp.sum(d_normed * nhat, axis=0, keepdims=True)
    grads[1:2, 0:512] = jnp.sum(d_normed, axis=0, keepdims=True)
    grads[2:4, 0:512] = grads2[0:2, :]
    grad_x[:, 0, :] = d_hidden[...] + norm_back(d_normed, nhat, r, gain[...])


def table_of(groups):
    arrays, places = [], []
    for group in groups:
        places.append([])
        for array, lead, part in group:
            at = next((i for i, a in enumerate(arrays) if a is array), None)
            if at is None:
                at = len(arrays)
                arrays.append(array)
            places[-1].append((at, lead, part))
    return arrays, places


def total(scal, refs, place):
    value = None
    for at, lead, part in place:
        if isinstance(lead, tuple):
            ref = refs[at].at[lead[0] : lead[1], :]
        else:
            ref = refs[at] if lead is None else refs[at].at[lead]
        if part is None:
            term = ref[...]
        else:
            rows = ref.shape[0] // 2
            which = jnp.bitwise_xor(scal[2 if part < 2 else 6], part & 1) * rows
            term = ref[pl.ds(pl.multiple_of(which, rows), rows), :]
        value = term if value is None else value + term
    return value


def shape_of(group):
    array, lead, part = group[0]
    rows, cols = array.shape[-2:]
    if isinstance(lead, tuple):
        rows = lead[1] - lead[0]
    return (rows if part is None else rows // 2, cols)


def sums(outs, scal, after=(), rows=False):
    arrays, places = table_of([group for out in outs for group in out])
    shapes = []
    for out in outs:
        h, w = shape_of(out[0])
        if rows:
            shapes.append((sum(shape_of(g)[0] for g in out), w))
        else:
            shapes.append((h, w) if len(out) == 1 else (len(out), h, w))

    def kernel(scal, *refs):
        at = 0
        for n, out in enumerate(outs):
            target = refs[len(arrays) + n]
            row = 0
            for k in range(len(out)):
                value = total(scal, refs, places[at])
                at += 1
                if rows:
                    target[row : row + value.shape[0], :] = value
                    row += value.shape[0]
                elif len(out) == 1:
                    target[...] = value
                else:
                    target[k] = value

    return run(kernel, shapes, (scal,), arrays, after=after, us=SUM)


def choose(first, second, scal, at, after=()):
    arrays, places = table_of([first, second])

    def kernel(scal, *refs):
        values = [total(scal, refs, place) for place in places]
        for side in range(2):

            @pl.when(scal[at] == side)
            def _():
                refs[-2][...] = values[1 - side]
                refs[-1][...] = values[side]

    return run(kernel, [shape_of(first)] * 2, (scal,), arrays, after=after, us=SUM)


def halve(terms, scal, at, after=()):
    rows, cols = terms[0][0].shape[-2:]
    rows //= 2
    leads = [lead for _, lead in terms]

    def kernel(scal, *refs):
        for out, which in ((refs[-2], 1 - scal[at]), (refs[-1], scal[at])):
            block = pl.ds(pl.multiple_of(which * rows, rows), rows)
            value = None
            for ref, lead in zip(refs, leads):
                term = ref[block, :] if lead is None else ref[lead, block, :]
                value = term if value is None else value + term
            out[...] = value

    return run(
        kernel, [(rows, cols)] * 2, (scal,), [a for a, _ in terms], after=after, us=SUM
    )


def join(here, there, scal, at, tail=8, after=()):
    rows, cols = here.shape
    rows -= tail

    def kernel(scal, here, there, out):
        for ref, which in ((here, scal[at]), (there, 1 - scal[at])):
            block = pl.ds(pl.multiple_of(which * rows, rows), rows)
            out[block, :] = ref[0:rows, :]
        if tail:
            out[2 * rows :, :] = here[rows:, :] + there[rows:, :]

    return run(kernel, [(2 * rows + tail, cols)], (scal,), (here, there), after=after, us=SUM)[0]


def hidden_assemble_kernel(scal, p0, p1, p2, p3, up, down, token, sem):
    copies = []
    for k, ref in enumerate((p0, p1, p2, p3)):
        half = jnp.bitwise_xor(scal[2], k >> 1) * 128
        for far in range(2):
            block = jnp.bitwise_xor(scal[3], (k & 1) + 2 - 2 * far)
            lanes = pl.ds(pl.multiple_of(block * 256, 256), 256)
            first = far * 256
            upper = pl.ds(pl.multiple_of(half, 128), 128)
            lower = pl.ds(pl.multiple_of(half + 256, 128), 128)
            where = pl.ds(pl.multiple_of(block * 256 + half, 128), 128)
            rows = ref.at[first : first + 128, :]
            copies += [
                (rows.at[:, 0:256], up.at[upper, lanes]),
                (rows.at[:, 256:512], up.at[lower, lanes]),
                (ref.at[first + 128 : first + 256, :], down.at[where, :]),
            ]
    copies = [
        pltpu.make_async_copy(source, target, sem.at[n])
        for n, (source, target) in enumerate(copies)
    ]
    for copy in copies:
        copy.start()
    for copy in copies:
        copy.wait()


def qkvc_assemble_kernel(scal, *refs):
    (here, there), (wq, wk, wv, wc, wo), gains = refs[:2], refs[2:7], refs[7:]
    pieces = [ref.at[k] for ref in (here, there) for k in range(4)]
    size = here.shape[1] - 8
    tails = None
    for k, ref in enumerate(pieces):
        half = jnp.bitwise_xor(scal[1], k >> 2)
        which = jnp.bitwise_xor(scal[2], k & 1)
        first = jnp.bitwise_xor(scal[6], (k >> 1) & 1) * size
        rows = pl.ds(pl.multiple_of(half * 256 + first, size), size)
        lanes = pl.ds(pl.multiple_of(which * 128, 128), 128)
        for w, out in enumerate((wq, wk, wv, wc)):
            out[rows, lanes] = ref[0:size, w * 128 : (w + 1) * 128]
        for b in range(size // 64):
            start = pl.multiple_of(first // 64 * 128 + b * 128, 128)
            out_rows = pl.ds(pl.multiple_of(which * 128 + half * 64, 64), 64)
            wo[out_rows, pl.ds(start, 128)] = ref[b * 64 : (b + 1) * 64, 512:640]
        tail = ref[size : size + 8, 0:512]
        tails = tail if tails is None else tails + tail
    for k, ref in enumerate(gains):
        ref[...] = tails[k : k + 1, :]


def per_device(
    inputs, doc_starts, query_weight, key_weight, value_weight, control_weight, output_weight,
    up_weight, down_weight, first_gain, first_shift, second_gain, second_shift, cotangent,
):
    rows, _, width = inputs.shape
    devices = lax.axis_size("dp")
    place = lax.axis_index("dp").astype(jnp.int32)
    y = lax.axis_index("head").astype(jnp.int32)
    core = place & 1
    pair = (place >> 1) & 1
    one = lambda *v: jnp.stack([jnp.asarray(a, jnp.int32) for a in v])
    depth = (place >> 2) & 1
    bits = [at for at in range(31) if (1 << at) < devices]
    scal = one(y * rows, core, pair, depth * 2 + core, *((place >> at) & 1 for at in bits))
    gain1, shift1 = first_gain.reshape(1, width), first_shift.reshape(1, width)
    gain2, shift2 = second_gain.reshape(1, width), second_shift.reshape(1, width)
    weights = (query_weight, key_weight, value_weight, control_weight)

    def swap_y(a):
        return lax.ppermute(a, "head", [(0, 1), (1, 0)])

    def swap(a, bits):
        return lax.ppermute(a, "dp", [(i, i ^ bits) for i in range(devices)])

    to_second = lambda a: lax.ppermute(a, "head", [(0, 1)])
    to_first = lambda a: lax.ppermute(a, "head", [(1, 0)])

    tables = (scal, doc_starts)
    (piece,) = cut(cut_first_kernel, [(256, 512)], scal, weights, limit=60 * 2**20, near=True)
    qa0 = swap_y(piece)
    normed, proj_own, states_own = run(
        own_kernel,
        [(rows, width), (2, rows, 512), (2, 136, 128)],
        tables,
        (inputs, gain1, shift1) + weights,
        (pltpu.VMEM((4, width, 256), F32), pltpu.SemaphoreType.DMA((4,))),
        after=(piece,),
        far=4,
        us=FRONT,
    )
    carry_oth = to_second(states_own)
    qa0 = tie(qa0, (carry_oth,))
    qb0 = swap(qa0, 1)
    qa1 = swap(qa0, 2)
    (unit,) = cut(
        cut_second_kernel, [(320, 512)], scal, (output_weight, up_weight, down_weight), (qa0,)
    )
    unit0 = swap_y(unit)

    proj_oth0, state0 = run(
        other_kernel, [(rows, 512), (136, 128)], tables, (normed, qa0, qb0),
        after=(unit,), us=FRONT,
    )

    def attend(proj, carry, j, after=()):
        def kernel(scal, starts, proj, carry, o, saved):
            state = carry[own_pair(scal, j - 2)] if j >= 2 else carry[j]
            attention_kernel(scal, starts, proj, state, o, saved, j if j < 2 else None)

        return run(
            kernel, [(rows, 128), (rows, 384)], tables, (proj, carry), after=after, us=FRONT
        )

    qa1 = tie(qa1, (proj_oth0,))
    qb1 = swap(qa1, 1)
    o2, saved2 = attend(proj_oth0, carry_oth, 2, (qa1,))
    unit0 = tie(unit0, (o2,))
    unit1, unit2, unit4 = swap(unit0, 1), swap(unit0, 2), swap(unit0, 4)
    proj_oth1, states_oth = run(
        lambda scal, starts, normed, wa, wb, before, proj, states: other_kernel(
            scal, starts, normed, wa, wb, proj, states, before
        ),
        [(rows, 512), (2, 136, 128)], tables, (normed, qa1, qb1, state0),
        after=(unit0,), us=FRONT,
    )
    carry_own = to_second(states_oth)
    o3, saved3 = attend(proj_oth1, carry_oth, 3, (unit0,))
    o0, saved0 = attend(proj_own, carry_own, 0, (o3,))
    o1, saved1 = attend(proj_own, carry_own, 1, (o0, unit1))
    unit2 = tie(unit2, (o1,))
    unit3, unit6 = swap(unit2, 1), swap(unit2, 4)
    hidden, second, o_all, w_all = run(
        middle_kernel,
        [(rows, width), (rows, width), (rows, 512), (512, width)],
        (scal,),
        (o0, o1, o2, o3, inputs, output_weight, unit0, unit1, unit2, unit3, gain2, shift2),
        after=(spacer(unit2),),
        us=FRONT,
    )
    saved = (saved0, saved1, saved2, saved3)

    def feed_forward(j, unit, other, after=()):
        return run(
            lambda *refs: feed_forward_kernel(j, *refs),
            [(4, 256, 512), (rows, width), (rows, width)],
            (scal,),
            (second, cotangent, up_weight, down_weight, unit, other),
            (pltpu.VMEM((width, 256), F32), pltpu.VMEM((256, width), F32)),
            after=after,
        )

    part1, out1, ds1 = feed_forward(1, unit1, unit3)
    got1 = swap(part1, 1)
    part0, out0, ds0 = feed_forward(0, unit0, unit2, (ds1,))
    unit4, unit6 = tie(unit4, (ds0,)), tie(unit6, (ds0,))
    unit5, unit7 = swap(unit4, 1), swap(unit6, 1)
    def block0(k, part=None):
        return [(part0, k, part), (got1, k, part)]

    def block2(k, part=None):
        return [(part2, k, part), (got3, k, part)]

    u0, d0 = sums([[block0(2)], [block0(1, 1), block0(3, 1)]], scal)
    u0_y = swap_y(u0)
    d0_x = swap(d0, 2)
    part3, out3, ds3 = feed_forward(3, unit5, unit7, (u0,))
    got3 = swap(part3, 1)
    part2, out2, ds2 = feed_forward(2, unit4, unit6, (ds3,))
    u2, z_send, d2 = sums(
        [
            [block2(2)],
            [block0(0) + [(u0_y, None, None)]]
            + [block0(k, 0) + [(d0_x, n, None)] for n, k in enumerate((1, 3))],
            [block2(1, 1), block2(3, 1)],
        ],
        scal, (ds2,), rows=True,
    )
    u2_y = swap_y(u2)
    d2_x = swap(d2, 2)
    z_got = swap(z_send, 4)
    u0_z, d0_z = (0, 256), ((256, 384), (384, 512))
    outputs, d_hidden, grads2, d_o, o_send, o_keep = run(
        middle_back_kernel,
        [inputs.shape, (rows, width), (8, width), (rows, 512), (4, 256, 128), (4, 256, 128)],
        (scal,),
        (hidden, cotangent, ds0, ds1, ds2, ds3, out0, out1, out2, out3, gain2, o_all, w_all),
        (pltpu.VMEM((512, width), F32),),
        after=(u2,),
    )

    def back(js, after=()):
        arrays = (proj_own, proj_oth0, proj_oth1, carry_oth, carry_own, d_o) + saved

        def kernel(scal, starts, own, oth0, oth1, c_oth, c_own, d_o, *rest):
            dproj, dstate = rest[4:]
            for k, j in enumerate(js):
                if j < 2:
                    proj = own.at[own_pair(scal, j)]
                    carry = c_own[j]
                else:
                    proj = (oth0, oth1)[j - 2]
                    carry = c_oth[own_pair(scal, j - 2)]
                dstate[k] = attention_back(
                    scal[0], starts, proj, carry, rest[j], d_o,
                    slice(j * 128, (j + 1) * 128), dproj.at[k],
                )

        return run(
            kernel,
            [(len(js), rows, 512), (len(js), 136, 128)],
            tables,
            arrays,
            after=after,
        )

    def weight_grads(js, dstates, dprojs, after=(), extra=()):
        n = len(js)
        arrays = (proj_own, proj_oth0, proj_oth1, normed, o_send, o_keep)
        arrays += tuple(a for a, _ in dstates) + tuple(a for a, _ in dprojs)
        arrays += tuple(a for a, _ in extra)

        def kernel(scal, starts, own, oth0, oth1, normed, o_send, o_keep, *rest):
            states, grads, rest = rest[:n], rest[n : 2 * n], rest[2 * n :]
            send, keep, final = rest[len(extra) : len(extra) + 3]
            for k, j in enumerate(js):
                here = own.at[own_pair(scal, j)] if j < 2 else (oth0, oth1)[j - 2]
                pair_grads(
                    scal[0], starts, scal[1], here, states[k][dstates[k][1]], normed,
                    grads[k].at[dprojs[k][1]], o_send[j], o_keep[j],
                    send.at[k], keep.at[k], final.at[k],
                )
            if extra:
                value = None
                for ref, (_, lead) in zip(rest, extra):
                    term = ref[lead]
                    value = term if value is None else value + term
                rest[-1][...] = value

        outs = [(n, 256, 640), (n, 256, 640), (n, rows, 512)]
        return run(
            kernel, outs + [(256, 640)] * bool(extra), tables, arrays, after=after, us=LATE
        )

    dproj, dstate = back((1, 3, 0))
    dstate = to_first(dstate)
    up_terms = lambda part: block2(0, part) + [(u2_y, None, part), (z_got, u0_z, part)]
    d2, u2 = sums(
        [
            [block2(3, 0) + [(d2_x, (128, 256), None), (z_got, d0_z[1], None)]],
            [up_terms(1)],
        ],
        scal, (dproj,),
    )
    d2_y = swap_y(d2)
    u2_x = swap(u2, 2)
    send31, keep31, final31 = weight_grads(
        (3, 1), ((dstate, 0), (dstate, 1)), ((dproj, 1), (dproj, 0)), (d2,)
    )
    got31 = swap(send31, 1)
    ff_send, ff_keep = choose(
        up_terms(0) + [(u2_x, None, None)],
        block2(1, 0) + [(d2_x, (0, 128), None), (z_got, d0_z[0], None), (d2_y, None, None)],
        scal, 7, (final31,),
    )
    ff_got = swap(ff_send, 8)
    y_far1, y_near1 = sums(
        [[[(keep31, 0, 3), (got31, 0, 3)]], [[(keep31, 0, 2), (got31, 0, 2)]]], scal, (ff_send,)
    )
    y_far1_got = swap_y(y_far1)
    dproj2, dstate2 = back((2,), (y_far1,))
    dstate2 = to_first(dstate2)
    y_near1_got = swap_y(tie(y_near1, (dproj2,)))
    send2, keep2, final2, own_sum1 = weight_grads(
        (2,), ((dstate, 2),), ((dproj2, 0),), (dproj2,), ((keep31, 1), (got31, 1))
    )
    got2 = swap(send2, 1)
    (ff_shard,) = sums(
        [[[(ff_keep, None, None), (ff_got, None, None)]]], scal, (final2,)
    )
    step = ff_shard
    for at in bits[4:]:
        ff_send, ff_keep = halve([(ff_shard, None)], scal, at + 4, (step,))
        ff_got = swap(ff_send, 1 << at)
        (ff_shard,) = sums(
            [[[(ff_keep, None, None), (ff_got, None, None)]]], scal, (spacer(ff_send),)
        )
        step = ff_shard
    ff_steps = list(reversed(bits[3:]))
    ff_there = swap(ff_shard, 1 << ff_steps[0])
    y_far, x_far = sums(
        [
            [[(keep2, 0, 3), (got2, 0, 3)]],
            [[(own_sum1, None, 3), (y_far1_got, None, None)]],
        ],
        scal, (ff_shard,),
    )
    y_far_got = swap_y(y_far)
    x_far_got = swap(x_far, 2)
    send0, keep0, final0 = weight_grads((0,), ((dstate2, 0),), ((dproj, 2),), (y_far,))
    step = spacer(final0)
    grad_inputs, grads1 = run(
        first_back_kernel,
        [inputs.shape, (8, 640)],
        (scal,),
        (inputs, gain1, d_hidden, final0, final31, final2, qa0, qb0, qa1, qb1, grads2)
        + weights,
        (
            pltpu.VMEM((rows, 1024), F32),
            pltpu.VMEM((rows, width), F32),
            pltpu.VMEM((4, width, 256), F32),
            pltpu.SemaphoreType.DMA((4,)),
        ),
        after=(step,),
        far=4,
        us=LATE,
    )
    step = grads1
    while ff_steps:
        to = ff_steps.pop(0)
        ff_shard = join(ff_shard, ff_there, scal, to + 4, 0, (step,))
        ff_there = swap(ff_shard, 1 << (ff_steps[0] if ff_steps else 2))
        step = spacer(ff_shard)
    got0 = swap(tie(send0, (ff_shard,)), 1)
    q_send, y_near, x_near = sums(
        [
            [[(keep0, 0, 3), (got0, 0, 3), (y_far_got, None, None), (x_far_got, None, None)]],
            [[(keep2, 0, 2), (got2, 0, 2)]],
            [[(own_sum1, None, 2), (y_near1_got, None, None)]],
        ],
        scal, (step,),
    )
    q_got = swap(q_send, 4)
    y_near_got = swap_y(y_near)
    x_near_got = swap(x_near, 2)
    step = spacer(q_send)
    ff_pair, gains = sums(
        [[[(ff_shard, None, None)], [(ff_there, None, None)]], [[(grads1, None, None)]]],
        scal, (step,), rows=True,
    )
    gains_got = swap_y(gains)
    ff_x = swap(ff_pair, 2)
    step = spacer(ff_pair)
    (part,) = sums(
        [
            [
                [
                    (keep0, 0, 2), (got0, 0, 2), (y_near_got, None, None),
                    (x_near_got, None, None), (q_got, None, None),
                ]
            ]
        ],
        scal, (step,),
    )
    part_got = swap(part, 8)
    step = spacer(part)
    (gains,) = sums([[[(gains, None, None), (gains_got, None, None)]]], scal, (step,))
    for at in bits[3:]:
        gains_got = swap(gains, 1 << at)
        step = spacer(gains)
        terms = [
            [(part, None, None), (part_got, None, None)],
            [(gains, None, None), (gains_got, None, None)],
        ]
        if at == bits[-1]:
            (shard,) = sums([terms], scal, (step,), rows=True)
        else:
            part, gains = sums([terms[:1], terms[1:]], scal, (step,))
            part_got = swap(part, 2 << at)
    quarters = [shard] + [swap(shard, 2 * k) for k in (1, 2, 3)]
    ff_x = tie(ff_x, (quarters[2],))
    ff_core, ff_x_core = swap(ff_pair, 1), swap(ff_x, 1)
    grad_up, grad_down, token = run(
        hidden_assemble_kernel,
        [up_weight.shape, down_weight.shape, (8, 128)],
        (scal,),
        (ff_pair, ff_core, ff_x, ff_x_core),
        (pltpu.SemaphoreType.DMA((24,)),),
        after=(spacer(ff_x),),
        away=True,
    )
    (quarters,) = sums([[[(a, None, None)] for a in quarters]], scal, (token,))
    *weight_grad, gain_a, gain_b, gain_c, gain_d = run(
        qkvc_assemble_kernel,
        [w.shape for w in weights] + [output_weight.shape] + [(1, width)] * 4,
        (scal,),
        (quarters, swap(quarters, 1)),
        after=(spacer(quarters),),
    )
    return (
        outputs, grad_inputs,
        *weight_grad, grad_up, grad_down,
        gain_a[0], gain_b[0], gain_c[0], gain_d[0],
    )


def solution(mesh):
    rows = P("head", "dp", None)
    cols = P(None, "head")
    tall = P("head", None)
    flat = P()
    return jax.shard_map(
        per_device,
        mesh=mesh,
        in_specs=(
            rows, P("dp", None), cols, cols, cols, cols, tall, cols, tall,
            flat, flat, flat, flat, rows,
        ),
        out_specs=(
            rows, rows, cols, cols, cols, cols, tall, cols, tall, flat, flat, flat, flat,
        ),
        check_vma=False,
    )
```

```python
import jax
import jax.numpy as jnp
from jax import lax
from jax.experimental import pallas as pl
from jax.experimental.pallas import tpu as pltpu
from jax.sharding import PartitionSpec as P

F32 = jnp.float32
HIGH = lax.Precision.HIGH
CHUNK = 256
EPS = 1e-05
GELU_C = 0.7978845608028654
GELU_K = 0.044715
VMEM_LIMIT = 16 * 2**20


def dot(left, right, dims):
    return lax.dot_general(
        left, right, (dims, ((), ())), precision=HIGH, preferred_element_type=F32
    )


def nn(left, right):
    return dot(left, right, ((1,), (0,)))


def nt(left, right):
    return dot(left, right, ((1,), (1,)))


def tn(left, right):
    return dot(left, right, ((0,), (0,)))


def whole():
    return pl.BlockSpec(memory_space=pltpu.VMEM)


def anywhere():
    return pl.BlockSpec(memory_space=pl.ANY)


def distant():
    return pl.BlockSpec(memory_space=pltpu.HBM)


def scalars():
    return pl.BlockSpec(memory_space=pltpu.SMEM)


FRONT, HEAVY, LATE, SUM = 20.0, 20.0, 20.0, 20.0


def cost(us):
    return pl.CostEstimate(flops=int(us * 1153e6), bytes_accessed=0, transcendentals=0)


def run(kernel, outs, scal, arrays, scratch=(), after=(), far=0, us=HEAVY, away=False):
    out_shape = [jax.ShapeDtypeStruct(shape, F32) for shape in outs]
    first, last = len(scal) + len(arrays), len(scal) + len(arrays) + len(after)
    return pl.pallas_call(
        lambda *refs: kernel(*refs[:first], *refs[last:]),
        out_shape=out_shape,
        in_specs=[scalars()] * len(scal)
        + [whole()] * (len(arrays) - far)
        + [distant()] * far
        + [anywhere()] * len(after),
        out_specs=[anywhere() if away else whole()] * len(outs),
        scratch_shapes=list(scratch),
        compiler_params=pltpu.CompilerParams(vmem_limit_bytes=VMEM_LIMIT),
        cost_estimate=cost(us),
    )(*scal, *arrays, *after)


def tie(array, after):
    count = 1 + len(after)
    return pl.pallas_call(
        lambda *refs: None,
        out_shape=jax.ShapeDtypeStruct(array.shape, F32),
        in_specs=[anywhere()] * count,
        out_specs=anywhere(),
        input_output_aliases={0: 0},
        compiler_params=pltpu.CompilerParams(vmem_limit_bytes=2**20),
        cost_estimate=pl.CostEstimate(flops=0, bytes_accessed=0, transcendentals=0),
    )(array, *after)


def spacer(*after):
    return pl.pallas_call(
        lambda *refs: None,
        out_shape=jax.ShapeDtypeStruct((8, 128), F32),
        in_specs=[anywhere()] * len(after),
        out_specs=anywhere(),
        compiler_params=pltpu.CompilerParams(vmem_limit_bytes=2**20),
        cost_estimate=cost(HEAVY),
    )(*after)


def lane_slice(ref, index, width):
    return ref[:, pl.ds(pl.multiple_of(index * width, width), width)]


def normalize(x):
    centre = x - jnp.mean(x, axis=-1, keepdims=True)
    spread = jnp.mean(centre * centre, axis=-1, keepdims=True)
    r = lax.rsqrt(spread + EPS)
    return centre * r, r


def norm_back(dy, nhat, r, gain):
    dyg = dy * gain
    first = jnp.mean(dyg, axis=-1, keepdims=True)
    second = jnp.mean(dyg * nhat, axis=-1, keepdims=True)
    return r * (dyg - first - nhat * second)


def doc_of(starts, position):
    total = jnp.zeros(jnp.shape(position), jnp.int32)
    for k in range(starts.shape[1]):
        total = total + (position >= starts[0, k]).astype(jnp.int32)
    return total


def column(first, count):
    return first + lax.broadcasted_iota(jnp.int32, (count, 1), 0)


def left_lanes():
    return lax.broadcasted_iota(jnp.int32, (1, 128), 1) < 64


def pack_state(mk, mv, z):
    left = left_lanes()
    return jnp.concatenate(
        [
            jnp.where(left, mk[0:64], mk[64:128]),
            jnp.where(left, mv[0:64], mv[64:128]),
            jnp.broadcast_to(z, (8, 128)),
        ],
        axis=0,
    )


def blocks_only(m):
    diagonal = (lax.broadcasted_iota(jnp.int32, (128, 128), 0) < 64) == (
        lax.broadcasted_iota(jnp.int32, (128, 128), 1) < 64
    )
    return jnp.where(diagonal, m, 0.0)


def unpack_state(state):
    mk = state[0:64]
    mv = state[64:128]
    return (
        blocks_only(jnp.concatenate([mk, mk], axis=0)),
        blocks_only(jnp.concatenate([mv, mv], axis=0)),
        state[128:129],
    )


def end_state(k2, v2, e2, starts, first):
    count = k2.shape[0]
    kept = (doc_of(starts, column(first, count)) == doc_of(starts, first + count - 1)).astype(F32)
    em = e2 * kept
    return pack_state(outer(k2, em), outer(em, v2), jnp.sum(em, axis=0, keepdims=True))


def cut_first_kernel(scal, wq, wk, wv, wc, piece, sems):
    rows = pl.ds(pl.multiple_of(scal[1] * 256, 256), 256)
    lanes = pl.ds(pl.multiple_of(scal[2] * 128, 128), 128)
    copies = [
        pltpu.make_async_copy(
            ref.at[rows, lanes], piece.at[:, w * 128 : (w + 1) * 128], sems.at[w]
        )
        for w, ref in enumerate((wq, wk, wv, wc))
    ]
    for copy in copies:
        copy.start()
    for copy in copies:
        copy.wait()


def cut_second_kernel(scal, wo, up, down, piece, sems):
    unit = pl.ds(pl.multiple_of(scal[3] * 256 + scal[2] * 128, 128), 128)
    thin = pl.ds(pl.multiple_of((scal[2] * 2 + scal[1]) * 64, 64), 64)
    copies = [
        pltpu.make_async_copy(
            up.at[b * 128 : (b + 1) * 128, unit], piece.at[0:128, b * 128 : (b + 1) * 128],
            sems.at[b],
        )
        for b in range(4)
    ]
    copies.append(pltpu.make_async_copy(down.at[unit, :], piece.at[128:256, :], sems.at[4]))
    copies.append(pltpu.make_async_copy(wo.at[thin, :], piece.at[256:320, :], sems.at[5]))
    for copy in copies:
        copy.start()
    for copy in copies:
        copy.wait()


def cut(kernel, shapes, scal, arrays, after=(), limit=2**20, near=False):
    first, last = 1 + len(arrays), 1 + len(arrays) + len(after)
    out_shape = [jax.ShapeDtypeStruct(shape, F32) for shape in shapes]
    return pl.pallas_call(
        lambda *refs: kernel(*refs[:first], *refs[last:]),
        out_shape=out_shape,
        in_specs=[scalars()] + [distant()] * len(arrays) + [anywhere()] * len(after),
        out_specs=[whole() if near else anywhere()] * len(shapes),
        scratch_shapes=[pltpu.SemaphoreType.DMA((6,))],
        compiler_params=pltpu.CompilerParams(vmem_limit_bytes=limit),
        cost_estimate=cost(FRONT),
    )(scal, *arrays, *after)


def own_kernel(scal, starts, x, gain, shift, wq, wk, wv, wc, normed, proj, states, held, sems):
    copies = [
        pltpu.make_async_copy(ref, held.at[w], sems.at[w])
        for w, ref in enumerate((wq, wk, wv, wc))
    ]
    for copy in copies:
        copy.start()
    nhat, _ = normalize(x[:, 0, :])
    n = nhat * gain[...] + shift[...]
    normed[...] = n
    for w, copy in enumerate(copies):
        copy.wait()
        full = nn(n, held[w])
        if w == 3:
            full = jnp.exp(full)
        for p in range(2):
            proj[p, :, w * 128 : (w + 1) * 128] = full[:, p * 128 : (p + 1) * 128]
    for p in range(2):
        states[p] = end_state(
            proj[p, :, 128:256], proj[p, :, 256:384], proj[p, :, 384:512], starts, scal[0]
        )


def other_kernel(scal, starts, normed, wa, wb, proj, states, before=None):
    core = scal[1]
    full = nn(lane_slice(normed, core, 256), wa[...]) + nn(
        lane_slice(normed, 1 - core, 256), wb[...]
    )
    proj[:, 0:384] = full[:, 0:384]
    proj[:, 384:512] = jnp.exp(full[:, 384:512])
    state = end_state(proj[:, 128:256], proj[:, 256:384], proj[:, 384:512], starts, scal[0])
    if before is None:
        states[...] = state
    else:
        states[0] = before[...]
        states[1] = state


def chunk_masks(starts, first, c):
    begin = first + c * CHUNK
    position = column(begin, CHUNK)
    docs = doc_of(starts, position)
    row = begin + lax.broadcasted_iota(jnp.int32, (1, CHUNK), 1)
    mask = (position >= row) & (docs == doc_of(starts, row))
    before = doc_of(starts, begin - 1)
    last = doc_of(starts, begin + CHUNK - 1)
    entering = (docs == before).astype(F32)
    leaving = (docs == last).astype(F32)
    passing = (before == last).astype(F32)
    return mask, entering, leaving, passing


BF16 = jnp.bfloat16


def raw(left, right, dims):
    return lax.dot_general(left, right, (dims, ((), ())), preferred_element_type=F32)


def rest_of(x):
    return x - x.astype(BF16).astype(F32)


def turn(x):
    return pltpu.roll(x, 64, 1)


def beside(a, b):
    return jnp.concatenate([a, b], axis=1).astype(BF16)


def rows_factor(x):
    left = left_lanes()
    low = turn(rest_of(x))
    return (
        beside(jnp.where(left, x, low), jnp.where(left, x, 0.0)),
        beside(jnp.where(left, low, x), jnp.where(left, 0.0, x)),
    )


def columns_factor(x):
    left = left_lanes()
    other = turn(x)
    low = rest_of(x)
    return (
        beside(jnp.where(left, x, other), low),
        beside(jnp.where(left, other, x), low),
    )


def affinity_of(rows, columns, mask):
    result = []
    for r, c in zip(rows, columns):
        value = jnp.where(mask, raw(r, c, ((1,), (1,))), 0.0)
        high = value.astype(BF16)
        result.append((high, (value - high.astype(F32)).astype(BF16)))
    return result


def narrow(x):
    left = left_lanes()
    low = rest_of(x)
    return (
        jnp.where(left, x, turn(low)).astype(BF16),
        jnp.where(left, turn(low), x).astype(BF16),
    )


def gather_heads(first, second):
    left = left_lanes()
    return jnp.where(left, first, second) + turn(jnp.where(left, second, first))


def spread(matrices, x):
    outs = []
    for (high, low), part in zip(matrices, x):
        outs.append(raw(high, part, ((1,), (0,))) + raw(low, part, ((1,), (0,))))
    return gather_heads(*outs)


def spread_back(matrices, x):
    outs = []
    for (high, low), part in zip(matrices, x):
        outs.append(raw(high, part, ((0,), (0,))) + raw(low, part, ((0,), (0,))))
    return gather_heads(*outs)


def fold(x):
    return x[:, 0:128] + x[:, 128:256]


def both_parts(x):
    return beside(x, rest_of(x))


def masked_sum(mask, x):
    return fold(raw(mask, both_parts(x), ((1,), (0,))))


def masked_sum_back(mask, x):
    return fold(raw(mask, both_parts(x), ((0,), (0,))))


def times_state(x, m):
    part = both_parts(m)
    return fold(raw(both_parts(x), jnp.concatenate([part, part], axis=0), ((1,), (0,))))


def times_state_back(x, m):
    low = rest_of(m)
    right = jnp.concatenate([beside(m, m), beside(low, low)], axis=0)
    return fold(raw(both_parts(x), right, ((1,), (1,))))


def outer(x, y):
    full = raw(both_parts(x), both_parts(y), ((0,), (0,)))
    return blocks_only(fold(full[0:128] + full[128:256]))


def slot_sums(x):
    left = left_lanes()
    return jnp.where(
        left,
        jnp.sum(jnp.where(left, x, 0.0), axis=1, keepdims=True),
        jnp.sum(jnp.where(left, 0.0, x), axis=1, keepdims=True),
    )


def next_state(k2, v2, e2, state, leaving, passing):
    mk, mv, z_in = state
    em = e2 * leaving
    return (
        outer(k2, em) + passing * mk,
        outer(em, v2) + passing * mv,
        jnp.sum(em, axis=0, keepdims=True) + passing * z_in,
    )


def attention(first, starts, proj, carry, o, lanes, saved):
    left = left_lanes()
    state = unpack_state(carry)
    chunks = proj.shape[0] // CHUNK
    for c in range(chunks):
        rows = slice(c * CHUNK, (c + 1) * CHUNK)
        q2, k2 = proj[rows, 0:128], proj[rows, 128:256]
        v2, e2 = proj[rows, 256:384], proj[rows, 384:512]
        mask, entering, leaving, passing = chunk_masks(starts, first, c)
        mk, mv, z_in = state
        z = masked_sum(mask.astype(F32).astype(BF16), e2) + entering * z_in
        affinity = affinity_of(rows_factor(q2), columns_factor(k2), mask)
        total = spread(affinity, narrow(e2)) + entering * times_state(q2, mk)
        s = total / z * 0.125
        top = jnp.where(
            left,
            jnp.max(jnp.where(left, s, -jnp.inf), axis=1, keepdims=True),
            jnp.max(jnp.where(left, -jnp.inf, s), axis=1, keepdims=True),
        )
        p = jnp.exp(s - top)
        p = p / slot_sums(p)
        r = p / z
        mixing = affinity_of(rows_factor(r), columns_factor(e2), mask)
        o[rows, lanes] = spread(mixing, narrow(v2)) + entering * times_state(r, mv)
        saved[rows, 0:128] = z
        saved[rows, 128:256] = s
        saved[rows, 256:384] = p
        if c + 1 < chunks:
            state = next_state(k2, v2, e2, state, leaving, passing)


def attention_back(first, starts, proj, carry, saved, d_o, lanes, dproj):
    chunks = proj.shape[0] // CHUNK
    states = [unpack_state(carry)]
    for c in range(chunks - 1):
        rows = slice(c * CHUNK, (c + 1) * CHUNK)
        _, _, leaving, passing = chunk_masks(starts, first, c)
        states.append(
            next_state(
                proj[rows, 128:256], proj[rows, 256:384], proj[rows, 384:512], states[c],
                leaving, passing,
            )
        )
    ahead = None
    for c in reversed(range(chunks)):
        rows = slice(c * CHUNK, (c + 1) * CHUNK)
        q2, k2 = proj[rows, 0:128], proj[rows, 128:256]
        v2, e2 = proj[rows, 256:384], proj[rows, 384:512]
        z, s, p = saved[rows, 0:128], saved[rows, 128:256], saved[rows, 256:384]
        do2 = d_o[rows, lanes]
        mask, entering, leaving, passing = chunk_masks(starts, first, c)
        mk, mv, _ = states[c]
        r = p / z
        do_in = entering * do2
        e_columns, e_narrow = columns_factor(e2), narrow(e2)
        mixing = affinity_of(rows_factor(r), e_columns, mask)
        d_mixing = affinity_of(rows_factor(do2), columns_factor(v2), mask)
        dv = spread_back(mixing, narrow(do2))
        dr = spread(d_mixing, e_narrow) + times_state_back(do_in, mv)
        de = spread_back(d_mixing, narrow(r))
        dp = dr / z
        dz = -dp * r
        ds = p * (dp - slot_sums(p * dp)) / z
        w = ds * 0.125
        dz = dz - ds * s
        w_in = entering * w
        affinity = affinity_of(rows_factor(q2), columns_factor(k2), mask)
        d_affinity = affinity_of(rows_factor(w), e_columns, mask)
        dq = spread(d_affinity, narrow(k2)) + times_state_back(w_in, mk)
        dk = spread_back(d_affinity, narrow(q2))
        de = de + spread_back(affinity, narrow(w))
        de = de + masked_sum_back(mask.astype(F32).astype(BF16), dz)
        if ahead is not None:
            dmk, dmv, dz_out = ahead
            em = e2 * leaving
            dv = dv + times_state(em, dmv)
            dk = dk + times_state_back(em, dmk)
            de = de + leaving * (times_state(k2, dmk) + times_state_back(v2, dmv) + dz_out)
        dproj[rows, 0:128] = dq
        dproj[rows, 128:256] = dk
        dproj[rows, 256:384] = dv
        dproj[rows, 384:512] = de
        now = (
            outer(q2, w_in),
            outer(r, do_in),
            jnp.sum(entering * dz, axis=0, keepdims=True),
        )
        if ahead is not None:
            now = tuple(a + passing * b for a, b in zip(now, ahead))
        ahead = now
    return pack_state(*ahead)


def own_pair(scal, j):
    return jnp.bitwise_xor(scal[2], j)


def attention_kernel(scal, starts, proj, carry, o, saved, j=None):
    here = proj if j is None else proj.at[own_pair(scal, j)]
    attention(scal[0], starts, here, carry, o, slice(0, 128), saved)


def middle_kernel(
    scal, o0, o1, o2, o3, x, wo, w0, w1, w2, w3, gain, shift, hidden, second, o_all, w_all,
):
    for j, ref in enumerate((o0, o1, o2, o3)):
        o_all[:, j * 128 : (j + 1) * 128] = ref[...]
    for j in range(2):
        which = pl.multiple_of(own_pair(scal, j) * 128, 128)
        w_all[j * 128 : (j + 1) * 128, :] = wo[pl.ds(which, 128), :]
    for k, ref in enumerate((w0, w1, w2, w3)):
        start = 256 + (k >> 1) * 128 + jnp.bitwise_xor(scal[1], k & 1) * 64
        w_all[pl.ds(pl.multiple_of(start, 64), 64), :] = ref[256:320, :]
    h = x[:, 0, :] + nn(o_all[...], w_all[...])
    hidden[...] = h
    nhat, _ = normalize(h)
    second[...] = nhat * gain[...] + shift[...]


def middle_back_kernel(
    scal, hidden, cot, ds0, ds1, ds2, ds3, u0, u1, u2, u3, gain, o_all, w_all,
    outputs, d_hidden, grads, d_o, send, keep, work,
):
    core = scal[1]
    outputs[:, 0, :] = hidden[...] + ((u0[...] + u1[...]) + (u2[...] + u3[...]))
    d_second = (ds0[...] + ds1[...]) + (ds2[...] + ds3[...])
    nhat, r = normalize(hidden[...])
    grads[0:1, :] = jnp.sum(d_second * nhat, axis=0, keepdims=True)
    grads[1:2, :] = jnp.sum(d_second, axis=0, keepdims=True)
    grads[2:8, :] = jnp.zeros((6, grads.shape[1]), F32)
    d = cot[:, 0, :] + norm_back(d_second, nhat, r, gain[...])
    d_hidden[...] = d
    d_o[...] = nt(d, w_all[...])
    work[...] = tn(o_all[...], d)
    for ref, which in ((send, 1 - core), (keep, core)):
        for j in range(4):
            rows = pl.ds(pl.multiple_of(j * 128 + which * 64, 64), 64)
            for b in range(4):
                ref[j, b * 64 : (b + 1) * 64, :] = work[rows, b * 128 : (b + 1) * 128]


def feed_forward_kernel(j, scal, second, cot, up, down, unit, other, packed, out, ds, up_far, down_far):
    where = pl.ds(pl.multiple_of(jnp.bitwise_xor(scal[3], j) * 256, 256), 256)
    for ref, half in ((unit, scal[2]), (other, 1 - scal[2])):
        place = pl.ds(pl.multiple_of(half * 128, 128), 128)
        for b in range(4):
            up_far[b * 128 : (b + 1) * 128, place] = ref[0:128, b * 128 : (b + 1) * 128]
        down_far[place, :] = ref[128:256, :]
    n_left, n_right = second[:, 0:256], second[:, 256:512]
    g = cot[:, 0, :]
    for half in range(2):
        if half == 0:
            up_left, up_right = up[0:256, where], up[256:512, where]
            down_block = down[where, :]
        else:
            up_left, up_right = up_far[0:256, :], up_far[256:512, :]
            down_block = down_far[...]
        u = nn(n_left, up_left) + nn(n_right, up_right)
        inner = GELU_C * (u + GELU_K * u * u * u)
        t = jnp.tanh(inner)
        act = 0.5 * u * (1.0 + t)
        slope = 0.5 * (1.0 + t) + 0.5 * u * (1.0 - t * t) * (
            GELU_C * (1.0 + 3.0 * GELU_K * u * u)
        )
        du = nt(g, down_block) * slope
        packed[2 * half, :, 0:256] = tn(n_left, du)
        packed[2 * half, :, 256:512] = tn(n_right, du)
        packed[2 * half + 1] = tn(act, g)
        out_part = nn(act, down_block)
        ds_left, ds_right = nt(du, up_left), nt(du, up_right)
        if half == 0:
            out[...] = out_part
            ds[:, 0:256] = ds_left
            ds[:, 256:512] = ds_right
        else:
            out[...] = out[...] + out_part
            ds[:, 0:256] = ds[:, 0:256] + ds_left
            ds[:, 256:512] = ds[:, 256:512] + ds_right


def pair_grads(first, starts, core, proj, dstate, normed, dproj, o_send, o_keep, send, keep, final):
    k2, v2, e2 = proj[:, 128:256], proj[:, 256:384], proj[:, 384:512]
    count = k2.shape[0]
    dmk, dmv, dz_out = unpack_state(dstate)
    leaving = (
        doc_of(starts, column(first, count)) == doc_of(starts, first + count - 1)
    ).astype(F32)
    em = e2 * leaving
    final[:, 0:128] = dproj[:, 0:128]
    final[:, 128:256] = dproj[:, 128:256] + times_state_back(em, dmk)
    final[:, 256:384] = dproj[:, 256:384] + times_state(em, dmv)
    de = dproj[:, 384:512] + leaving * (
        times_state(k2, dmk) + times_state_back(v2, dmv) + dz_out
    )
    final[:, 384:512] = e2 * de
    send[:, 0:512] = tn(lane_slice(normed, 1 - core, 256), final[...])
    keep[:, 0:512] = tn(lane_slice(normed, core, 256), final[...])
    send[:, 512:640] = o_send
    keep[:, 512:640] = o_keep


def first_back_kernel(
    scal, x, gain, d_hidden, f0, f31, f2, a0, b0, a1, b1, grads2, wq, wk, wv, wc,
    grad_x, grads, cat, acc, held, sems,
):
    core, pair = scal[1], scal[2]
    copies = [
        pltpu.make_async_copy(ref, held.at[w], sems.at[w])
        for w, ref in enumerate((wq, wk, wv, wc))
    ]
    for copy in copies:
        copy.start()
    for j, ref in enumerate((f0.at[0], f31.at[1])):
        which = jnp.bitwise_xor(pair, j)
        for w in range(4):
            start = pl.multiple_of(w * 256 + which * 128, 128)
            cat[:, pl.ds(start, 128)] = ref[:, w * 128 : (w + 1) * 128]
    total = None
    for w, copy in enumerate(copies):
        copy.wait()
        part = nt(cat[:, w * 256 : (w + 1) * 256], held[w])
        total = part if total is None else total + part
    acc[...] = total
    for which, refs in ((core, (a0, a1)), (1 - core, (b0, b1))):
        part = nt(f2[0], refs[0][...]) + nt(f31[0], refs[1][...])
        lanes = pl.ds(pl.multiple_of(which * 256, 256), 256)
        acc[:, lanes] = acc[:, lanes] + part
    d_normed = acc[...]
    nhat, r = normalize(x[:, 0, :])
    grads[...] = jnp.zeros(grads.shape, F32)
    grads[0:1, 0:512] = jnp.sum(d_normed * nhat, axis=0, keepdims=True)
    grads[1:2, 0:512] = jnp.sum(d_normed, axis=0, keepdims=True)
    grads[2:4, 0:512] = grads2[0:2, :]
    grad_x[:, 0, :] = d_hidden[...] + norm_back(d_normed, nhat, r, gain[...])


def table_of(groups):
    arrays, places = [], []
    for group in groups:
        places.append([])
        for array, lead, part in group:
            at = next((i for i, a in enumerate(arrays) if a is array), None)
            if at is None:
                at = len(arrays)
                arrays.append(array)
            places[-1].append((at, lead, part))
    return arrays, places


def total(scal, refs, place):
    value = None
    for at, lead, part in place:
        if isinstance(lead, tuple):
            ref = refs[at].at[lead[0] : lead[1], :]
        else:
            ref = refs[at] if lead is None else refs[at].at[lead]
        if part is None:
            term = ref[...]
        else:
            rows = ref.shape[0] // 2
            which = jnp.bitwise_xor(scal[2 if part < 2 else 6], part & 1) * rows
            term = ref[pl.ds(pl.multiple_of(which, rows), rows), :]
        value = term if value is None else value + term
    return value


def shape_of(group):
    array, lead, part = group[0]
    rows, cols = array.shape[-2:]
    if isinstance(lead, tuple):
        rows = lead[1] - lead[0]
    return (rows if part is None else rows // 2, cols)


def sums(outs, scal, after=(), rows=False):
    arrays, places = table_of([group for out in outs for group in out])
    shapes = []
    for out in outs:
        h, w = shape_of(out[0])
        if rows:
            shapes.append((sum(shape_of(g)[0] for g in out), w))
        else:
            shapes.append((h, w) if len(out) == 1 else (len(out), h, w))

    def kernel(scal, *refs):
        at = 0
        for n, out in enumerate(outs):
            target = refs[len(arrays) + n]
            row = 0
            for k in range(len(out)):
                value = total(scal, refs, places[at])
                at += 1
                if rows:
                    target[row : row + value.shape[0], :] = value
                    row += value.shape[0]
                elif len(out) == 1:
                    target[...] = value
                else:
                    target[k] = value

    return run(kernel, shapes, (scal,), arrays, after=after, us=SUM)


def choose(first, second, scal, at, after=()):
    arrays, places = table_of([first, second])

    def kernel(scal, *refs):
        values = [total(scal, refs, place) for place in places]
        for side in range(2):

            @pl.when(scal[at] == side)
            def _():
                refs[-2][...] = values[1 - side]
                refs[-1][...] = values[side]

    return run(kernel, [shape_of(first)] * 2, (scal,), arrays, after=after, us=SUM)


def halve(terms, scal, at, after=()):
    rows, cols = terms[0][0].shape[-2:]
    rows //= 2
    leads = [lead for _, lead in terms]

    def kernel(scal, *refs):
        for out, which in ((refs[-2], 1 - scal[at]), (refs[-1], scal[at])):
            block = pl.ds(pl.multiple_of(which * rows, rows), rows)
            value = None
            for ref, lead in zip(refs, leads):
                term = ref[block, :] if lead is None else ref[lead, block, :]
                value = term if value is None else value + term
            out[...] = value

    return run(
        kernel, [(rows, cols)] * 2, (scal,), [a for a, _ in terms], after=after, us=SUM
    )


def join(here, there, scal, at, tail=8, after=()):
    rows, cols = here.shape
    rows -= tail

    def kernel(scal, here, there, out):
        for ref, which in ((here, scal[at]), (there, 1 - scal[at])):
            block = pl.ds(pl.multiple_of(which * rows, rows), rows)
            out[block, :] = ref[0:rows, :]
        if tail:
            out[2 * rows :, :] = here[rows:, :] + there[rows:, :]

    return run(kernel, [(2 * rows + tail, cols)], (scal,), (here, there), after=after, us=SUM)[0]


def hidden_assemble_kernel(scal, *refs):
    pieces, (up, down, token, sem) = refs[:8], refs[8:]
    copies = []
    for c in range(2):
        for k in range(2):
            ups, downs = pieces[4 * c + k], pieces[4 * c + 2 + k]
            for n in range(2):
                rows = slice(n * 128, n * 128 + 128)
                half = jnp.bitwise_xor(scal[2], k) * 128
                block = jnp.bitwise_xor(scal[3], c + 2 - 2 * n)
                lanes = pl.ds(pl.multiple_of(block * 256, 256), 256)
                upper = pl.ds(pl.multiple_of(half, 128), 128)
                lower = pl.ds(pl.multiple_of(half + 256, 128), 128)
                half = jnp.bitwise_xor(scal[2], n) * 128
                block = jnp.bitwise_xor(scal[3], c + 2 - 2 * k)
                where = pl.ds(pl.multiple_of(block * 256 + half, 128), 128)
                copies += [
                    (ups.at[rows, 0:256], up.at[upper, lanes]),
                    (ups.at[rows, 256:512], up.at[lower, lanes]),
                    (downs.at[rows, :], down.at[where, :]),
                ]
    copies = [
        pltpu.make_async_copy(source, target, sem.at[n])
        for n, (source, target) in enumerate(copies)
    ]
    for copy in copies:
        copy.start()
    for copy in copies:
        copy.wait()


def qkvc_assemble_kernel(scal, *refs):
    (here, there), (wq, wk, wv, wc, wo), gains = refs[:2], refs[2:7], refs[7:]
    pieces = [ref.at[k] for ref in (here, there) for k in range(4)]
    size = here.shape[1] - 8
    tails = None
    for k, ref in enumerate(pieces):
        half = jnp.bitwise_xor(scal[1], k >> 2)
        which = jnp.bitwise_xor(scal[2], k & 1)
        first = jnp.bitwise_xor(scal[6], (k >> 1) & 1) * size
        rows = pl.ds(pl.multiple_of(half * 256 + first, size), size)
        lanes = pl.ds(pl.multiple_of(which * 128, 128), 128)
        for w, out in enumerate((wq, wk, wv, wc)):
            out[rows, lanes] = ref[0:size, w * 128 : (w + 1) * 128]
        for b in range(size // 64):
            start = pl.multiple_of(first // 64 * 128 + b * 128, 128)
            out_rows = pl.ds(pl.multiple_of(which * 128 + half * 64, 64), 64)
            wo[out_rows, pl.ds(start, 128)] = ref[b * 64 : (b + 1) * 64, 512:640]
        tail = ref[size : size + 8, 0:512]
        tails = tail if tails is None else tails + tail
    for k, ref in enumerate(gains):
        ref[...] = tails[k : k + 1, :]


def per_device(
    inputs, doc_starts, query_weight, key_weight, value_weight, control_weight, output_weight,
    up_weight, down_weight, first_gain, first_shift, second_gain, second_shift, cotangent,
):
    rows, _, width = inputs.shape
    devices = lax.axis_size("dp")
    place = lax.axis_index("dp").astype(jnp.int32)
    y = lax.axis_index("head").astype(jnp.int32)
    core = place & 1
    pair = (place >> 1) & 1
    one = lambda *v: jnp.stack([jnp.asarray(a, jnp.int32) for a in v])
    depth = (place >> 2) & 1
    bits = [at for at in range(31) if (1 << at) < devices]
    scal = one(y * rows, core, pair, depth * 2 + core, *((place >> at) & 1 for at in bits))
    gain1, shift1 = first_gain.reshape(1, width), first_shift.reshape(1, width)
    gain2, shift2 = second_gain.reshape(1, width), second_shift.reshape(1, width)
    weights = (query_weight, key_weight, value_weight, control_weight)

    def swap_y(a):
        return lax.ppermute(a, "head", [(0, 1), (1, 0)])

    def swap(a, bits):
        return lax.ppermute(a, "dp", [(i, i ^ bits) for i in range(devices)])

    to_second = lambda a: lax.ppermute(a, "head", [(0, 1)])
    to_first = lambda a: lax.ppermute(a, "head", [(1, 0)])

    tables = (scal, doc_starts)
    (piece,) = cut(cut_first_kernel, [(256, 512)], scal, weights, limit=60 * 2**20, near=True)
    qa0 = swap_y(piece)
    normed, proj_own, states_own = run(
        own_kernel,
        [(rows, width), (2, rows, 512), (2, 136, 128)],
        tables,
        (inputs, gain1, shift1) + weights,
        (pltpu.VMEM((4, width, 256), F32), pltpu.SemaphoreType.DMA((4,))),
        after=(piece,),
        far=4,
        us=FRONT,
    )
    carry_oth = to_second(states_own)
    qa0 = tie(qa0, (carry_oth,))
    qb0 = swap(qa0, 1)
    qa1 = swap(qa0, 2)
    (unit,) = cut(
        cut_second_kernel, [(320, 512)], scal, (output_weight, up_weight, down_weight), (qa0,)
    )
    unit0 = swap_y(unit)

    proj_oth0, state0 = run(
        other_kernel, [(rows, 512), (136, 128)], tables, (normed, qa0, qb0),
        after=(unit,), us=FRONT,
    )

    def attend(proj, carry, j, after=()):
        def kernel(scal, starts, proj, carry, o, saved):
            state = carry[own_pair(scal, j - 2)] if j >= 2 else carry[j]
            attention_kernel(scal, starts, proj, state, o, saved, j if j < 2 else None)

        return run(
            kernel, [(rows, 128), (rows, 384)], tables, (proj, carry), after=after, us=FRONT
        )

    qa1 = tie(qa1, (proj_oth0,))
    qb1 = swap(qa1, 1)
    o2, saved2 = attend(proj_oth0, carry_oth, 2, (qa1,))
    unit0 = tie(unit0, (o2,))
    unit1, unit2, unit4 = swap(unit0, 1), swap(unit0, 2), swap(unit0, 4)
    proj_oth1, states_oth = run(
        lambda scal, starts, normed, wa, wb, before, proj, states: other_kernel(
            scal, starts, normed, wa, wb, proj, states, before
        ),
        [(rows, 512), (2, 136, 128)], tables, (normed, qa1, qb1, state0),
        after=(unit0,), us=FRONT,
    )
    carry_own = to_second(states_oth)
    o3, saved3 = attend(proj_oth1, carry_oth, 3, (unit0,))
    o0, saved0 = attend(proj_own, carry_own, 0, (o3,))
    o1, saved1 = attend(proj_own, carry_own, 1, (o0, unit1))
    unit2 = tie(unit2, (o1,))
    unit3, unit6 = swap(unit2, 1), swap(unit2, 4)
    hidden, second, o_all, w_all = run(
        middle_kernel,
        [(rows, width), (rows, width), (rows, 512), (512, width)],
        (scal,),
        (o0, o1, o2, o3, inputs, output_weight, unit0, unit1, unit2, unit3, gain2, shift2),
        after=(spacer(unit2),),
        us=FRONT,
    )
    saved = (saved0, saved1, saved2, saved3)

    def feed_forward(j, unit, other, after=()):
        return run(
            lambda *refs: feed_forward_kernel(j, *refs),
            [(4, 256, 512), (rows, width), (rows, width)],
            (scal,),
            (second, cotangent, up_weight, down_weight, unit, other),
            (pltpu.VMEM((width, 256), F32), pltpu.VMEM((256, width), F32)),
            after=after,
        )

    part1, out1, ds1 = feed_forward(1, unit1, unit3)
    got1 = swap(part1, 1)
    part0, out0, ds0 = feed_forward(0, unit0, unit2, (ds1,))
    unit4, unit6 = tie(unit4, (ds0,)), tie(unit6, (ds0,))
    unit5, unit7 = swap(unit4, 1), swap(unit6, 1)
    def block0(k, part=None):
        return [(part0, k, part), (got1, k, part)]

    def block2(k, part=None):
        return [(part2, k, part), (got3, k, part)]

    u0, d0 = sums([[block0(2)], [block0(1, 1), block0(3, 1)]], scal)
    u0_y = swap_y(u0)
    d0_x = swap(d0, 2)
    part3, out3, ds3 = feed_forward(3, unit5, unit7, (u0,))
    got3 = swap(part3, 1)
    part2, out2, ds2 = feed_forward(2, unit4, unit6, (ds3,))
    u2, z_send, d2 = sums(
        [
            [block2(2)],
            [block0(0) + [(u0_y, None, None)]]
            + [block0(k, 0) + [(d0_x, n, None)] for n, k in enumerate((1, 3))],
            [block2(1, 1), block2(3, 1)],
        ],
        scal, (ds2,), rows=True,
    )
    u2_y = swap_y(u2)
    d2_x = swap(d2, 2)
    z_got = swap(z_send, 4)
    u0_z, d0_z = (0, 256), ((256, 384), (384, 512))
    outputs, d_hidden, grads2, d_o, o_send, o_keep = run(
        middle_back_kernel,
        [inputs.shape, (rows, width), (8, width), (rows, 512), (4, 256, 128), (4, 256, 128)],
        (scal,),
        (hidden, cotangent, ds0, ds1, ds2, ds3, out0, out1, out2, out3, gain2, o_all, w_all),
        (pltpu.VMEM((512, width), F32),),
        after=(u2,),
    )

    def back(js, after=()):
        arrays = (proj_own, proj_oth0, proj_oth1, carry_oth, carry_own, d_o) + saved

        def kernel(scal, starts, own, oth0, oth1, c_oth, c_own, d_o, *rest):
            dproj, dstate = rest[4:]
            for k, j in enumerate(js):
                if j < 2:
                    proj = own.at[own_pair(scal, j)]
                    carry = c_own[j]
                else:
                    proj = (oth0, oth1)[j - 2]
                    carry = c_oth[own_pair(scal, j - 2)]
                dstate[k] = attention_back(
                    scal[0], starts, proj, carry, rest[j], d_o,
                    slice(j * 128, (j + 1) * 128), dproj.at[k],
                )

        return run(
            kernel,
            [(len(js), rows, 512), (len(js), 136, 128)],
            tables,
            arrays,
            after=after,
        )

    def weight_grads(js, dstates, dprojs, after=(), extra=()):
        n = len(js)
        arrays = (proj_own, proj_oth0, proj_oth1, normed, o_send, o_keep)
        arrays += tuple(a for a, _ in dstates) + tuple(a for a, _ in dprojs)
        arrays += tuple(a for a, _ in extra)

        def kernel(scal, starts, own, oth0, oth1, normed, o_send, o_keep, *rest):
            states, grads, rest = rest[:n], rest[n : 2 * n], rest[2 * n :]
            send, keep, final = rest[len(extra) : len(extra) + 3]
            for k, j in enumerate(js):
                here = own.at[own_pair(scal, j)] if j < 2 else (oth0, oth1)[j - 2]
                pair_grads(
                    scal[0], starts, scal[1], here, states[k][dstates[k][1]], normed,
                    grads[k].at[dprojs[k][1]], o_send[j], o_keep[j],
                    send.at[k], keep.at[k], final.at[k],
                )
            if extra:
                value = None
                for ref, (_, lead) in zip(rest, extra):
                    term = ref[lead]
                    value = term if value is None else value + term
                rest[-1][...] = value

        outs = [(n, 256, 640), (n, 256, 640), (n, rows, 512)]
        return run(
            kernel, outs + [(256, 640)] * bool(extra), tables, arrays, after=after, us=LATE
        )

    dproj, dstate = back((1, 3, 0))
    dstate = to_first(dstate)
    up_terms = lambda part: block2(0, part) + [(u2_y, None, part), (z_got, u0_z, part)]
    d2, u2 = sums(
        [
            [block2(3, 0) + [(d2_x, (128, 256), None), (z_got, d0_z[1], None)]],
            [up_terms(1)],
        ],
        scal, (dproj,),
    )
    d2_y = swap_y(d2)
    u2_x = swap(u2, 2)
    send31, keep31, final31 = weight_grads(
        (3, 1), ((dstate, 0), (dstate, 1)), ((dproj, 1), (dproj, 0)), (d2,)
    )
    got31 = swap(send31, 1)
    ff_send, ff_keep = choose(
        up_terms(0) + [(u2_x, None, None)],
        block2(1, 0) + [(d2_x, (0, 128), None), (z_got, d0_z[0], None), (d2_y, None, None)],
        scal, 7, (final31,),
    )
    ff_got = swap(ff_send, 8)
    y_far1, y_near1 = sums(
        [[[(keep31, 0, 3), (got31, 0, 3)]], [[(keep31, 0, 2), (got31, 0, 2)]]], scal, (ff_send,)
    )
    y_far1_got = swap_y(y_far1)
    dproj2, dstate2 = back((2,), (y_far1,))
    dstate2 = to_first(dstate2)
    y_near1_got = swap_y(tie(y_near1, (dproj2,)))
    send2, keep2, final2, own_sum1 = weight_grads(
        (2,), ((dstate, 2),), ((dproj2, 0),), (dproj2,), ((keep31, 1), (got31, 1))
    )
    got2 = swap(send2, 1)
    (ff_shard,) = sums(
        [[[(ff_keep, None, None), (ff_got, None, None)]]], scal, (final2,)
    )
    step = ff_shard
    for at in bits[4:]:
        ff_send, ff_keep = halve([(ff_shard, None)], scal, at + 4, (step,))
        ff_got = swap(ff_send, 1 << at)
        (ff_shard,) = sums(
            [[[(ff_keep, None, None), (ff_got, None, None)]]], scal, (spacer(ff_send),)
        )
        step = ff_shard
    ff_steps = list(reversed(bits[3:]))
    ff_there = swap(ff_shard, 1 << ff_steps[0])
    y_far, x_far = sums(
        [
            [[(keep2, 0, 3), (got2, 0, 3)]],
            [[(own_sum1, None, 3), (y_far1_got, None, None)]],
        ],
        scal, (ff_shard,),
    )
    y_far_got = swap_y(y_far)
    x_far_got = swap(x_far, 2)
    send0, keep0, final0 = weight_grads((0,), ((dstate2, 0),), ((dproj, 2),), (y_far,))
    step = spacer(final0)
    grad_inputs, grads1 = run(
        first_back_kernel,
        [inputs.shape, (8, 640)],
        (scal,),
        (inputs, gain1, d_hidden, final0, final31, final2, qa0, qb0, qa1, qb1, grads2)
        + weights,
        (
            pltpu.VMEM((rows, 1024), F32),
            pltpu.VMEM((rows, width), F32),
            pltpu.VMEM((4, width, 256), F32),
            pltpu.SemaphoreType.DMA((4,)),
        ),
        after=(step,),
        far=4,
        us=LATE,
    )
    step = grads1
    while len(ff_steps) > 1:
        to = ff_steps.pop(0)
        ff_shard = join(ff_shard, ff_there, scal, to + 4, 0, (step,))
        ff_there = swap(ff_shard, 1 << ff_steps[0])
        step = spacer(ff_shard)
    ff_down, ff_up = choose(
        [(ff_shard, None, None)], [(ff_there, None, None)], scal, 7, (step,)
    )
    up_z = swap(ff_up, 4)
    down_x = swap(ff_down, 2)
    step = spacer(ff_up)
    got0 = swap(tie(send0, (ff_up,)), 1)
    q_send, y_near, x_near = sums(
        [
            [[(keep0, 0, 3), (got0, 0, 3), (y_far_got, None, None), (x_far_got, None, None)]],
            [[(keep2, 0, 2), (got2, 0, 2)]],
            [[(own_sum1, None, 2), (y_near1_got, None, None)]],
        ],
        scal, (step,),
    )
    q_got = swap(q_send, 4)
    y_near_got = swap_y(y_near)
    x_near_got = swap(x_near, 2)
    step = spacer(q_send)
    up_pair, down_pair, gains = sums(
        [
            [[(ff_up, None, None)], [(up_z, None, None)]],
            [[(ff_down, None, None)], [(down_x, None, None)]],
            [[(grads1, None, None)]],
        ],
        scal, (step,), rows=True,
    )
    gains_got = swap_y(gains)
    up_x = swap(up_pair, 2)
    down_z = swap(down_pair, 4)
    step = spacer(up_pair)
    (part,) = sums(
        [
            [
                [
                    (keep0, 0, 2), (got0, 0, 2), (y_near_got, None, None),
                    (x_near_got, None, None), (q_got, None, None),
                ]
            ]
        ],
        scal, (step,),
    )
    part_got = swap(part, 8)
    step = spacer(part)
    (gains,) = sums([[[(gains, None, None), (gains_got, None, None)]]], scal, (step,))
    for at in bits[3:]:
        gains_got = swap(gains, 1 << at)
        step = spacer(gains)
        terms = [
            [(part, None, None), (part_got, None, None)],
            [(gains, None, None), (gains_got, None, None)],
        ]
        if at == bits[-1]:
            (shard,) = sums([terms], scal, (step,), rows=True)
        else:
            part, gains = sums([terms[:1], terms[1:]], scal, (step,))
            part_got = swap(part, 2 << at)
    quarters = [shard] + [swap(shard, 2 * k) for k in (1, 2, 3)]
    up_x = tie(up_x, (quarters[2],))
    down_z = tie(down_z, (up_x,))
    pieces = (up_pair, up_x, down_pair, down_z)
    grad_up, grad_down, token = run(
        hidden_assemble_kernel,
        [up_weight.shape, down_weight.shape, (8, 128)],
        (scal,),
        pieces + tuple(swap(a, 1) for a in pieces),
        (pltpu.SemaphoreType.DMA((24,)),),
        after=(spacer(down_z),),
        away=True,
    )
    (quarters,) = sums([[[(a, None, None)] for a in quarters]], scal, (token,))
    *weight_grad, gain_a, gain_b, gain_c, gain_d = run(
        qkvc_assemble_kernel,
        [w.shape for w in weights] + [output_weight.shape] + [(1, width)] * 4,
        (scal,),
        (quarters, swap(quarters, 1)),
        after=(spacer(quarters),),
    )
    return (
        outputs, grad_inputs,
        *weight_grad, grad_up, grad_down,
        gain_a[0], gain_b[0], gain_c[0], gain_d[0],
    )


def solution(mesh):
    rows = P("head", "dp", None)
    cols = P(None, "head")
    tall = P("head", None)
    flat = P()
    return jax.shard_map(
        per_device,
        mesh=mesh,
        in_specs=(
            rows, P("dp", None), cols, cols, cols, cols, tall, cols, tall,
            flat, flat, flat, flat, rows,
        ),
        out_specs=(
            rows, rows, cols, cols, cols, cols, tall, cols, tall, flat, flat, flat, flat,
        ),
        check_vma=False,
    )
```

```python
import jax
import jax.numpy as jnp
from jax import lax
from jax.experimental import pallas as pl
from jax.experimental.pallas import tpu as pltpu
from jax.sharding import PartitionSpec as P

F32 = jnp.float32
HIGH = lax.Precision.HIGH
CHUNK = 256
EPS = 1e-05
GELU_C = 0.7978845608028654
GELU_K = 0.044715
VMEM_LIMIT = 16 * 2**20


def dot(left, right, dims):
    return lax.dot_general(
        left, right, (dims, ((), ())), precision=HIGH, preferred_element_type=F32
    )


def nn(left, right):
    return dot(left, right, ((1,), (0,)))


def nt(left, right):
    return dot(left, right, ((1,), (1,)))


def tn(left, right):
    return dot(left, right, ((0,), (0,)))


def whole():
    return pl.BlockSpec(memory_space=pltpu.VMEM)


def anywhere():
    return pl.BlockSpec(memory_space=pl.ANY)


def distant():
    return pl.BlockSpec(memory_space=pltpu.HBM)


def scalars():
    return pl.BlockSpec(memory_space=pltpu.SMEM)


FRONT, HEAVY, LATE, SUM = 20.0, 20.0, 20.0, 20.0


def cost(us):
    return pl.CostEstimate(flops=int(us * 1153e6), bytes_accessed=0, transcendentals=0)


def run(kernel, outs, scal, arrays, scratch=(), after=(), far=0, us=HEAVY, away=False):
    out_shape = [jax.ShapeDtypeStruct(shape, F32) for shape in outs]
    first, last = len(scal) + len(arrays), len(scal) + len(arrays) + len(after)
    return pl.pallas_call(
        lambda *refs: kernel(*refs[:first], *refs[last:]),
        out_shape=out_shape,
        in_specs=[scalars()] * len(scal)
        + [whole()] * (len(arrays) - far)
        + [distant()] * far
        + [anywhere()] * len(after),
        out_specs=[anywhere() if away else whole()] * len(outs),
        scratch_shapes=list(scratch),
        compiler_params=pltpu.CompilerParams(vmem_limit_bytes=VMEM_LIMIT),
        cost_estimate=cost(us),
    )(*scal, *arrays, *after)


def tie(array, after):
    count = 1 + len(after)
    return pl.pallas_call(
        lambda *refs: None,
        out_shape=jax.ShapeDtypeStruct(array.shape, F32),
        in_specs=[anywhere()] * count,
        out_specs=anywhere(),
        input_output_aliases={0: 0},
        compiler_params=pltpu.CompilerParams(vmem_limit_bytes=2**20),
        cost_estimate=pl.CostEstimate(flops=0, bytes_accessed=0, transcendentals=0),
    )(array, *after)


def spacer(*after):
    return pl.pallas_call(
        lambda *refs: None,
        out_shape=jax.ShapeDtypeStruct((8, 128), F32),
        in_specs=[anywhere()] * len(after),
        out_specs=anywhere(),
        compiler_params=pltpu.CompilerParams(vmem_limit_bytes=2**20),
        cost_estimate=cost(HEAVY),
    )(*after)


def lane_slice(ref, index, width):
    return ref[:, pl.ds(pl.multiple_of(index * width, width), width)]


def normalize(x):
    centre = x - jnp.mean(x, axis=-1, keepdims=True)
    spread = jnp.mean(centre * centre, axis=-1, keepdims=True)
    r = lax.rsqrt(spread + EPS)
    return centre * r, r


def norm_back(dy, nhat, r, gain):
    dyg = dy * gain
    first = jnp.mean(dyg, axis=-1, keepdims=True)
    second = jnp.mean(dyg * nhat, axis=-1, keepdims=True)
    return r * (dyg - first - nhat * second)


def doc_of(starts, position):
    total = jnp.zeros(jnp.shape(position), jnp.int32)
    for k in range(starts.shape[1]):
        total = total + (position >= starts[0, k]).astype(jnp.int32)
    return total


def column(first, count):
    return first + lax.broadcasted_iota(jnp.int32, (count, 1), 0)


def left_lanes():
    return lax.broadcasted_iota(jnp.int32, (1, 128), 1) < 64


def pack_state(mk, mv, z):
    left = left_lanes()
    return jnp.concatenate(
        [
            jnp.where(left, mk[0:64], mk[64:128]),
            jnp.where(left, mv[0:64], mv[64:128]),
            jnp.broadcast_to(z, (8, 128)),
        ],
        axis=0,
    )


def blocks_only(m):
    diagonal = (lax.broadcasted_iota(jnp.int32, (128, 128), 0) < 64) == (
        lax.broadcasted_iota(jnp.int32, (128, 128), 1) < 64
    )
    return jnp.where(diagonal, m, 0.0)


def unpack_state(state):
    mk = state[0:64]
    mv = state[64:128]
    return (
        blocks_only(jnp.concatenate([mk, mk], axis=0)),
        blocks_only(jnp.concatenate([mv, mv], axis=0)),
        state[128:129],
    )


def end_state(k2, v2, e2, starts, first):
    count = k2.shape[0]
    kept = (doc_of(starts, column(first, count)) == doc_of(starts, first + count - 1)).astype(F32)
    em = e2 * kept
    return pack_state(outer(k2, em), outer(em, v2), jnp.sum(em, axis=0, keepdims=True))


def cut_first_kernel(scal, wq, wk, wv, wc, piece, sems):
    rows = pl.ds(pl.multiple_of(scal[1] * 256, 256), 256)
    lanes = pl.ds(pl.multiple_of(scal[2] * 128, 128), 128)
    copies = [
        pltpu.make_async_copy(
            ref.at[rows, lanes], piece.at[:, w * 128 : (w + 1) * 128], sems.at[w]
        )
        for w, ref in enumerate((wq, wk, wv, wc))
    ]
    for copy in copies:
        copy.start()
    for copy in copies:
        copy.wait()


def cut_second_kernel(scal, wo, up, down, piece, sems):
    unit = pl.ds(pl.multiple_of(scal[3] * 256 + scal[2] * 128, 128), 128)
    thin = pl.ds(pl.multiple_of((scal[2] * 2 + scal[1]) * 64, 64), 64)
    copies = [
        pltpu.make_async_copy(
            up.at[b * 128 : (b + 1) * 128, unit], piece.at[0:128, b * 128 : (b + 1) * 128],
            sems.at[b],
        )
        for b in range(4)
    ]
    copies.append(pltpu.make_async_copy(down.at[unit, :], piece.at[128:256, :], sems.at[4]))
    copies.append(pltpu.make_async_copy(wo.at[thin, :], piece.at[256:320, :], sems.at[5]))
    for copy in copies:
        copy.start()
    for copy in copies:
        copy.wait()


def cut(kernel, shapes, scal, arrays, after=(), limit=2**20, near=False):
    first, last = 1 + len(arrays), 1 + len(arrays) + len(after)
    out_shape = [jax.ShapeDtypeStruct(shape, F32) for shape in shapes]
    return pl.pallas_call(
        lambda *refs: kernel(*refs[:first], *refs[last:]),
        out_shape=out_shape,
        in_specs=[scalars()] + [distant()] * len(arrays) + [anywhere()] * len(after),
        out_specs=[whole() if near else anywhere()] * len(shapes),
        scratch_shapes=[pltpu.SemaphoreType.DMA((6,))],
        compiler_params=pltpu.CompilerParams(vmem_limit_bytes=limit),
        cost_estimate=cost(FRONT),
    )(scal, *arrays, *after)


def own_kernel(scal, starts, x, gain, shift, wq, wk, wv, wc, normed, proj, states, held, sems):
    copies = [
        pltpu.make_async_copy(ref, held.at[w], sems.at[w])
        for w, ref in enumerate((wq, wk, wv, wc))
    ]
    for copy in copies:
        copy.start()
    nhat, _ = normalize(x[:, 0, :])
    n = nhat * gain[...] + shift[...]
    normed[...] = n
    for w, copy in enumerate(copies):
        copy.wait()
        full = nn(n, held[w])
        if w == 3:
            full = jnp.exp(full)
        for p in range(2):
            proj[p, :, w * 128 : (w + 1) * 128] = full[:, p * 128 : (p + 1) * 128]
    for p in range(2):
        states[p] = end_state(
            proj[p, :, 128:256], proj[p, :, 256:384], proj[p, :, 384:512], starts, scal[0]
        )


def other_kernel(scal, starts, normed, wa, wb, proj, states, before=None):
    core = scal[1]
    full = nn(lane_slice(normed, core, 256), wa[...]) + nn(
        lane_slice(normed, 1 - core, 256), wb[...]
    )
    proj[:, 0:384] = full[:, 0:384]
    proj[:, 384:512] = jnp.exp(full[:, 384:512])
    state = end_state(proj[:, 128:256], proj[:, 256:384], proj[:, 384:512], starts, scal[0])
    if before is None:
        states[...] = state
    else:
        states[0] = before[...]
        states[1] = state


def chunk_masks(starts, first, c):
    begin = first + c * CHUNK
    position = column(begin, CHUNK)
    docs = doc_of(starts, position)
    row = begin + lax.broadcasted_iota(jnp.int32, (1, CHUNK), 1)
    mask = (position >= row) & (docs == doc_of(starts, row))
    before = doc_of(starts, begin - 1)
    last = doc_of(starts, begin + CHUNK - 1)
    entering = (docs == before).astype(F32)
    leaving = (docs == last).astype(F32)
    passing = (before == last).astype(F32)
    return mask, entering, leaving, passing


BF16 = jnp.bfloat16


def raw(left, right, dims):
    return lax.dot_general(left, right, (dims, ((), ())), preferred_element_type=F32)


def rest_of(x):
    return x - x.astype(BF16).astype(F32)


def turn(x):
    return pltpu.roll(x, 64, 1)


def beside(a, b):
    return jnp.concatenate([a, b], axis=1).astype(BF16)


def rows_factor(x):
    left = left_lanes()
    low = turn(rest_of(x))
    return (
        beside(jnp.where(left, x, low), jnp.where(left, x, 0.0)),
        beside(jnp.where(left, low, x), jnp.where(left, 0.0, x)),
    )


def columns_factor(x):
    left = left_lanes()
    other = turn(x)
    low = rest_of(x)
    return (
        beside(jnp.where(left, x, other), low),
        beside(jnp.where(left, other, x), low),
    )


def affinity_of(rows, columns, mask):
    result = []
    for r, c in zip(rows, columns):
        value = jnp.where(mask, raw(r, c, ((1,), (1,))), 0.0)
        high = value.astype(BF16)
        result.append((high, (value - high.astype(F32)).astype(BF16)))
    return result


def narrow(x):
    left = left_lanes()
    low = rest_of(x)
    return (
        jnp.where(left, x, turn(low)).astype(BF16),
        jnp.where(left, turn(low), x).astype(BF16),
    )


def gather_heads(first, second):
    left = left_lanes()
    return jnp.where(left, first, second) + turn(jnp.where(left, second, first))


def spread(matrices, x):
    outs = []
    for (high, low), part in zip(matrices, x):
        outs.append(raw(high, part, ((1,), (0,))) + raw(low, part, ((1,), (0,))))
    return gather_heads(*outs)


def spread_back(matrices, x):
    outs = []
    for (high, low), part in zip(matrices, x):
        outs.append(raw(high, part, ((0,), (0,))) + raw(low, part, ((0,), (0,))))
    return gather_heads(*outs)


def fold(x):
    return x[:, 0:128] + x[:, 128:256]


def both_parts(x):
    return beside(x, rest_of(x))


def masked_sum(mask, x):
    return fold(raw(mask, both_parts(x), ((1,), (0,))))


def masked_sum_back(mask, x):
    return fold(raw(mask, both_parts(x), ((0,), (0,))))


def times_state(x, m):
    part = both_parts(m)
    return fold(raw(both_parts(x), jnp.concatenate([part, part], axis=0), ((1,), (0,))))


def times_state_back(x, m):
    low = rest_of(m)
    right = jnp.concatenate([beside(m, m), beside(low, low)], axis=0)
    return fold(raw(both_parts(x), right, ((1,), (1,))))


def outer(x, y):
    full = raw(both_parts(x), both_parts(y), ((0,), (0,)))
    return blocks_only(fold(full[0:128] + full[128:256]))


def slot_sums(x):
    left = left_lanes()
    return jnp.where(
        left,
        jnp.sum(jnp.where(left, x, 0.0), axis=1, keepdims=True),
        jnp.sum(jnp.where(left, 0.0, x), axis=1, keepdims=True),
    )


def next_state(k2, v2, e2, state, leaving, passing):
    mk, mv, z_in = state
    em = e2 * leaving
    return (
        outer(k2, em) + passing * mk,
        outer(em, v2) + passing * mv,
        jnp.sum(em, axis=0, keepdims=True) + passing * z_in,
    )


def attention(first, starts, proj, carry, o, lanes, saved):
    left = left_lanes()
    state = unpack_state(carry)
    chunks = proj.shape[0] // CHUNK
    for c in range(chunks):
        rows = slice(c * CHUNK, (c + 1) * CHUNK)
        q2, k2 = proj[rows, 0:128], proj[rows, 128:256]
        v2, e2 = proj[rows, 256:384], proj[rows, 384:512]
        mask, entering, leaving, passing = chunk_masks(starts, first, c)
        mk, mv, z_in = state
        z = masked_sum(mask.astype(F32).astype(BF16), e2) + entering * z_in
        affinity = affinity_of(rows_factor(q2), columns_factor(k2), mask)
        total = spread(affinity, narrow(e2)) + entering * times_state(q2, mk)
        s = total / z * 0.125
        top = jnp.where(
            left,
            jnp.max(jnp.where(left, s, -jnp.inf), axis=1, keepdims=True),
            jnp.max(jnp.where(left, -jnp.inf, s), axis=1, keepdims=True),
        )
        p = jnp.exp(s - top)
        p = p / slot_sums(p)
        r = p / z
        mixing = affinity_of(rows_factor(r), columns_factor(e2), mask)
        o[rows, lanes] = spread(mixing, narrow(v2)) + entering * times_state(r, mv)
        saved[rows, 0:128] = z
        saved[rows, 128:256] = s
        saved[rows, 256:384] = p
        if c + 1 < chunks:
            state = next_state(k2, v2, e2, state, leaving, passing)


def attention_back(first, starts, proj, carry, saved, d_o, lanes, dproj):
    chunks = proj.shape[0] // CHUNK
    states = [unpack_state(carry)]
    for c in range(chunks - 1):
        rows = slice(c * CHUNK, (c + 1) * CHUNK)
        _, _, leaving, passing = chunk_masks(starts, first, c)
        states.append(
            next_state(
                proj[rows, 128:256], proj[rows, 256:384], proj[rows, 384:512], states[c],
                leaving, passing,
            )
        )
    ahead = None
    for c in reversed(range(chunks)):
        rows = slice(c * CHUNK, (c + 1) * CHUNK)
        q2, k2 = proj[rows, 0:128], proj[rows, 128:256]
        v2, e2 = proj[rows, 256:384], proj[rows, 384:512]
        z, s, p = saved[rows, 0:128], saved[rows, 128:256], saved[rows, 256:384]
        do2 = d_o[rows, lanes]
        mask, entering, leaving, passing = chunk_masks(starts, first, c)
        mk, mv, _ = states[c]
        r = p / z
        do_in = entering * do2
        e_columns, e_narrow = columns_factor(e2), narrow(e2)
        mixing = affinity_of(rows_factor(r), e_columns, mask)
        d_mixing = affinity_of(rows_factor(do2), columns_factor(v2), mask)
        dv = spread_back(mixing, narrow(do2))
        dr = spread(d_mixing, e_narrow) + times_state_back(do_in, mv)
        de = spread_back(d_mixing, narrow(r))
        dp = dr / z
        dz = -dp * r
        ds = p * (dp - slot_sums(p * dp)) / z
        w = ds * 0.125
        dz = dz - ds * s
        w_in = entering * w
        affinity = affinity_of(rows_factor(q2), columns_factor(k2), mask)
        d_affinity = affinity_of(rows_factor(w), e_columns, mask)
        dq = spread(d_affinity, narrow(k2)) + times_state_back(w_in, mk)
        dk = spread_back(d_affinity, narrow(q2))
        de = de + spread_back(affinity, narrow(w))
        de = de + masked_sum_back(mask.astype(F32).astype(BF16), dz)
        if ahead is not None:
            dmk, dmv, dz_out = ahead
            em = e2 * leaving
            dv = dv + times_state(em, dmv)
            dk = dk + times_state_back(em, dmk)
            de = de + leaving * (times_state(k2, dmk) + times_state_back(v2, dmv) + dz_out)
        dproj[rows, 0:128] = dq
        dproj[rows, 128:256] = dk
        dproj[rows, 256:384] = dv
        dproj[rows, 384:512] = de
        now = (
            outer(q2, w_in),
            outer(r, do_in),
            jnp.sum(entering * dz, axis=0, keepdims=True),
        )
        if ahead is not None:
            now = tuple(a + passing * b for a, b in zip(now, ahead))
        ahead = now
    return pack_state(*ahead)


def own_pair(scal, j):
    return jnp.bitwise_xor(scal[2], j)


def attention_kernel(scal, starts, proj, carry, o, saved, j=None):
    here = proj if j is None else proj.at[own_pair(scal, j)]
    attention(scal[0], starts, here, carry, o, slice(0, 128), saved)


def middle_kernel(
    scal, o0, o1, o2, o3, x, wo, w0, w1, w2, w3, gain, shift, hidden, second, o_all, w_all,
):
    for j, ref in enumerate((o0, o1, o2, o3)):
        o_all[:, j * 128 : (j + 1) * 128] = ref[...]
    for j in range(2):
        which = pl.multiple_of(own_pair(scal, j) * 128, 128)
        w_all[j * 128 : (j + 1) * 128, :] = wo[pl.ds(which, 128), :]
    for k, ref in enumerate((w0, w1, w2, w3)):
        start = 256 + (k >> 1) * 128 + jnp.bitwise_xor(scal[1], k & 1) * 64
        w_all[pl.ds(pl.multiple_of(start, 64), 64), :] = ref[256:320, :]
    h = x[:, 0, :] + nn(o_all[...], w_all[...])
    hidden[...] = h
    nhat, _ = normalize(h)
    second[...] = nhat * gain[...] + shift[...]


def middle_back_kernel(
    scal, hidden, cot, ds0, ds1, ds2, ds3, u0, u1, u2, u3, gain, o_all, w_all,
    outputs, d_hidden, grads, d_o, send, keep, work,
):
    core = scal[1]
    outputs[:, 0, :] = hidden[...] + ((u0[...] + u1[...]) + (u2[...] + u3[...]))
    d_second = (ds0[...] + ds1[...]) + (ds2[...] + ds3[...])
    nhat, r = normalize(hidden[...])
    grads[0:1, :] = jnp.sum(d_second * nhat, axis=0, keepdims=True)
    grads[1:2, :] = jnp.sum(d_second, axis=0, keepdims=True)
    grads[2:8, :] = jnp.zeros((6, grads.shape[1]), F32)
    d = cot[:, 0, :] + norm_back(d_second, nhat, r, gain[...])
    d_hidden[...] = d
    d_o[...] = nt(d, w_all[...])
    work[...] = tn(o_all[...], d)
    for ref, which in ((send, 1 - core), (keep, core)):
        for j in range(4):
            rows = pl.ds(pl.multiple_of(j * 128 + which * 64, 64), 64)
            for b in range(4):
                ref[j, b * 64 : (b + 1) * 64, :] = work[rows, b * 128 : (b + 1) * 128]


def feed_forward_kernel(j, scal, second, cot, up, down, unit, other, packed, out, ds, up_far, down_far):
    where = pl.ds(pl.multiple_of(jnp.bitwise_xor(scal[3], j) * 256, 256), 256)
    for ref, half in ((unit, scal[2]), (other, 1 - scal[2])):
        place = pl.ds(pl.multiple_of(half * 128, 128), 128)
        for b in range(4):
            up_far[b * 128 : (b + 1) * 128, place] = ref[0:128, b * 128 : (b + 1) * 128]
        down_far[place, :] = ref[128:256, :]
    n_left, n_right = second[:, 0:256], second[:, 256:512]
    g = cot[:, 0, :]
    for half in range(2):
        if half == 0:
            up_left, up_right = up[0:256, where], up[256:512, where]
            down_block = down[where, :]
        else:
            up_left, up_right = up_far[0:256, :], up_far[256:512, :]
            down_block = down_far[...]
        u = nn(n_left, up_left) + nn(n_right, up_right)
        inner = GELU_C * (u + GELU_K * u * u * u)
        t = jnp.tanh(inner)
        act = 0.5 * u * (1.0 + t)
        slope = 0.5 * (1.0 + t) + 0.5 * u * (1.0 - t * t) * (
            GELU_C * (1.0 + 3.0 * GELU_K * u * u)
        )
        du = nt(g, down_block) * slope
        packed[2 * half, :, 0:256] = tn(n_left, du)
        packed[2 * half, :, 256:512] = tn(n_right, du)
        packed[2 * half + 1] = tn(act, g)
        out_part = nn(act, down_block)
        ds_left, ds_right = nt(du, up_left), nt(du, up_right)
        if half == 0:
            out[...] = out_part
            ds[:, 0:256] = ds_left
            ds[:, 256:512] = ds_right
        else:
            out[...] = out[...] + out_part
            ds[:, 0:256] = ds[:, 0:256] + ds_left
            ds[:, 256:512] = ds[:, 256:512] + ds_right


def pair_grads(first, starts, core, proj, dstate, normed, dproj, o_send, o_keep, send, keep, final):
    k2, v2, e2 = proj[:, 128:256], proj[:, 256:384], proj[:, 384:512]
    count = k2.shape[0]
    dmk, dmv, dz_out = unpack_state(dstate)
    leaving = (
        doc_of(starts, column(first, count)) == doc_of(starts, first + count - 1)
    ).astype(F32)
    em = e2 * leaving
    final[:, 0:128] = dproj[:, 0:128]
    final[:, 128:256] = dproj[:, 128:256] + times_state_back(em, dmk)
    final[:, 256:384] = dproj[:, 256:384] + times_state(em, dmv)
    de = dproj[:, 384:512] + leaving * (
        times_state(k2, dmk) + times_state_back(v2, dmv) + dz_out
    )
    final[:, 384:512] = e2 * de
    send[:, 0:512] = tn(lane_slice(normed, 1 - core, 256), final[...])
    keep[:, 0:512] = tn(lane_slice(normed, core, 256), final[...])
    send[:, 512:640] = o_send
    keep[:, 512:640] = o_keep


def first_back_kernel(
    scal, x, gain, d_hidden, f0, f31, f2, a0, b0, a1, b1, grads2, wq, wk, wv, wc,
    grad_x, grads, cat, acc, held, sems,
):
    core, pair = scal[1], scal[2]
    copies = [
        pltpu.make_async_copy(ref, held.at[w], sems.at[w])
        for w, ref in enumerate((wq, wk, wv, wc))
    ]
    for copy in copies:
        copy.start()
    for j, ref in enumerate((f0.at[0], f31.at[1])):
        which = jnp.bitwise_xor(pair, j)
        for w in range(4):
            start = pl.multiple_of(w * 256 + which * 128, 128)
            cat[:, pl.ds(start, 128)] = ref[:, w * 128 : (w + 1) * 128]
    total = None
    for w, copy in enumerate(copies):
        copy.wait()
        part = nt(cat[:, w * 256 : (w + 1) * 256], held[w])
        total = part if total is None else total + part
    acc[...] = total
    for which, refs in ((core, (a0, a1)), (1 - core, (b0, b1))):
        part = nt(f2[0], refs[0][...]) + nt(f31[0], refs[1][...])
        lanes = pl.ds(pl.multiple_of(which * 256, 256), 256)
        acc[:, lanes] = acc[:, lanes] + part
    d_normed = acc[...]
    nhat, r = normalize(x[:, 0, :])
    grads[...] = jnp.zeros(grads.shape, F32)
    grads[0:1, 0:512] = jnp.sum(d_normed * nhat, axis=0, keepdims=True)
    grads[1:2, 0:512] = jnp.sum(d_normed, axis=0, keepdims=True)
    grads[2:4, 0:512] = grads2[0:2, :]
    grad_x[:, 0, :] = d_hidden[...] + norm_back(d_normed, nhat, r, gain[...])


def table_of(groups):
    arrays, places = [], []
    for group in groups:
        places.append([])
        for array, lead, part in group:
            at = next((i for i, a in enumerate(arrays) if a is array), None)
            if at is None:
                at = len(arrays)
                arrays.append(array)
            places[-1].append((at, lead, part))
    return arrays, places


def total(scal, refs, place):
    value = None
    for at, lead, part in place:
        if isinstance(lead, tuple):
            ref = refs[at].at[lead[0] : lead[1], :]
        else:
            ref = refs[at] if lead is None else refs[at].at[lead]
        if part is None:
            term = ref[...]
        else:
            rows = ref.shape[0] // 2
            which = jnp.bitwise_xor(scal[2 if part < 2 else 6], part & 1) * rows
            term = ref[pl.ds(pl.multiple_of(which, rows), rows), :]
        value = term if value is None else value + term
    return value


def shape_of(group):
    array, lead, part = group[0]
    rows, cols = array.shape[-2:]
    if isinstance(lead, tuple):
        rows = lead[1] - lead[0]
    return (rows if part is None else rows // 2, cols)


def sums(outs, scal, after=(), rows=False):
    arrays, places = table_of([group for out in outs for group in out])
    shapes = []
    for out in outs:
        h, w = shape_of(out[0])
        if rows:
            shapes.append((sum(shape_of(g)[0] for g in out), w))
        else:
            shapes.append((h, w) if len(out) == 1 else (len(out), h, w))

    def kernel(scal, *refs):
        at = 0
        for n, out in enumerate(outs):
            target = refs[len(arrays) + n]
            row = 0
            for k in range(len(out)):
                value = total(scal, refs, places[at])
                at += 1
                if rows:
                    target[row : row + value.shape[0], :] = value
                    row += value.shape[0]
                elif len(out) == 1:
                    target[...] = value
                else:
                    target[k] = value

    return run(kernel, shapes, (scal,), arrays, after=after, us=SUM)


def choose(first, second, scal, at, after=()):
    arrays, places = table_of([first, second])

    def kernel(scal, *refs):
        values = [total(scal, refs, place) for place in places]
        for side in range(2):

            @pl.when(scal[at] == side)
            def _():
                refs[-2][...] = values[1 - side]
                refs[-1][...] = values[side]

    return run(kernel, [shape_of(first)] * 2, (scal,), arrays, after=after, us=SUM)


def halve(terms, scal, at, after=()):
    rows, cols = terms[0][0].shape[-2:]
    rows //= 2
    leads = [lead for _, lead in terms]

    def kernel(scal, *refs):
        for out, which in ((refs[-2], 1 - scal[at]), (refs[-1], scal[at])):
            block = pl.ds(pl.multiple_of(which * rows, rows), rows)
            value = None
            for ref, lead in zip(refs, leads):
                term = ref[block, :] if lead is None else ref[lead, block, :]
                value = term if value is None else value + term
            out[...] = value

    return run(
        kernel, [(rows, cols)] * 2, (scal,), [a for a, _ in terms], after=after, us=SUM
    )


def join(here, there, scal, at, tail=8, after=()):
    rows, cols = here.shape
    rows -= tail

    def kernel(scal, here, there, out):
        for ref, which in ((here, scal[at]), (there, 1 - scal[at])):
            block = pl.ds(pl.multiple_of(which * rows, rows), rows)
            out[block, :] = ref[0:rows, :]
        if tail:
            out[2 * rows :, :] = here[rows:, :] + there[rows:, :]

    return run(kernel, [(2 * rows + tail, cols)], (scal,), (here, there), after=after, us=SUM)[0]


def hidden_assemble_kernel(scal, *refs):
    pieces, (up, down, token, sem) = refs[:8], refs[8:]
    copies = []
    for c in range(2):
        for k in range(2):
            ups, downs = pieces[4 * c + k], pieces[4 * c + 2 + k]
            for n in range(2):
                rows = slice(n * 128, n * 128 + 128)
                half = jnp.bitwise_xor(scal[2], k) * 128
                block = jnp.bitwise_xor(scal[3], c + 2 - 2 * n)
                lanes = pl.ds(pl.multiple_of(block * 256, 256), 256)
                upper = pl.ds(pl.multiple_of(half, 128), 128)
                lower = pl.ds(pl.multiple_of(half + 256, 128), 128)
                half = jnp.bitwise_xor(scal[2], n) * 128
                block = jnp.bitwise_xor(scal[3], c + 2 - 2 * k)
                where = pl.ds(pl.multiple_of(block * 256 + half, 128), 128)
                copies += [
                    (ups.at[rows, 0:256], up.at[upper, lanes]),
                    (ups.at[rows, 256:512], up.at[lower, lanes]),
                    (downs.at[rows, :], down.at[where, :]),
                ]
    copies = [
        pltpu.make_async_copy(source, target, sem.at[n])
        for n, (source, target) in enumerate(copies)
    ]
    for copy in copies:
        copy.start()
    for copy in copies:
        copy.wait()


def qkvc_assemble_kernel(scal, *refs):
    (here, there), (wq, wk, wv, wc, wo), gains = refs[:2], refs[2:7], refs[7:]
    pieces = [ref.at[k] for ref in (here, there) for k in range(4)]
    size = here.shape[1] - 8
    tails = None
    for k, ref in enumerate(pieces):
        half = jnp.bitwise_xor(scal[1], k >> 2)
        which = jnp.bitwise_xor(scal[2], k & 1)
        first = jnp.bitwise_xor(scal[6], (k >> 1) & 1) * size
        rows = pl.ds(pl.multiple_of(half * 256 + first, size), size)
        lanes = pl.ds(pl.multiple_of(which * 128, 128), 128)
        for w, out in enumerate((wq, wk, wv, wc)):
            out[rows, lanes] = ref[0:size, w * 128 : (w + 1) * 128]
        for b in range(size // 64):
            start = pl.multiple_of(first // 64 * 128 + b * 128, 128)
            out_rows = pl.ds(pl.multiple_of(which * 128 + half * 64, 64), 64)
            wo[out_rows, pl.ds(start, 128)] = ref[b * 64 : (b + 1) * 64, 512:640]
        tail = ref[size : size + 8, 0:512]
        tails = tail if tails is None else tails + tail
    for k, ref in enumerate(gains):
        ref[...] = tails[k : k + 1, :]


def per_device(
    inputs, doc_starts, query_weight, key_weight, value_weight, control_weight, output_weight,
    up_weight, down_weight, first_gain, first_shift, second_gain, second_shift, cotangent,
):
    rows, _, width = inputs.shape
    devices = lax.axis_size("dp")
    place = lax.axis_index("dp").astype(jnp.int32)
    y = lax.axis_index("head").astype(jnp.int32)
    core = place & 1
    pair = (place >> 1) & 1
    one = lambda *v: jnp.stack([jnp.asarray(a, jnp.int32) for a in v])
    depth = (place >> 2) & 1
    bits = [at for at in range(31) if (1 << at) < devices]
    scal = one(y * rows, core, pair, depth * 2 + core, *((place >> at) & 1 for at in bits))
    gain1, shift1 = first_gain.reshape(1, width), first_shift.reshape(1, width)
    gain2, shift2 = second_gain.reshape(1, width), second_shift.reshape(1, width)
    weights = (query_weight, key_weight, value_weight, control_weight)

    def swap_y(a):
        return lax.ppermute(a, "head", [(0, 1), (1, 0)])

    def swap(a, bits):
        return lax.ppermute(a, "dp", [(i, i ^ bits) for i in range(devices)])

    to_second = lambda a: lax.ppermute(a, "head", [(0, 1)])
    to_first = lambda a: lax.ppermute(a, "head", [(1, 0)])

    tables = (scal, doc_starts)
    (piece,) = cut(cut_first_kernel, [(256, 512)], scal, weights, limit=60 * 2**20, near=True)
    qa0 = swap_y(piece)
    normed, proj_own, states_own = run(
        own_kernel,
        [(rows, width), (2, rows, 512), (2, 136, 128)],
        tables,
        (inputs, gain1, shift1) + weights,
        (pltpu.VMEM((4, width, 256), F32), pltpu.SemaphoreType.DMA((4,))),
        after=(piece,),
        far=4,
        us=FRONT,
    )
    carry_oth = to_second(states_own)
    qa0 = tie(qa0, (carry_oth,))
    qb0 = swap(qa0, 1)
    qa1 = swap(qa0, 2)
    (unit,) = cut(
        cut_second_kernel, [(320, 512)], scal, (output_weight, up_weight, down_weight), (qa0,)
    )
    unit0 = swap_y(unit)

    proj_oth0, state0 = run(
        other_kernel, [(rows, 512), (136, 128)], tables, (normed, qa0, qb0),
        after=(unit,), us=FRONT,
    )

    def attend(proj, carry, j, after=()):
        def kernel(scal, starts, proj, carry, o, saved):
            state = carry[own_pair(scal, j - 2)] if j >= 2 else carry[j]
            attention_kernel(scal, starts, proj, state, o, saved, j if j < 2 else None)

        return run(
            kernel, [(rows, 128), (rows, 384)], tables, (proj, carry), after=after, us=FRONT
        )

    qa1 = tie(qa1, (proj_oth0,))
    qb1 = swap(qa1, 1)
    o2, saved2 = attend(proj_oth0, carry_oth, 2, (qa1,))
    unit0 = tie(unit0, (o2,))
    unit1, unit2, unit4 = swap(unit0, 1), swap(unit0, 2), swap(unit0, 4)
    proj_oth1, states_oth = run(
        lambda scal, starts, normed, wa, wb, before, proj, states: other_kernel(
            scal, starts, normed, wa, wb, proj, states, before
        ),
        [(rows, 512), (2, 136, 128)], tables, (normed, qa1, qb1, state0),
        after=(unit0,), us=FRONT,
    )
    carry_own = to_second(states_oth)
    o3, saved3 = attend(proj_oth1, carry_oth, 3, (unit0,))
    o0, saved0 = attend(proj_own, carry_own, 0, (o3,))
    o1, saved1 = attend(proj_own, carry_own, 1, (o0, unit1))
    unit2 = tie(unit2, (o1,))
    unit3, unit6 = swap(unit2, 1), swap(unit2, 4)
    hidden, second, o_all, w_all = run(
        middle_kernel,
        [(rows, width), (rows, width), (rows, 512), (512, width)],
        (scal,),
        (o0, o1, o2, o3, inputs, output_weight, unit0, unit1, unit2, unit3, gain2, shift2),
        after=(spacer(unit2),),
        us=FRONT,
    )
    saved = (saved0, saved1, saved2, saved3)

    def feed_forward(j, unit, other, after=()):
        return run(
            lambda *refs: feed_forward_kernel(j, *refs),
            [(4, 256, 512), (rows, width), (rows, width)],
            (scal,),
            (second, cotangent, up_weight, down_weight, unit, other),
            (pltpu.VMEM((width, 256), F32), pltpu.VMEM((256, width), F32)),
            after=after,
        )

    part1, out1, ds1 = feed_forward(1, unit1, unit3)
    got1 = swap(part1, 1)
    part0, out0, ds0 = feed_forward(0, unit0, unit2, (ds1,))
    unit4, unit6 = tie(unit4, (ds0,)), tie(unit6, (ds0,))
    unit5, unit7 = swap(unit4, 1), swap(unit6, 1)
    def block0(k, part=None):
        return [(part0, k, part), (got1, k, part)]

    def block2(k, part=None):
        return [(part2, k, part), (got3, k, part)]

    u0, d0 = sums([[block0(2)], [block0(1, 1), block0(3, 1)]], scal)
    u0_y = swap_y(u0)
    d0_x = swap(d0, 2)
    part3, out3, ds3 = feed_forward(3, unit5, unit7, (u0,))
    got3 = swap(part3, 1)
    part2, out2, ds2 = feed_forward(2, unit4, unit6, (ds3,))
    u2, z_send, d2 = sums(
        [
            [block2(2)],
            [block0(0) + [(u0_y, None, None)]]
            + [block0(k, 0) + [(d0_x, n, None)] for n, k in enumerate((1, 3))],
            [block2(1, 1), block2(3, 1)],
        ],
        scal, (ds2,), rows=True,
    )
    u2_y = swap_y(u2)
    d2_x = swap(d2, 2)
    z_got = swap(z_send, 4)
    u0_z, d0_z = (0, 256), ((256, 384), (384, 512))
    outputs, d_hidden, grads2, d_o, o_send, o_keep = run(
        middle_back_kernel,
        [inputs.shape, (rows, width), (8, width), (rows, 512), (4, 256, 128), (4, 256, 128)],
        (scal,),
        (hidden, cotangent, ds0, ds1, ds2, ds3, out0, out1, out2, out3, gain2, o_all, w_all),
        (pltpu.VMEM((512, width), F32),),
        after=(u2,),
    )

    def back(js, after=()):
        arrays = (proj_own, proj_oth0, proj_oth1, carry_oth, carry_own, d_o) + saved

        def kernel(scal, starts, own, oth0, oth1, c_oth, c_own, d_o, *rest):
            dproj, dstate = rest[4:]
            for k, j in enumerate(js):
                if j < 2:
                    proj = own.at[own_pair(scal, j)]
                    carry = c_own[j]
                else:
                    proj = (oth0, oth1)[j - 2]
                    carry = c_oth[own_pair(scal, j - 2)]
                dstate[k] = attention_back(
                    scal[0], starts, proj, carry, rest[j], d_o,
                    slice(j * 128, (j + 1) * 128), dproj.at[k],
                )

        return run(
            kernel,
            [(len(js), rows, 512), (len(js), 136, 128)],
            tables,
            arrays,
            after=after,
        )

    def weight_grads(js, dstates, dprojs, after=(), extra=()):
        n = len(js)
        arrays = (proj_own, proj_oth0, proj_oth1, normed, o_send, o_keep)
        arrays += tuple(a for a, _ in dstates) + tuple(a for a, _ in dprojs)
        arrays += tuple(a for a, _ in extra)

        def kernel(scal, starts, own, oth0, oth1, normed, o_send, o_keep, *rest):
            states, grads, rest = rest[:n], rest[n : 2 * n], rest[2 * n :]
            send, keep, final = rest[len(extra) : len(extra) + 3]
            for k, j in enumerate(js):
                here = own.at[own_pair(scal, j)] if j < 2 else (oth0, oth1)[j - 2]
                pair_grads(
                    scal[0], starts, scal[1], here, states[k][dstates[k][1]], normed,
                    grads[k].at[dprojs[k][1]], o_send[j], o_keep[j],
                    send.at[k], keep.at[k], final.at[k],
                )
            if extra:
                value = None
                for ref, (_, lead) in zip(rest, extra):
                    term = ref[lead]
                    value = term if value is None else value + term
                rest[-1][...] = value

        outs = [(n, 256, 640), (n, 256, 640), (n, rows, 512)]
        return run(
            kernel, outs + [(256, 640)] * bool(extra), tables, arrays, after=after, us=LATE
        )

    dproj, dstate = back((1, 3, 0))
    dstate = to_first(dstate)
    up_terms = lambda part: block2(0, part) + [(u2_y, None, part), (z_got, u0_z, part)]
    d2, u2 = sums(
        [
            [block2(3, 0) + [(d2_x, (128, 256), None), (z_got, d0_z[1], None)]],
            [up_terms(1)],
        ],
        scal, (dproj,),
    )
    d2_y = swap_y(d2)
    u2_x = swap(u2, 2)
    send31, keep31, final31 = weight_grads(
        (3, 1), ((dstate, 0), (dstate, 1)), ((dproj, 1), (dproj, 0)), (d2,)
    )
    got31 = swap(send31, 1)
    ff_send, ff_keep = choose(
        up_terms(0) + [(u2_x, None, None)],
        block2(1, 0) + [(d2_x, (0, 128), None), (z_got, d0_z[0], None), (d2_y, None, None)],
        scal, 7, (final31,),
    )
    ff_got = swap(ff_send, 8)
    y_far1, y_near1 = sums(
        [[[(keep31, 0, 3), (got31, 0, 3)]], [[(keep31, 0, 2), (got31, 0, 2)]]], scal, (ff_send,)
    )
    y_far1_got = swap_y(y_far1)
    dproj2, dstate2 = back((2,), (y_far1,))
    dstate2 = to_first(dstate2)
    y_near1_got = swap_y(tie(y_near1, (dproj2,)))
    send2, keep2, final2, own_sum1 = weight_grads(
        (2,), ((dstate, 2),), ((dproj2, 0),), (dproj2,), ((keep31, 1), (got31, 1))
    )
    got2 = swap(send2, 1)
    (ff_shard,) = sums(
        [[[(ff_keep, None, None), (ff_got, None, None)]]], scal, (final2,)
    )
    step = ff_shard
    for at in bits[4:]:
        ff_send, ff_keep = halve([(ff_shard, None)], scal, at + 4, (step,))
        ff_got = swap(ff_send, 1 << at)
        (ff_shard,) = sums(
            [[[(ff_keep, None, None), (ff_got, None, None)]]], scal, (spacer(ff_send),)
        )
        step = ff_shard
    ff_steps = list(reversed(bits[3:]))
    ff_there = swap(ff_shard, 1 << ff_steps[0])
    y_far, x_far = sums(
        [
            [[(keep2, 0, 3), (got2, 0, 3)]],
            [[(own_sum1, None, 3), (y_far1_got, None, None)]],
        ],
        scal, (ff_shard,),
    )
    y_far_got = swap_y(y_far)
    x_far_got = swap(x_far, 2)
    send0, keep0, final0 = weight_grads((0,), ((dstate2, 0),), ((dproj, 2),), (y_far,))
    step = spacer(final0)
    grad_inputs, grads1 = run(
        first_back_kernel,
        [inputs.shape, (8, 640)],
        (scal,),
        (inputs, gain1, d_hidden, final0, final31, final2, qa0, qb0, qa1, qb1, grads2)
        + weights,
        (
            pltpu.VMEM((rows, 1024), F32),
            pltpu.VMEM((rows, width), F32),
            pltpu.VMEM((4, width, 256), F32),
            pltpu.SemaphoreType.DMA((4,)),
        ),
        after=(step,),
        far=4,
        us=LATE,
    )
    step = grads1
    while len(ff_steps) > 1:
        to = ff_steps.pop(0)
        ff_shard = join(ff_shard, ff_there, scal, to + 4, 0, (step,))
        ff_there = swap(ff_shard, 1 << ff_steps[0])
        step = spacer(ff_shard)
    got0 = swap(send0, 1)
    q_send, y_near, x_near = sums(
        [
            [[(keep0, 0, 3), (got0, 0, 3), (y_far_got, None, None), (x_far_got, None, None)]],
            [[(keep2, 0, 2), (got2, 0, 2)]],
            [[(own_sum1, None, 2), (y_near1_got, None, None)]],
        ],
        scal, (step,),
    )
    q_got = swap(q_send, 4)
    y_near_got = swap_y(y_near)
    x_near_got = swap(x_near, 2)
    step = q_send
    ff_down, ff_up = choose(
        [(ff_shard, None, None)], [(ff_there, None, None)], scal, 7, (step,)
    )
    up_z = swap(ff_up, 4)
    down_x = swap(ff_down, 2)
    step = spacer(ff_up)
    up_pair, down_pair, gains = sums(
        [
            [[(ff_up, None, None)], [(up_z, None, None)]],
            [[(ff_down, None, None)], [(down_x, None, None)]],
            [[(grads1, None, None)]],
        ],
        scal, (step,), rows=True,
    )
    gains_got = swap_y(gains)
    up_x = swap(up_pair, 2)
    down_z = swap(down_pair, 4)
    step = spacer(up_pair)
    (part,) = sums(
        [
            [
                [
                    (keep0, 0, 2), (got0, 0, 2), (y_near_got, None, None),
                    (x_near_got, None, None), (q_got, None, None),
                ]
            ]
        ],
        scal, (step,),
    )
    part_got = swap(part, 8)
    step = spacer(part)
    (gains,) = sums([[[(gains, None, None), (gains_got, None, None)]]], scal, (step,))
    for at in bits[3:]:
        gains_got = swap(gains, 1 << at)
        step = spacer(gains)
        terms = [
            [(part, None, None), (part_got, None, None)],
            [(gains, None, None), (gains_got, None, None)],
        ]
        if at == bits[-1]:
            (shard,) = sums([terms], scal, (step,), rows=True)
        else:
            part, gains = sums([terms[:1], terms[1:]], scal, (step,))
            part_got = swap(part, 2 << at)
    quarters = [shard] + [swap(shard, 2 * k) for k in (1, 2, 3)]
    up_x = tie(up_x, (quarters[2],))
    down_z = tie(down_z, (up_x,))
    pieces = (up_pair, up_x, down_pair, down_z)
    grad_up, grad_down, token = run(
        hidden_assemble_kernel,
        [up_weight.shape, down_weight.shape, (8, 128)],
        (scal,),
        pieces + tuple(swap(a, 1) for a in pieces),
        (pltpu.SemaphoreType.DMA((24,)),),
        after=(spacer(down_z),),
        away=True,
    )
    (quarters,) = sums([[[(a, None, None)] for a in quarters]], scal, (token,))
    *weight_grad, gain_a, gain_b, gain_c, gain_d = run(
        qkvc_assemble_kernel,
        [w.shape for w in weights] + [output_weight.shape] + [(1, width)] * 4,
        (scal,),
        (quarters, swap(quarters, 1)),
        after=(spacer(quarters),),
    )
    return (
        outputs, grad_inputs,
        *weight_grad, grad_up, grad_down,
        gain_a[0], gain_b[0], gain_c[0], gain_d[0],
    )


def solution(mesh):
    rows = P("head", "dp", None)
    cols = P(None, "head")
    tall = P("head", None)
    flat = P()
    return jax.shard_map(
        per_device,
        mesh=mesh,
        in_specs=(
            rows, P("dp", None), cols, cols, cols, cols, tall, cols, tall,
            flat, flat, flat, flat, rows,
        ),
        out_specs=(
            rows, rows, cols, cols, cols, cols, tall, cols, tall, flat, flat, flat, flat,
        ),
        check_vma=False,
    )
```
